32 devices in a mesh: pipe: 2 (over x), dp: 4 (over z), tensor: 4 (over y, core).
Axes of the slice: x: 2, y: 2, z: 4, core: 2. Of those that a mesh axis runs over, the one named last changes fastest.
Arguments:
- pipe_ends: bfloat16 [2, 2, 4, 384, 768], P('pipe', None, 'dp', 'tensor'), may hold values from -6 to 6
- bounds: int32 [2, 4, 2], P(None, 'dp'), may hold values from 1 to 384, as said below
- query_weight: bfloat16 [2, 768, 768], P('pipe', None, 'tensor'), may hold values from -0.3125 to 0.3125
- key_weight: bfloat16 [2, 768, 768], P('pipe', None, 'tensor'), may hold values from -0.3125 to 0.3125
- value_weight: bfloat16 [2, 768, 768], P('pipe', None, 'tensor'), may hold values from -0.21875 to 0.21875
- attention_out_weight: bfloat16 [2, 768, 768], P('pipe', 'tensor'), may hold values from -0.875 to 0.875
- feedforward_in_weight: bfloat16 [2, 768, 3072], P('pipe', None, 'tensor'), may hold values from -0.21875 to 0.21875
- down_weight: bfloat16 [2, 3072, 768], P('pipe', 'tensor'), may hold values from -0.109375 to 0.109375
- norm_gain: float32 [2, 2, 768], P('pipe'), may hold values from 0.5 to 1.5
- norm_bias: float32 [2, 2, 768], P('pipe'), may hold values from -1 to 1
- rel_table: bfloat16 [512, 768], replicated, may hold values from -6 to 6
Outputs:
- end_values: float32 [2, 2, 4, 384, 768], P('pipe', None, 'dp', 'tensor')
- query_weight_gradient: float32 [2, 768, 768], P('pipe', None, 'tensor')
- key_weight_gradient: float32 [2, 768, 768], P('pipe', None, 'tensor')
- value_weight_gradient: float32 [2, 768, 768], P('pipe', None, 'tensor')
- grad_out: float32 [2, 768, 768], P('pipe', 'tensor')
- grad_in: float32 [2, 768, 3072], P('pipe', None, 'tensor')
- down_weight_gradient: float32 [2, 3072, 768], P('pipe', 'tensor')
- grad_gain: float32 [2, 2, 768], P('pipe')
- grad_bias: float32 [2, 2, 768], P('pipe')
- grad_table: float32 [512, 768], replicated
The draws below stay inside these ranges and needn't reach their ends.
Inputs may be any that keep to these rules, and one draw needn't show every extreme that they name: `bounds`: each row is (split point, length) of one sequence: 1 <= split < length <= 384; tokens at or after the length are padding. In every micro-batch one of the 4 sequences has length 384.
All inputs are finite; a program needn't handle non-finite values.
Results may differ from the reference program's by a relative error of at most 0.03.
The reference program's roundings to bfloat16 on the way count: a program that leaves them out, or rounds other values in their place, can miss the bound.
Values may be sent and summed in bfloat16 or wider, within the bound.
No kernel may reach another device: no remote copies, remote signals or barrier semaphores. Data moves between devices by JAX's collectives and lax.ppermute only.
A program may use at most 256 MiB of HBM per device.

```python
import math
from functools import partial
import jax
import jax.numpy as jnp
from jax import lax

D = 768
HEADS = 12
HEAD = 64
FF = 3072
SPAN = 256
BUCKETS = 512
LEN = 384
MICRO = 2
SEQS = 4
LAYERS = 2


def draw_bounds(key, part):
    key = jax.random.fold_in(key, 11)
    key_length, key_split, key_chosen = jax.random.split(key, 3)
    lengths = jax.random.randint(key_length, (MICRO, SEQS), 3 * LEN // 4 + 1, LEN + 1)
    chosen = jax.random.randint(key_chosen, (MICRO, 1), 0, SEQS)
    slot_index = jnp.arange(SEQS, dtype=jnp.int32)[None, :]
    full_row = slot_index == chosen
    lengths = jnp.where(full_row, LEN, lengths)
    fraction = jax.random.randint(key_split, (MICRO, SEQS), 0, 1 << 20)
    low_split = lengths // 5
    high_split = 4 * lengths // 5
    split_at = low_split + fraction * (high_split - low_split) // (1 << 20)
    return jnp.stack([split_at, lengths], axis=-1).astype(jnp.int32)


def block_levels(stream_key, dims, shards, low, top_value):
    factor_of, own = 1.0, jax.random.fold_in(stream_key, 6)
    for axis_at, parts in shards:
        heights = jnp.exp(jax.random.uniform(jax.random.fold_in(own, axis_at), (parts,), jnp.float32, low / len(shards), top_value / len(shards)))
        factor_of = factor_of * jnp.repeat(heights, dims[axis_at] // parts).reshape([-1 if axis == axis_at else 1 for axis in range(len(dims))])
    return factor_of


def scatter_about(key, extent, width, most, pieces=(), held_as=jnp.bfloat16):
    drawn = jax.random.normal(key, extent, jnp.float32) * width
    if len(pieces) > 0:
        drawn = block_levels(key, extent, pieces, -0.22, 0.18) * drawn
    return jnp.clip(drawn, min=-most, max=most).astype(held_as)


def setup_inputs(seed: int = 0) -> dict:
    streams_of = jax.random.split(jax.random.key(seed), 12)
    return {
        "pipe_ends": scatter_about(streams_of[0], (LAYERS, MICRO, SEQS, LEN, D), 1.0, 6.0, ((0, 2), (2, 4), (3, 4))),
        "bounds": draw_bounds(jax.random.fold_in(streams_of[11], 71), 0),
        "query_weight": scatter_about(streams_of[2], (LAYERS, D, D), (D // 2) ** -0.5, 0.3125, ((0, 2), (2, 4))),
        "key_weight": scatter_about(streams_of[3], (LAYERS, D, D), (D // 2) ** -0.5, 0.3125, ((0, 2), (2, 4))),
        "value_weight": scatter_about(streams_of[4], (LAYERS, D, D), D ** -0.5, 0.21875, ((0, 2), (2, 4))),
        "attention_out_weight": scatter_about(streams_of[5], (LAYERS, D, D), (D // 16) ** -0.5, 0.875, ((0, 2), (1, 4))),
        "feedforward_in_weight": scatter_about(streams_of[6], (LAYERS, D, FF), D ** -0.5, 0.21875, ((0, 2), (2, 4))),
        "down_weight": scatter_about(streams_of[7], (LAYERS, FF, D), FF ** -0.5, 0.109375, ((0, 2), (1, 4))),
        "norm_gain": jnp.clip(1.0 + 0.1 * jax.random.normal(streams_of[8], (LAYERS, 2, D), jnp.float32), 0.5, 1.5),
        "norm_bias": scatter_about(streams_of[9], (LAYERS, 2, D), 0.2, 1.0, ((0, 2),), jnp.float32),
        "rel_table": scatter_about(streams_of[10], (BUCKETS, D), 1.0, 6.0),
    }


@jax.custom_vjp
def low(v):
    return lax.optimization_barrier(v.astype(jnp.bfloat16)).astype(jnp.float32)

@jax.custom_vjp
def low_back(v):
    return v

def low_keep(v):
    return (low(v), None)

def low_pass(kept, grad):
    return (grad,)

def back_keep(v):
    return (v, None)

def back_low(kept, grad):
    return (low(grad),)
low.defvjp(low_keep, low_pass)
low_back.defvjp(back_keep, back_low)
EPSILON = 1e-05
MASKED = -1e+30

def exact_dot(left_side, right_side):
    return jnp.dot(left_side, right_side, precision=lax.Precision.HIGHEST, preferred_element_type=jnp.float32)

def smooth_unit(values):
    return 0.5 * values * (1.0 + lax.erf(values * (1.0 / math.sqrt(2.0))))

def layer_norm(summed, gain_row, offset_row):
    row_mean = lax.optimization_barrier(jnp.mean(summed, axis=-1, keepdims=True))
    centred = summed - row_mean
    spread = lax.optimization_barrier(jnp.mean(centred * centred, axis=-1, keepdims=True))
    return centred * lax.rsqrt(spread + EPSILON) * gain_row + offset_row

def relative_index(bound_pair):
    places = jnp.arange(LEN, dtype=jnp.int32)
    split_at = bound_pair[0]
    within = jnp.where(places < split_at, places, places - split_at)
    offsets = within[:, None] - within[None, :]
    near_index = jnp.clip(offsets, -SPAN, SPAN - 1) + SPAN
    far_index = jnp.clip(-offsets, -SPAN, SPAN - 1) + SPAN
    return (near_index, far_index, places < bound_pair[1])

def attend_sequence(operands, table_keys, table_queries):
    queries, keys_all, values_all, bound_pair = operands
    near_index, far_index, live_keys = relative_index(bound_pair)
    query_per_head = queries.reshape(LEN, HEADS, HEAD)
    head_keys = keys_all.reshape(LEN, HEADS, HEAD)
    head_values = values_all.reshape(LEN, HEADS, HEAD)
    table_key_heads = table_keys.reshape(BUCKETS, HEADS, HEAD)
    table_qh = table_queries.reshape(BUCKETS, HEADS, HEAD)
    highest_precision = lax.Precision.HIGHEST
    content = jnp.einsum('ihd,jhd->hij', query_per_head, head_keys, precision=highest_precision)
    query_axis_terms = low_back(jnp.einsum('pac,rac->apr', query_per_head, table_key_heads, precision=highest_precision))
    along_keys = low_back(jnp.einsum('jhd,bhd->hbj', head_keys, table_qh, precision=highest_precision))
    first_term = jnp.take_along_axis(query_axis_terms, jnp.broadcast_to(near_index[None], content.shape), axis=2)
    second_term = jnp.take_along_axis(along_keys, jnp.broadcast_to(far_index[None], content.shape), axis=1)
    scores = low_back(content + first_term + second_term) * (3.0 * HEAD) ** (-0.5)
    scores = jnp.where(live_keys[None, None, :], scores, MASKED)
    row_peak = lax.optimization_barrier(jnp.max(scores, axis=-1, keepdims=True))
    raised = jnp.exp(scores - row_peak)
    weights_full = raised / lax.optimization_barrier(jnp.sum(raised, axis=-1, keepdims=True))
    mixture = jnp.einsum('hij,jhd->ihd', low(weights_full), head_values, precision=highest_precision)
    return low(low_back(mixture.reshape(LEN, D)))

def one_layer(layer_in, bound_rows, query_weight, key_weight, value_weight, attention_out_weight, feedforward_in_weight, down_weight, gain_pair, bias_pair, rel_table):
    queries = low(low_back(exact_dot(layer_in, query_weight)))
    keys_all = low(low_back(exact_dot(layer_in, key_weight)))
    values_all = low(low_back(exact_dot(layer_in, value_weight)))
    table_keys = low(exact_dot(rel_table, key_weight))
    table_queries = low(exact_dot(rel_table, query_weight))
    attend = jax.checkpoint(partial(attend_sequence, table_keys=table_keys, table_queries=table_queries))
    context_rows = lax.map(attend, (queries, keys_all, values_all, bound_rows))
    attn = low_back(exact_dot(context_rows, attention_out_weight))
    hidden = layer_norm(layer_in + attn, gain_pair[0], bias_pair[0])
    upward_rows = low_back(exact_dot(low(hidden), feedforward_in_weight))
    active_rows = low(smooth_unit(upward_rows))
    ffn = low_back(exact_dot(active_rows, down_weight))
    return layer_norm(hidden + ffn, gain_pair[1], bias_pair[1])

def forward(first_in, query_weight, key_weight, value_weight, attention_out_weight, feedforward_in_weight, down_weight, norm_gain, norm_bias, rel_table, bounds):
    layer = jax.checkpoint(one_layer)
    results = []
    for micro_index in range(MICRO):
        middle = layer(first_in[micro_index], bounds[micro_index], query_weight[0], key_weight[0], value_weight[0], attention_out_weight[0], feedforward_in_weight[0], down_weight[0], norm_gain[0], norm_bias[0], rel_table)
        results.append(layer(low_back(low(middle)), bounds[micro_index], query_weight[1], key_weight[1], value_weight[1], attention_out_weight[1], feedforward_in_weight[1], down_weight[1], norm_gain[1], norm_bias[1], rel_table))
    return jnp.stack(results)

def reference(pipe_ends, bounds, query_weight, key_weight, value_weight, attention_out_weight, feedforward_in_weight, down_weight, norm_gain, norm_bias, rel_table):
    first_in = pipe_ends[0].astype(jnp.float32)
    cotangent = pipe_ends[1].astype(jnp.float32)
    primals = (first_in, query_weight.astype(jnp.float32), key_weight.astype(jnp.float32), value_weight.astype(jnp.float32), attention_out_weight.astype(jnp.float32), feedforward_in_weight.astype(jnp.float32), down_weight.astype(jnp.float32), norm_gain.astype(jnp.float32), norm_bias.astype(jnp.float32), rel_table.astype(jnp.float32))

    def wrapped(*inputs_all):
        return forward(*inputs_all, bounds)
    result, pullback = jax.vjp(wrapped, *primals)
    grads = pullback(cotangent)
    end_values = jnp.stack([grads[0], result])
    return (end_values, grads[1], grads[2], grads[3], grads[4], grads[5], grads[6], grads[7], grads[8], grads[9])
```

```python
import math

import jax
import jax.numpy as jnp
from jax import lax
from jax.experimental import pallas as pl
from jax.experimental.pallas import tpu as pltpu
from jax.sharding import PartitionSpec as P

HEAD = 64
BLOCK = 128
EPSILON = 1e-05
MASKED = -1e30
BF = jnp.bfloat16
F32 = jnp.float32
VMEM_BYTES = 50 * 2**20
MOST_DIRECT = 8


def dot(left, right):
    return lax.dot_general(left, right, (((1,), (0,)), ((), ())), preferred_element_type=F32)


def dot_t(left, right):
    return lax.dot_general(left, right, (((1,), (1,)), ((), ())), preferred_element_type=F32)


def t_dot(left, right):
    return lax.dot_general(left, right, (((0,), (0,)), ((), ())), preferred_element_type=F32)


def send_ahead(block, axis, distance):
    count = lax.axis_size(axis)
    return lax.ppermute(block, axis, [(i, (i + distance) % count) for i in range(count)])


def swap_pipe(block):
    return lax.ppermute(block, "pipe", [(0, 1), (1, 0)])


def chunk_at(rows, index, count):
    size = rows.shape[0] // count
    return lax.dynamic_slice_in_dim(rows, index * size, size, 0)


def scatter_sum(partial, axis):
    count = lax.axis_size(axis)
    me = lax.axis_index(axis)
    low = partial.astype(BF)
    if count > MOST_DIRECT:
        return lax.psum_scatter(low, axis, scatter_dimension=0, tiled=True).astype(F32)
    total = chunk_at(partial, me, count).astype(F32)
    for distance in range(1, count):
        outgoing = chunk_at(low, (me + distance) % count, count)
        total = total + send_ahead(outgoing, axis, distance).astype(F32)
    return total


def gather_rows(chunk, axis):
    count = lax.axis_size(axis)
    me = lax.axis_index(axis)
    size = chunk.shape[0]
    if count > MOST_DIRECT:
        return lax.all_gather(chunk, axis, axis=0, tiled=True)
    whole = jnp.zeros((count * size,) + chunk.shape[1:], chunk.dtype)
    whole = lax.dynamic_update_slice_in_dim(whole, chunk, me * size, 0)
    for distance in range(1, count):
        arrived = send_ahead(chunk, axis, distance)
        source = (me - distance) % count
        whole = lax.dynamic_update_slice_in_dim(whole, arrived, source * size, 0)
    return whole


def gather_tokens(rows):
    return lax.all_gather(rows, "tensor", axis=0, tiled=True)


def smooth_unit(values):
    return 0.5 * values * (1.0 + lax.erf(values * (1.0 / math.sqrt(2.0))))


def smooth_slope(values):
    below = 0.5 * (1.0 + lax.erf(values * (1.0 / math.sqrt(2.0))))
    density = jnp.exp(-0.5 * values * values) * (1.0 / math.sqrt(2.0 * math.pi))
    return below + values * density


def norm_forward(summed, gain_row, offset_row):
    row_mean = jnp.mean(summed, axis=-1, keepdims=True)
    centred = summed - row_mean
    spread = jnp.mean(centred * centred, axis=-1, keepdims=True)
    inverse = lax.rsqrt(spread + EPSILON)
    normed = centred * inverse
    return (normed * gain_row + offset_row, (normed, inverse))


def norm_backward(grad_result, kept, gain_row):
    normed, inverse = kept
    grad_gain = jnp.sum(grad_result * normed, axis=0)
    grad_offset = jnp.sum(grad_result, axis=0)
    scaled = grad_result * gain_row
    centre_one = jnp.mean(scaled, axis=-1, keepdims=True)
    centre_two = jnp.mean(scaled * normed, axis=-1, keepdims=True)
    return (inverse * (scaled - centre_one - normed * centre_two), grad_gain, grad_offset)


def by_segment(rows, split_at):
    first = lax.broadcasted_iota(jnp.int32, rows.shape, 0) < split_at
    zero = jnp.zeros_like(rows)
    return jnp.concatenate([jnp.where(first, rows, zero), jnp.where(first, zero, rows)], axis=1)


def placed_blocks(rows, first_table, second_table, first_columns):
    total = rows.shape[0]
    span = total + BLOCK
    blocks = []
    for start in range(0, total, BLOCK):
        low = total - BLOCK - start
        part = rows[start : start + BLOCK]
        first = dot_t(part, first_table[low : low + span])
        second = dot_t(part, second_table[low : low + span])
        shift = total + 1
        first = pltpu.roll(first, shift, 1, stride=1, stride_axis=0)[:, :total]
        second = pltpu.roll(second, shift, 1, stride=1, stride_axis=0)[:, :total]
        blocks.append(jnp.where(first_columns, first, second))
    return blocks


def attend_kernel(bound_ref, x_ref, weight_ref, table_ref, qkv_ref, probs_ref, context_ref):
    split_at = bound_ref[0]
    total = x_ref.shape[0]
    width = weight_ref.shape[1] // 3
    qkv = dot(x_ref[...], weight_ref[...]).astype(BF)
    qkv_ref[...] = qkv
    table = table_ref[...]
    wide = table.astype(F32)
    later = pltpu.roll(wide, wide.shape[0] - split_at, 0).astype(BF)
    earlier = pltpu.roll(wide, split_at, 0).astype(BF)
    first_columns = lax.broadcasted_iota(jnp.int32, (BLOCK, total), 1) < split_at
    live = lax.broadcasted_iota(jnp.int32, (total, total), 1) < bound_ref[1]
    contexts = []
    for head in range(width // HEAD):
        at = head * HEAD
        query = qkv[:, at : at + HEAD]
        key = qkv[:, width + at : width + at + HEAD]
        value = qkv[:, 2 * width + at : 2 * width + at + HEAD]

        def tables(offset):
            cut = slice(offset + at, offset + at + HEAD)
            return (
                jnp.concatenate([table[:, cut], later[:, cut]], 1),
                jnp.concatenate([earlier[:, cut], table[:, cut]], 1),
            )

        near = jnp.concatenate(
            placed_blocks(by_segment(query, split_at), *tables(0), first_columns), 0
        )
        far = placed_blocks(by_segment(key, split_at), *tables(width), first_columns)
        far = jnp.concatenate([block.T for block in far], 1)
        scores = (dot_t(query, key) + near + far) * (3.0 * HEAD) ** (-0.5)
        scores = jnp.where(live, scores, MASKED)
        raised = jnp.exp(scores - jnp.max(scores, axis=1, keepdims=True))
        probs = raised / jnp.sum(raised, axis=1, keepdims=True)
        probs_ref[head] = probs
        contexts.append(dot(probs.astype(BF), value).astype(BF))
    context_ref[...] = jnp.concatenate(contexts, 1)


def whole_specs(count):
    return [pl.BlockSpec(memory_space=pltpu.VMEM)] * count


def attend_forward(bound, rows, qkv_weight, table):
    total = rows.shape[0]
    width = qkv_weight.shape[1] // 3
    return pl.pallas_call(
        attend_kernel,
        out_shape=(
            jax.ShapeDtypeStruct((total, 3 * width), BF),
            jax.ShapeDtypeStruct((width // HEAD, total, total), F32),
            jax.ShapeDtypeStruct((total, width), BF),
        ),
        in_specs=[pl.BlockSpec(memory_space=pltpu.SMEM)] + whole_specs(3),
        out_specs=tuple(whole_specs(3)),
        compiler_params=pltpu.CompilerParams(vmem_limit_bytes=VMEM_BYTES),
    )(bound, rows, qkv_weight, table)


def attend_back_kernel(
    bound_ref, grad_ref, weight_ref, qkv_ref, probs_ref, table_ref, grad_qkv_ref, grad_table_ref, held_ref
):
    split_at = bound_ref[0]
    total = grad_ref.shape[0]
    width = weight_ref.shape[0]
    heads = width // HEAD
    span = total + BLOCK
    grad_context = dot_t(grad_ref[...], weight_ref[...]).astype(BF)
    grad_context_t = grad_context.astype(F32).T.astype(BF)
    qkv = qkv_ref[...]
    rows_t = qkv[:, : 2 * width].astype(F32).T.astype(BF)
    table = table_ref[...]
    moved = pltpu.roll(table.astype(F32), split_at, 0).astype(BF)
    row_ids = lax.broadcasted_iota(jnp.int32, (total, total), 0)
    places = jnp.where(row_ids < split_at, row_ids, row_ids - split_at)
    turned = lax.broadcasted_iota(jnp.int32, (total, total), 1) == total - 1 - places
    merge = jnp.where(turned, 1.0, 0.0).astype(BF)
    first_lanes = lax.broadcasted_iota(jnp.int32, (HEAD, total), 1) < split_at
    first_rows = lax.broadcasted_iota(jnp.int32, (total, HEAD), 0) < split_at
    pad = jnp.zeros((BLOCK, BLOCK), F32)
    held_ref[...] = jnp.zeros(held_ref.shape, F32)

    def along_table(merged, offset, head):
        cut = slice(offset + head * HEAD, offset + (head + 1) * HEAD)
        pair = jnp.concatenate([table[:, cut], moved[:, cut]], 1)
        turned_rows = rows_t[cut]
        zero = jnp.zeros_like(turned_rows)
        turned_rows = jnp.concatenate(
            [jnp.where(first_lanes, turned_rows, zero), jnp.where(first_lanes, zero, turned_rows)],
            0,
        )
        parts = []
        slot = offset // HEAD + head
        for start in range(0, total, BLOCK):
            block = jnp.concatenate([merged[start : start + BLOCK], pad], 1)
            block = pltpu.roll(block, 1, 1, stride=1, stride_axis=0).astype(BF)
            parts.append(dot(block, pair[start : start + span]))
            held_ref[slot, :, start : start + span] += dot(
                turned_rows[:, start : start + BLOCK], block
            )
        both = jnp.concatenate(parts, 0)
        return jnp.where(first_rows, both[:, :HEAD], both[:, HEAD:])

    grad_queries = []
    grad_keys = []
    grad_values_t = []
    for head in range(heads):
        at = head * HEAD
        cut = slice(at, at + HEAD)
        query = qkv[:, at : at + HEAD]
        key = qkv[:, width + at : width + at + HEAD]
        value = qkv[:, 2 * width + at : 2 * width + at + HEAD]
        grad_probs = dot_t(grad_context[:, cut], value)
        probs = probs_ref[head]
        centre = jnp.sum(probs * grad_probs, axis=1, keepdims=True)
        score_grad = (probs * (grad_probs - centre) * (3.0 * HEAD) ** (-0.5)).astype(BF)
        score_grad_t = score_grad.astype(F32).T.astype(BF)
        grad_values_t.append(dot(grad_context_t[cut], probs.astype(BF)))
        grad_queries.append(
            dot(score_grad, key) + along_table(dot(score_grad, merge), 0, head)
        )
        grad_keys.append(
            dot(score_grad_t, query) + along_table(dot(score_grad_t, merge), width, head)
        )
    grad_values = jnp.concatenate(grad_values_t, 0).T
    grad_qkv_ref[...] = jnp.concatenate(grad_queries + grad_keys + [grad_values], 1).astype(BF)
    lanes = lax.broadcasted_iota(jnp.int32, (HEAD, total + BLOCK), 1)
    for slot in range(2 * heads):
        first = held_ref[slot, :HEAD]
        second = pltpu.roll(held_ref[slot, HEAD:], 2 * total - split_at, 1)
        both = first + second
        bottom = jnp.sum(both[:, :BLOCK], axis=1, keepdims=True)
        top = jnp.sum(both[:, 2 * total - BLOCK :], axis=1, keepdims=True)
        middle = both[:, BLOCK : 2 * total - BLOCK]
        middle = middle + jnp.where(lanes == 0, bottom, 0.0)
        middle = middle + jnp.where(lanes == total + BLOCK - 1, top, 0.0)
        grad_table_ref[slot * HEAD : (slot + 1) * HEAD] = middle.astype(BF)


def attend_backward(bound, grad_rows, out_weight, qkv, probs, table):
    total = grad_rows.shape[0]
    width = out_weight.shape[0]
    return pl.pallas_call(
        attend_back_kernel,
        out_shape=(
            jax.ShapeDtypeStruct((total, 3 * width), BF),
            jax.ShapeDtypeStruct((2 * width, total + BLOCK), BF),
        ),
        in_specs=[pl.BlockSpec(memory_space=pltpu.SMEM)] + whole_specs(5),
        out_specs=tuple(whole_specs(2)),
        scratch_shapes=[pltpu.VMEM((2 * width // HEAD, 2 * HEAD, 2 * total), F32)],
        compiler_params=pltpu.CompilerParams(vmem_limit_bytes=VMEM_BYTES),
    )(bound, grad_rows, out_weight, qkv, probs, table)


def layer_forward(rows, bound, weights, gain_pair, bias_pair, table):
    qkv_weight, out_weight, in_weight, down_weight = weights
    rows_whole = gather_tokens(rows)
    qkv, probs, context = attend_forward(bound, rows_whole, qkv_weight, table)
    attn = scatter_sum(dot(context, out_weight), "tensor")
    hidden, norm_one = norm_forward(rows.astype(F32) + attn, gain_pair[0], bias_pair[0])
    hidden_whole = gather_tokens(hidden.astype(BF))
    upward = dot(hidden_whole, in_weight)
    active = smooth_unit(upward).astype(BF)
    ffn = scatter_sum(dot(active, down_weight), "tensor")
    result, norm_two = norm_forward(hidden + ffn, gain_pair[1], bias_pair[1])
    saved = (rows_whole, qkv, probs, context, norm_one, hidden_whole, upward, active, norm_two)
    return (result, saved)


def layer_backward(grad_result, saved, bound, weights, gain_pair, table, rel_table):
    qkv_weight, out_weight, in_weight, down_weight = weights
    rows_whole, qkv, probs, context, norm_one, hidden_whole, upward, active, norm_two = saved
    width = out_weight.shape[0]
    grad_two, gain_two, bias_two = norm_backward(grad_result, norm_two, gain_pair[1])
    grad_ffn = gather_tokens(grad_two.astype(BF))
    grad_up = (dot_t(grad_ffn, down_weight) * smooth_slope(upward)).astype(BF)
    grad_hidden = grad_two + scatter_sum(dot_t(grad_up, in_weight), "tensor")
    grad_down = t_dot(active, grad_ffn)
    grad_in = t_dot(hidden_whole, grad_up)
    grad_one, gain_one, bias_one = norm_backward(grad_hidden, norm_one, gain_pair[0])
    grad_attn = gather_tokens(grad_one.astype(BF))
    grad_qkv, grad_table_t = attend_backward(bound, grad_attn, out_weight, qkv, probs, table)
    grad_rows = grad_one + scatter_sum(dot_t(grad_qkv, qkv_weight), "tensor")
    grad_out_t = t_dot(grad_attn, context)
    from_rows = t_dot(rows_whole, grad_qkv)
    from_table = lax.dot_general(
        rel_table, grad_table_t, (((0,), (1,)), ((), ())), preferred_element_type=F32
    )
    grad_attention = jnp.concatenate(
        [
            from_rows[:, :width] + from_table[:, width:],
            from_rows[:, width : 2 * width] + from_table[:, :width],
            from_rows[:, 2 * width :],
            grad_out_t,
        ],
        1,
    )
    key_query = jnp.concatenate([qkv_weight[:, width : 2 * width], qkv_weight[:, :width]], 1)
    table_part = lax.dot_general(
        grad_table_t, key_query, (((0,), (1,)), ((), ())), preferred_element_type=F32
    )
    norm_rows = jnp.stack([gain_one, gain_two, bias_one, bias_two])
    matrices = tuple(grad.astype(BF) for grad in (grad_attention, grad_in, grad_down))
    return (grad_rows, matrices, table_part, norm_rows)


def sum_matrix(partial, layer):
    section = lax.axis_index("pipe")
    kept = chunk_at(partial, section, 2)
    half = kept.astype(F32) + swap_pipe(chunk_at(partial, 1 - section, 2)).astype(F32)
    own = scatter_sum(half, "dp")
    half = gather_rows(own.astype(BF), "dp")
    other = lax.ppermute(half, "pipe", [(1 - layer, layer)])
    pair = [half, other] if layer == 0 else [other, half]
    return jnp.concatenate(pair, 0)


def sum_small(partial):
    own = scatter_sum(partial, "tensor").astype(BF)
    own = own.astype(F32) + swap_pipe(own).astype(F32)
    own = scatter_sum(own, "dp").astype(BF)
    return gather_rows(gather_rows(own, "dp"), "tensor")


def per_device(
    pipe_ends,
    bounds,
    query_weight,
    key_weight,
    value_weight,
    attention_out_weight,
    feedforward_in_weight,
    down_weight,
    norm_gain,
    norm_bias,
    rel_table,
):
    section = lax.axis_index("pipe")
    ends = pipe_ends[0, :, 0]
    total = ends.shape[1] * lax.axis_size("tensor")
    buckets, features = rel_table.shape
    width = query_weight.shape[2]
    bound = lax.dynamic_index_in_dim(bounds, section, 0, keepdims=False)[0]
    from_other = swap_pipe(lax.dynamic_index_in_dim(ends, 1 - section, 0, keepdims=False))
    first_in = jnp.where(section == 0, ends[0], from_other)
    last_grad = jnp.where(section == 0, from_other, ends[1]).astype(F32)
    own_weights = (
        jnp.concatenate([query_weight[0], key_weight[0], value_weight[0]], 1),
        attention_out_weight[0],
        feedforward_in_weight[0],
        down_weight[0],
    )
    own_norms = jnp.concatenate([norm_gain[0], norm_bias[0]], 0)
    other_norms = swap_pipe(own_norms)
    other_weights = tuple(swap_pipe(weight) for weight in own_weights)

    def of_layer(layer, own, other):
        return jnp.where(section == layer, own, other)

    weights = [
        tuple(of_layer(layer, own, other) for own, other in zip(own_weights, other_weights))
        for layer in range(2)
    ]
    norms = [of_layer(layer, own_norms, other_norms) for layer in range(2)]
    wide = jnp.arange(2 * total, dtype=jnp.int32)
    near_rows = jnp.clip(wide - (total - buckets // 2), 0, buckets - 1)
    pick = jnp.concatenate([near_rows[::-1], near_rows])
    one_hot = (pick[:, None] == jnp.arange(buckets, dtype=jnp.int32)[None, :]).astype(BF)
    rel_wide = dot(one_hot, rel_table).astype(BF)
    tables = []
    for layer in range(2):
        qkv_weight = weights[layer][0]
        key_query = jnp.concatenate([qkv_weight[:, width : 2 * width], qkv_weight[:, :width]], 1)
        both = dot(rel_wide, key_query).astype(BF)
        tables.append((both[: 2 * total], both[2 * total :]))

    saved = []
    rows = first_in
    for layer in range(2):
        result, kept = layer_forward(
            rows, bound, weights[layer], norms[layer][:2], norms[layer][2:], tables[layer][0]
        )
        saved.append(kept)
        rows = result.astype(BF)
    result_low = rows
    other_result = lax.ppermute(result_low, "pipe", [(0, 1)])
    grad = last_grad
    summed = [None, None]
    table_parts = []
    norm_rows = [None, None]
    for layer in (1, 0):
        if layer == 0:
            grad = grad.astype(BF).astype(F32)
        grad, matrices, table_part, norm_rows[layer] = layer_backward(
            grad, saved[layer], bound, weights[layer], norms[layer][:2], tables[layer][1], rel_table
        )
        table_parts.append(table_part)
        summed[layer] = [sum_matrix(matrix, layer) for matrix in matrices]
    other_grad = lax.ppermute(grad.astype(BF), "pipe", [(1, 0)]).astype(F32)
    end_values = jnp.where(
        section == 0,
        jnp.stack([grad, other_grad]),
        jnp.stack([other_result.astype(F32), result]),
    )
    small_rows = 8 * lax.axis_size("dp") * lax.axis_size("tensor")
    padding = -(buckets + 8) % small_rows
    small = jnp.concatenate(
        [table_parts[0] + table_parts[1]] + norm_rows + [jnp.zeros((padding, features), F32)], 0
    )
    small = sum_small(small).astype(F32)
    norm_sums = lax.dynamic_slice_in_dim(small, buckets + 4 * section, 4, 0)
    attention, into, down = (
        jnp.where(section == 0, first, second).astype(F32) for first, second in zip(*summed)
    )
    return (
        end_values[None, :, None],
        attention[:, :width][None],
        attention[:, width : 2 * width][None],
        attention[:, 2 * width : 3 * width][None],
        attention[:, 3 * width :].T[None],
        into[None],
        down[None],
        norm_sums[:2][None],
        norm_sums[2:][None],
        small[:buckets],
    )


def solution(mesh):
    in_specs = (
        P("pipe", None, "dp", "tensor", None),
        P(None, "dp", None),
        P("pipe", None, "tensor"),
        P("pipe", None, "tensor"),
        P("pipe", None, "tensor"),
        P("pipe", "tensor", None),
        P("pipe", None, "tensor"),
        P("pipe", "tensor", None),
        P("pipe", None, None),
        P("pipe", None, None),
        P(),
    )
    out_specs = (
        P("pipe", None, "dp", "tensor", None),
        P("pipe", None, "tensor"),
        P("pipe", None, "tensor"),
        P("pipe", None, "tensor"),
        P("pipe", "tensor", None),
        P("pipe", None, "tensor"),
        P("pipe", "tensor", None),
        P("pipe", None, None),
        P("pipe", None, None),
        P(),
    )
    return jax.shard_map(
        per_device, mesh=mesh, in_specs=in_specs, out_specs=out_specs, check_vma=False
    )
```

```python
import functools
import math

import jax
import jax.numpy as jnp
from jax import lax
from jax.experimental import pallas as pl
from jax.experimental.pallas import tpu as pltpu
from jax.sharding import PartitionSpec as P

HEAD = 64
BLOCK = 128
EPSILON = 1e-05
MASKED = -1e30
BF = jnp.bfloat16
F32 = jnp.float32
SCALE = (3.0 * HEAD) ** (-0.5)


def dot(left, right):
    return lax.dot_general(left, right, (((1,), (0,)), ((), ())), preferred_element_type=F32)


def dot_t(left, right):
    return lax.dot_general(left, right, (((1,), (1,)), ((), ())), preferred_element_type=F32)


def t_dot(left, right):
    return lax.dot_general(left, right, (((0,), (0,)), ((), ())), preferred_element_type=F32)


def low(shape):
    return jax.ShapeDtypeStruct(shape, BF)


def wide(shape):
    return jax.ShapeDtypeStruct(shape, F32)


def run_kernel(body, outs, scalars, arrays, after=(), scratch=(), spare=4):
    after = tuple(after)
    held = sum(math.prod(one.shape) * one.dtype.itemsize for one in (*outs, *arrays, *scratch))
    vmem = pl.BlockSpec(memory_space=pltpu.VMEM)

    def with_after(*refs):
        lead = len(scalars) + len(arrays)
        body(*refs[:lead], *refs[lead + len(after) :])

    return pl.pallas_call(
        with_after,
        out_shape=tuple(outs),
        in_specs=[pl.BlockSpec(memory_space=pltpu.SMEM)] * len(scalars)
        + [vmem] * len(arrays)
        + [pl.BlockSpec(memory_space=pl.ANY)] * len(after),
        out_specs=tuple(vmem for _ in outs),
        scratch_shapes=list(scratch),
        compiler_params=pltpu.CompilerParams(vmem_limit_bytes=held + spare * 2**20),
    )(*scalars, *arrays, *after)


def gate(array, after):
    def nothing(*refs):
        del refs

    anywhere = pl.BlockSpec(memory_space=pl.ANY)
    return pl.pallas_call(
        nothing,
        out_shape=jax.ShapeDtypeStruct(array.shape, array.dtype),
        in_specs=[anywhere] * (1 + len(after)),
        out_specs=anywhere,
        input_output_aliases={0: 0},
    )(array, *after)


def to_partner(block, axis, distance):
    count = lax.axis_size(axis)
    return lax.ppermute(block, axis, [(i, i ^ distance) for i in range(count)])


def swap_pipe(block):
    return to_partner(block, "pipe", 1)


def spread(block):
    count = lax.axis_size("tensor")
    distances = [2**step for step in range(1, count.bit_length() - 1)]
    blocks = {0: block}
    for distance in distances:
        blocks.update({d + distance: to_partner(blocks[d], "tensor", distance) for d in list(blocks)})
    blocks.update({d + 1: to_partner(blocks[d], "tensor", 1) for d in list(blocks)})
    return [blocks[d] for d in range(count)]


def exchange(parts):
    return [parts[0]] + [to_partner(parts[d], "tensor", d) for d in range(1, len(parts))]


def row_place(index_ref, distance, size):
    return pl.ds(pl.multiple_of((index_ref[0] ^ distance) * size, size), size)


def store_parts(index_ref, whole_ref, part_refs):
    size = part_refs[0].shape[0]
    for distance, part_ref in enumerate(part_refs):
        part_ref[...] = whole_ref[row_place(index_ref, distance, size), :].astype(part_ref.dtype)


def part_shapes(count, size, features):
    return [wide((size, features))] + [low((size, features))] * (count - 1)


def added(refs):
    total = refs[0][...].astype(F32)
    for ref in refs[1:]:
        total = total + ref[...].astype(F32)
    return total


def normalize(summed):
    row_mean = jnp.mean(summed, axis=-1, keepdims=True)
    centred = summed - row_mean
    spread_of = jnp.mean(centred * centred, axis=-1, keepdims=True)
    inverse = lax.rsqrt(spread_of + EPSILON)
    return centred * inverse, inverse


def normalize_back(grad_result, normed, inverse, gain_row):
    sums = jnp.concatenate(
        [
            jnp.sum(grad_result * normed, axis=0, keepdims=True),
            jnp.sum(grad_result, axis=0, keepdims=True),
        ],
        0,
    )
    scaled = grad_result * gain_row
    centre_one = jnp.mean(scaled, axis=-1, keepdims=True)
    centre_two = jnp.mean(scaled * normed, axis=-1, keepdims=True)
    return inverse * (scaled - centre_one - normed * centre_two), sums


def by_segment(rows, split_at):
    first = lax.broadcasted_iota(jnp.int32, rows.shape, 0) < split_at
    zero = jnp.zeros_like(rows)
    return jnp.concatenate([jnp.where(first, rows, zero), jnp.where(first, zero, rows)], axis=1)


def placed_blocks(rows, first_table, second_table, first_columns):
    total = rows.shape[0]
    span = total + BLOCK
    blocks = []
    for start in range(0, total, BLOCK):
        begin = total - BLOCK - start
        part = rows[start : start + BLOCK]
        first = dot_t(part, first_table[begin : begin + span])
        second = dot_t(part, second_table[begin : begin + span])
        first = pltpu.roll(first, total + 1, 1, stride=1, stride_axis=0)[:, :total]
        second = pltpu.roll(second, total + 1, 1, stride=1, stride_axis=0)[:, :total]
        blocks.append(jnp.where(first_columns, first, second))
    return blocks


def attend_kernel(count, index_ref, bound_ref, *refs):
    blocks = refs[:count]
    qkv_weight_ref, out_weight_ref, table_ref = refs[count : count + 3]
    rows_ref, qkv_ref, probs_ref, context_ref = refs[count + 3 : count + 7]
    part_refs = refs[count + 7 : 2 * count + 7]
    held_ref = refs[2 * count + 7]
    size = blocks[0].shape[0]
    for distance, block in enumerate(blocks):
        rows_ref[row_place(index_ref, distance, size), :] = block[...]
    split_at = bound_ref[0]
    total = rows_ref.shape[0]
    width = out_weight_ref.shape[0]
    qkv = dot(rows_ref[...], qkv_weight_ref[...]).astype(BF)
    qkv_ref[...] = qkv
    table = table_ref[...]
    table_wide = table.astype(F32)
    later = pltpu.roll(table_wide, 2 * total - split_at, 0).astype(BF)
    earlier = pltpu.roll(table_wide, split_at, 0).astype(BF)
    first_columns = lax.broadcasted_iota(jnp.int32, (BLOCK, total), 1) < split_at
    live = lax.broadcasted_iota(jnp.int32, (total, total), 1) < bound_ref[1]
    contexts = []
    for head in range(width // HEAD):
        at = head * HEAD
        query = qkv[:, at : at + HEAD]
        key = qkv[:, width + at : width + at + HEAD]
        value = qkv[:, 2 * width + at : 2 * width + at + HEAD]

        def tables(offset):
            cut = slice(offset + at, offset + at + HEAD)
            return (
                jnp.concatenate([table[:, cut], later[:, cut]], 1),
                jnp.concatenate([earlier[:, cut], table[:, cut]], 1),
            )

        near = jnp.concatenate(
            placed_blocks(by_segment(query, split_at), *tables(0), first_columns), 0
        )
        far = placed_blocks(by_segment(key, split_at), *tables(width), first_columns)
        far = jnp.concatenate([block.T for block in far], 1)
        scores = jnp.where(live, (dot_t(query, key) + near + far) * SCALE, MASKED)
        raised = jnp.exp(scores - jnp.max(scores, axis=1, keepdims=True))
        probs = raised / jnp.sum(raised, axis=1, keepdims=True)
        probs_ref[head] = probs
        contexts.append(dot(probs.astype(BF), value).astype(BF))
    context = jnp.concatenate(contexts, 1)
    context_ref[...] = context
    held_ref[...] = dot(context, out_weight_ref[...])
    store_parts(index_ref, held_ref, part_refs)


def attend_forward(index, bound, blocks, qkv_weight, out_weight, table):
    count = len(blocks)
    size, features = blocks[0].shape
    total = count * size
    width = out_weight.shape[0]
    outs = run_kernel(
        functools.partial(attend_kernel, count),
        [
            low((total, features)),
            low((total, 3 * width)),
            wide((width // HEAD, total, total)),
            low((total, width)),
        ]
        + part_shapes(count, size, features),
        (index, bound),
        (*blocks, qkv_weight, out_weight, table),
        scratch=[pltpu.VMEM((total, features), F32)],
        spare=16,
    )
    return outs[:4], outs[4:]


def attend_back_kernel(count, index_ref, bound_ref, *refs):
    blocks = refs[:count]
    out_weight_ref, qkv_weight_ref, qkv_ref, probs_ref, table_ref = refs[count : count + 5]
    rows_ref, grad_qkv_ref, grad_table_ref = refs[count + 5 : count + 8]
    part_refs = refs[count + 8 : 2 * count + 8]
    held_ref, sum_ref = refs[2 * count + 8 :]
    size = blocks[0].shape[0]
    for distance, block in enumerate(blocks):
        rows_ref[row_place(index_ref, distance, size), :] = block[...]
    split_at = bound_ref[0]
    total = rows_ref.shape[0]
    width = out_weight_ref.shape[0]
    heads = width // HEAD
    span = total + BLOCK
    grad_context = dot_t(rows_ref[...], out_weight_ref[...]).astype(BF)
    grad_context_t = grad_context.astype(F32).T.astype(BF)
    qkv = qkv_ref[...]
    rows_t = qkv[:, : 2 * width].astype(F32).T.astype(BF)
    table = table_ref[...]
    moved = pltpu.roll(table.astype(F32), split_at, 0).astype(BF)
    row_ids = lax.broadcasted_iota(jnp.int32, (total, total), 0)
    places = jnp.where(row_ids < split_at, row_ids, row_ids - split_at)
    turned = lax.broadcasted_iota(jnp.int32, (total, total), 1) == total - 1 - places
    merge = jnp.where(turned, 1.0, 0.0).astype(BF)
    first_lanes = lax.broadcasted_iota(jnp.int32, (HEAD, total), 1) < split_at
    first_rows = lax.broadcasted_iota(jnp.int32, (total, HEAD), 0) < split_at
    pad = jnp.zeros((BLOCK, BLOCK), F32)
    held_ref[...] = jnp.zeros(held_ref.shape, F32)

    def along_table(merged, offset, head):
        cut = slice(offset + head * HEAD, offset + (head + 1) * HEAD)
        pair = jnp.concatenate([table[:, cut], moved[:, cut]], 1)
        turned_rows = rows_t[cut]
        zero = jnp.zeros_like(turned_rows)
        turned_rows = jnp.concatenate(
            [jnp.where(first_lanes, turned_rows, zero), jnp.where(first_lanes, zero, turned_rows)],
            0,
        )
        parts = []
        slot = offset // HEAD + head
        for start in range(0, total, BLOCK):
            block = jnp.concatenate([merged[start : start + BLOCK], pad], 1)
            block = pltpu.roll(block, 1, 1, stride=1, stride_axis=0).astype(BF)
            parts.append(dot(block, pair[start : start + span]))
            held_ref[slot, :, start : start + span] += dot(
                turned_rows[:, start : start + BLOCK], block
            )
        both = jnp.concatenate(parts, 0)
        return jnp.where(first_rows, both[:, :HEAD], both[:, HEAD:])

    grad_queries = []
    grad_keys = []
    grad_values_t = []
    for head in range(heads):
        at = head * HEAD
        cut = slice(at, at + HEAD)
        query = qkv[:, at : at + HEAD]
        key = qkv[:, width + at : width + at + HEAD]
        value = qkv[:, 2 * width + at : 2 * width + at + HEAD]
        grad_probs = dot_t(grad_context[:, cut], value)
        probs = probs_ref[head]
        centre = jnp.sum(probs * grad_probs, axis=1, keepdims=True)
        score_grad = (probs * (grad_probs - centre) * SCALE).astype(BF)
        score_grad_t = score_grad.astype(F32).T.astype(BF)
        grad_values_t.append(dot(grad_context_t[cut], probs.astype(BF)))
        grad_queries.append(dot(score_grad, key) + along_table(dot(score_grad, merge), 0, head))
        grad_keys.append(
            dot(score_grad_t, query) + along_table(dot(score_grad_t, merge), width, head)
        )
    grad_values = jnp.concatenate(grad_values_t, 0).T
    grad_qkv = jnp.concatenate(grad_queries + grad_keys + [grad_values], 1).astype(BF)
    grad_qkv_ref[...] = grad_qkv
    sum_ref[...] = dot_t(grad_qkv, qkv_weight_ref[...])
    store_parts(index_ref, sum_ref, part_refs)
    lanes = lax.broadcasted_iota(jnp.int32, (HEAD, span), 1)
    for slot in range(2 * heads):
        first = held_ref[slot, :HEAD]
        second = pltpu.roll(held_ref[slot, HEAD:], 2 * total - split_at, 1)
        both = first + second
        bottom = jnp.sum(both[:, :BLOCK], axis=1, keepdims=True)
        top = jnp.sum(both[:, 2 * total - BLOCK :], axis=1, keepdims=True)
        middle = both[:, BLOCK : 2 * total - BLOCK]
        middle = middle + jnp.where(lanes == 0, bottom, 0.0)
        middle = middle + jnp.where(lanes == span - 1, top, 0.0)
        grad_table_ref[slot * HEAD : (slot + 1) * HEAD] = middle.astype(BF)


def attend_backward(index, bound, blocks, out_weight, qkv_weight, qkv, probs, table, after):
    count = len(blocks)
    size, features = blocks[0].shape
    total = count * size
    width = out_weight.shape[0]
    outs = run_kernel(
        functools.partial(attend_back_kernel, count),
        [low((total, features)), low((total, 3 * width)), low((2 * width, total + BLOCK))]
        + part_shapes(count, size, features),
        (index, bound),
        (*blocks, out_weight, qkv_weight, qkv, probs, table),
        after=after,
        scratch=[
            pltpu.VMEM((2 * width // HEAD, 2 * HEAD, 2 * total), F32),
            pltpu.VMEM((total, features), F32),
        ],
        spare=16,
    )
    return outs[:3], outs[3:]


def feed_kernel(count, *refs):
    blocks = refs[:count]
    in_ref, down_ref = refs[count : count + 2]
    rows_ref, active_ref, slope_ref = refs[count + 2 : count + 5]
    part_refs = refs[count + 5 : 2 * count + 5]
    size = blocks[0].shape[0]
    for distance, block in enumerate(blocks):
        cut = slice(distance * size, (distance + 1) * size)
        rows = block[...]
        rows_ref[cut] = rows
        upward = dot(rows, in_ref[...])
        below = 0.5 * (1.0 + lax.erf(upward * (1.0 / math.sqrt(2.0))))
        density = jnp.exp(-0.5 * upward * upward) * (1.0 / math.sqrt(2.0 * math.pi))
        active = (upward * below).astype(BF)
        active_ref[cut] = active
        slope_ref[cut] = below + upward * density
        part_refs[distance][...] = dot(active, down_ref[...]).astype(part_refs[distance].dtype)


def feed_forward(blocks, in_weight, down_weight):
    count = len(blocks)
    size, features = blocks[0].shape
    units = in_weight.shape[1]
    total = count * size
    outs = run_kernel(
        functools.partial(feed_kernel, count),
        [low((total, features)), low((total, units)), wide((total, units))]
        + part_shapes(count, size, features),
        (),
        (*blocks, in_weight, down_weight),
    )
    return outs[:3], outs[3:]


def feed_back_kernel(count, *refs):
    blocks = refs[:count]
    in_ref, down_ref, slope_ref = refs[count : count + 3]
    rows_ref, grad_up_ref = refs[count + 3 : count + 5]
    part_refs = refs[count + 5 : 2 * count + 5]
    size = blocks[0].shape[0]
    for distance, block in enumerate(blocks):
        cut = slice(distance * size, (distance + 1) * size)
        rows = block[...]
        rows_ref[cut] = rows
        grad_up = (dot_t(rows, down_ref[...]) * slope_ref[cut]).astype(BF)
        grad_up_ref[cut] = grad_up
        part_refs[distance][...] = dot_t(grad_up, in_ref[...]).astype(part_refs[distance].dtype)


def feed_backward(blocks, in_weight, down_weight, slope, after):
    count = len(blocks)
    size, features = blocks[0].shape
    units = in_weight.shape[1]
    total = count * size
    outs = run_kernel(
        functools.partial(feed_back_kernel, count),
        [low((total, features)), low((total, units))] + part_shapes(count, size, features),
        (),
        (*blocks, in_weight, down_weight, slope),
        after=after,
    )
    return outs[:2], outs[2:]


def norm_one_kernel(count, *refs):
    rows_ref, gain_ref, bias_ref, hidden_ref, low_ref, normed_ref, inverse_ref = refs[count:]
    normed, inverse = normalize(rows_ref[...].astype(F32) + added(refs[:count]))
    hidden = normed * gain_ref[...] + bias_ref[...]
    hidden_ref[...] = hidden
    low_ref[...] = hidden.astype(BF)
    normed_ref[...] = normed
    inverse_ref[...] = inverse


def norm_one(parts, rows, gain_row, bias_row):
    shape = rows.shape
    return run_kernel(
        functools.partial(norm_one_kernel, len(parts)),
        [wide(shape), low(shape), wide(shape), wide((shape[0], 1))],
        (),
        (*parts, rows, gain_row, bias_row),
    )


def norm_two_kernel(count, *refs):
    hidden_ref, gain_ref, bias_ref, low_ref, normed_ref, inverse_ref = refs[count:]
    normed, inverse = normalize(hidden_ref[...] + added(refs[:count]))
    low_ref[...] = (normed * gain_ref[...] + bias_ref[...]).astype(BF)
    normed_ref[...] = normed
    inverse_ref[...] = inverse


def norm_two(parts, hidden, gain_row, bias_row):
    shape = hidden.shape
    return run_kernel(
        functools.partial(norm_two_kernel, len(parts)),
        [low(shape), wide(shape), wide((shape[0], 1))],
        (),
        (*parts, hidden, gain_row, bias_row),
    )


def turn_kernel(count, *refs):
    hidden_ref, gain_ref, bias_ref, grad_ref, result_ref, back_ref, low_ref, sums_ref = refs[count:]
    normed, inverse = normalize(hidden_ref[...] + added(refs[:count]))
    result_ref[...] = normed * gain_ref[...] + bias_ref[...]
    back, sums_ref[...] = normalize_back(
        grad_ref[...].astype(F32), normed, inverse, gain_ref[...]
    )
    back_ref[...] = back
    low_ref[...] = back.astype(BF)


def turn(parts, hidden, gain_row, bias_row, grad):
    shape = hidden.shape
    return run_kernel(
        functools.partial(turn_kernel, len(parts)),
        [wide(shape), wide(shape), low(shape), wide((2, shape[1]))],
        (),
        (*parts, hidden, gain_row, bias_row, grad),
    )


def norm_back_kernel(count, rounded, *refs):
    add_ref, normed_ref, inverse_ref, gain_ref, back_ref, low_ref, sums_ref = refs[count:]
    grad = add_ref[...] + added(refs[:count])
    if rounded:
        grad = grad.astype(BF).astype(F32)
    back, sums_ref[...] = normalize_back(
        grad, normed_ref[...], inverse_ref[...], gain_ref[...]
    )
    back_ref[...] = back
    low_ref[...] = back.astype(BF)


def norm_back(parts, add, normed, inverse, gain_row, rounded, after):
    shape = add.shape
    return run_kernel(
        functools.partial(norm_back_kernel, len(parts), rounded),
        [wide(shape), low(shape), wide((2, shape[1]))],
        (),
        (*parts, add, normed, inverse, gain_row),
        after=after,
    )


def feed_halves_kernel(section_ref, hidden_ref, grad_up_ref, active_ref, grad_ref, *refs):
    held_ref = refs[-1]
    pairs = ((hidden_ref, grad_up_ref, refs[:2]), (active_ref, grad_ref, refs[2:4]))
    half = held_ref.shape[0] // 2
    for left, right, (keep_ref, send_ref) in pairs:
        held_ref[...] = t_dot(left[...], right[...])
        keep_ref[...] = held_ref[row_place(section_ref, 0, half), :].astype(BF)
        send_ref[...] = held_ref[row_place(section_ref, 1, half), :].astype(BF)


def feed_halves(section, hidden, grad_up, active, grad, after=()):
    features = hidden.shape[1]
    units = active.shape[1]
    return run_kernel(
        feed_halves_kernel,
        [low((features // 2, units))] * 2 + [low((units // 2, features))] * 2,
        (section,),
        (hidden, grad_up, active, grad),
        after=after,
        scratch=[pltpu.VMEM((features, units), F32)],
        spare=8,
    )


def attend_halves_kernel(
    section_ref,
    rows_ref,
    grad_qkv_ref,
    grad_ref,
    context_ref,
    rel_ref,
    grad_table_ref,
    weight_ref,
    keep_ref,
    send_ref,
    table_ref,
    held_ref,
):
    width = context_ref.shape[1]
    of_keys = grad_table_ref[:width, :]
    of_queries = grad_table_ref[width:, :]
    rel_t = rel_ref[...].astype(F32).T.astype(BF)
    from_rows = t_dot(rows_ref[...], grad_qkv_ref[...])
    held_ref[:, :width] = from_rows[:, :width] + dot_t(rel_t, of_queries)
    held_ref[:, width : 2 * width] = from_rows[:, width : 2 * width] + dot_t(rel_t, of_keys)
    held_ref[:, 2 * width : 3 * width] = from_rows[:, 2 * width :]
    held_ref[:, 3 * width :] = t_dot(grad_ref[...], context_ref[...])
    half = held_ref.shape[0] // 2
    keep_ref[...] = held_ref[row_place(section_ref, 0, half), :].astype(BF)
    send_ref[...] = held_ref[row_place(section_ref, 1, half), :].astype(BF)
    table_ref[...] = dot_t(
        of_keys.astype(F32).T.astype(BF), weight_ref[:, width : 2 * width]
    ) + dot_t(of_queries.astype(F32).T.astype(BF), weight_ref[:, :width])


def attend_halves(section, rows, grad_qkv, grad, context, rel_table, grad_table, qkv_weight, after):
    features = rows.shape[1]
    width = context.shape[1]
    half = low((features // 2, 4 * width))
    return run_kernel(
        attend_halves_kernel,
        [half, half, wide(rel_table.shape)],
        (section,),
        (rows, grad_qkv, grad, context, rel_table, grad_table, qkv_weight),
        after=after,
        scratch=[pltpu.VMEM((features, 4 * width), F32)],
    )


class Sum:
    def __init__(self, keep, send, after=()):
        self.pairs = [(keep, swap_pipe(gate(send, after) if after else send))]
        self.held = self.final = None


def slot_kernel(pairs, first, second, third, crossing, flags_ref, *refs):
    refs = list(refs)

    def take(count):
        taken = refs[:count]
        del refs[:count]
        return taken

    entering = take(2 * pairs)
    in_first, in_second, in_third = take(first), take(second), take(third)
    (by_neighbour,) = take(1) if first or third else (None,)
    (by_middle,) = take(1) if second else (None,)
    across = take(crossing)
    at_end = flags_ref[1] == 1
    sums = {}

    def give(name, value):
        (ref,) = take(1)
        ref[...] = value
        sums[name] = value

    if pairs:
        (ref,) = take(1)
        start = 0
        for keep, arrived in zip(entering[::2], entering[1::2]):
            rows = keep.shape[0]
            ref[start : start + rows] = (keep[...].astype(F32) + arrived[...].astype(F32)).astype(BF)
            start += rows
        sums["entered"] = ref[...]
    if first:
        held = in_first[0][...]
        arrived = by_neighbour[: held.shape[0]]
        total = (held.astype(F32) + arrived.astype(F32)).astype(BF)
        give("first", jnp.where(at_end, held, total))
    if second:
        held = in_second[0][...].astype(F32)
        give("second", (held + by_middle[: held.shape[0]].astype(F32)).astype(BF))
    if third:
        held = in_third[0][...]
        give("third", jnp.where(at_end, by_neighbour[: held.shape[0]], held))
    if pairs and second:
        (ref,) = take(1)
        small, large = sums["second"].shape[0], sums["entered"].shape[0]
        ref[:small] = jnp.where(at_end, sums["entered"][:small], sums["second"])
        if large > small:
            ref[small:] = sums["entered"][small:]
    if crossing:
        (ref,) = take(1)
        from_zero = across[0][...]
        from_one = across[1][...] if crossing == 2 else sums["third"]
        ref[...] = jnp.where(flags_ref[0] == 0, from_zero, from_one)


class Line:
    def __init__(self, flags):
        self.flags = flags
        self.direct = lax.axis_size("dp") == 4
        self.first = self.second = self.third = None
        self.by_neighbour = self.by_middle = None

    def slot(self, entering=None, crossing=(), after=()):
        first, second, third = self.first, self.second, self.third
        arrays = [array for pair in (entering.pairs if entering else ()) for array in pair]
        outs = []
        if entering:
            rows = sum(keep.shape[0] for keep, moved in entering.pairs)
            outs.append(low((rows, arrays[0].shape[1])))
        for one in (first, second, third):
            if one:
                arrays.append(one.held)
                outs.append(low(one.held.shape))
        if first or third:
            arrays.append(self.by_neighbour)
        if second:
            arrays.append(self.by_middle)
        across = [one.final for one in crossing if one.final is not None]
        arrays += across
        if entering and second:
            outs.append(outs[0])
        if crossing:
            outs.append(low(across[0].shape))
        body = functools.partial(
            slot_kernel,
            len(entering.pairs) if entering else 0,
            int(first is not None),
            int(second is not None),
            int(third is not None),
            len(across),
        )
        if not outs:
            return []
        results = list(run_kernel(body, outs, (self.flags,), arrays, after=after))
        done = list(results)
        payload = None
        if entering:
            payload = entering.held = results.pop(0)
        if first:
            first.held = results.pop(0)
        if second:
            second.held = results.pop(0)
            payload = second.held if payload is None else payload
        if third:
            third.final = results.pop(0)
        if entering and second:
            payload = results.pop(0)
        if not self.direct:
            if entering:
                entering.final = lax.psum(entering.held, "dp")
        else:
            if payload is not None:
                self.by_neighbour = lax.ppermute(
                    payload, "dp", [(0, 1), (1, 0), (2, 3), (3, 2)]
                )
            if first:
                self.by_middle = lax.ppermute(first.held, "dp", [(1, 2), (2, 1)])
            self.first, self.second, self.third = entering, first, second
        if crossing:
            return done, swap_pipe(results.pop(0))
        return done


def table_kernel(rel_ref, weight_ref, out_ref):
    width = weight_ref.shape[1] // 3
    out_ref[:, :width] = dot(rel_ref[...], weight_ref[:, width : 2 * width]).astype(BF)
    out_ref[:, width:] = dot(rel_ref[...], weight_ref[:, :width]).astype(BF)


def table_rows(rel_rows, qkv_weight):
    outs = [low((rel_rows.shape[0], 2 * qkv_weight.shape[1] // 3))]
    return run_kernel(table_kernel, outs, (), (rel_rows, qkv_weight))[0]


def halved(part, axis, distance):
    bit = (lax.axis_index(axis) // distance) % 2
    half = part.shape[0] // 2
    keep = lax.dynamic_slice_in_dim(part, bit * half, half, 0)
    send = lax.dynamic_slice_in_dim(part, (1 - bit) * half, half, 0).astype(BF)
    return keep + to_partner(send, axis, distance).astype(F32)


def rejoined(part, axis, distance):
    bit = (lax.axis_index(axis) // distance) % 2
    other = to_partner(part, axis, distance)
    return jnp.where(
        bit == 0, jnp.concatenate([part, other], 0), jnp.concatenate([other, part], 0)
    )


def join_kernel(cuts, section_ref, *refs):
    out_refs = refs[4:]
    half = refs[3].shape[0]

    def write(first_ref, second_ref):
        if cuts is None:
            out_refs[0][:half] = first_ref[...].astype(F32)
            out_refs[0][half:] = second_ref[...].astype(F32)
            return
        for number, out_ref in enumerate(out_refs[:-1]):
            cut = slice(cuts * number, cuts * (number + 1))
            out_ref[:half] = first_ref[:half, cut].astype(F32)
            out_ref[half:] = second_ref[:half, cut].astype(F32)
        last = slice(cuts * (len(out_refs) - 1), None)
        out_refs[-1][:, :half] = first_ref[:half, last].astype(F32).T
        out_refs[-1][:, half:] = second_ref[:half, last].astype(F32).T

    @pl.when(section_ref[0] == 0)
    def first_section():
        write(refs[0], refs[1])

    @pl.when(section_ref[0] == 1)
    def second_section():
        write(refs[3], refs[2])


def join(section, halves, cuts=None):
    arrays = [array for pair in halves for array in pair]
    rows, columns = 2 * arrays[2].shape[0], arrays[2].shape[1]
    if cuts is None:
        outs = [wide((rows, columns))]
    else:
        outs = [wide((rows, cuts))] * 3 + [wide((cuts, rows))]
    return run_kernel(functools.partial(join_kernel, cuts), outs, (section,), arrays)


def choose_kernel(flags_ref, own_ref, mine_ref, theirs_ref, first_ref, second_ref):
    half = mine_ref.shape[0]
    own = row_place(flags_ref.at[pl.ds(1, 1)], 0, half)
    other = row_place(flags_ref.at[pl.ds(1, 1)], 1, half)

    def write(own_out_ref, other_out_ref):
        own_out_ref[...] = own_ref[...]
        other_out_ref[own, :] = mine_ref[...]
        other_out_ref[other, :] = theirs_ref[...]

    @pl.when(flags_ref[0] == 0)
    def first_section():
        write(first_ref, second_ref)

    @pl.when(flags_ref[0] == 1)
    def second_section():
        write(second_ref, first_ref)


def both_layers(flags, own, mine, theirs, after=()):
    shape = low(own.shape)
    return run_kernel(choose_kernel, [shape, shape], (flags,), (own, mine, theirs), after=after)


def per_device(
    pipe_ends,
    bounds,
    query_weight,
    key_weight,
    value_weight,
    attention_out_weight,
    feedforward_in_weight,
    down_weight,
    norm_gain,
    norm_bias,
    rel_table,
):
    section = lax.axis_index("pipe")
    index = lax.axis_index("tensor").reshape(1)
    section_index = section.reshape(1)
    ends = pipe_ends[0, :, 0]
    size = ends.shape[1]
    total = size * lax.axis_size("tensor")
    buckets, features = rel_table.shape
    width = query_weight.shape[2]
    bound = lax.dynamic_index_in_dim(bounds, section, 0, keepdims=False)[0]
    parity = lax.axis_index("dp") % 2
    flags = jnp.stack([section, parity])

    def own_half(weight):
        half = weight.shape[0] // 2
        return lax.dynamic_slice_in_dim(weight, parity * half, half, 0)

    def of_layer(layer, own, other):
        return jnp.where(section == layer, own, other)

    qkv_own = jnp.concatenate([query_weight[0], key_weight[0], value_weight[0]], 1)
    out_own, in_own, down_own = attention_out_weight[0], feedforward_in_weight[0], down_weight[0]
    qkv_mine = swap_pipe(own_half(qkv_own))
    from_other = swap_pipe(lax.dynamic_index_in_dim(ends, 1 - section, 0, keepdims=False))
    out_other = swap_pipe(out_own)
    own_norms = jnp.concatenate([norm_gain[0], norm_bias[0]], 0)
    other_norms = swap_pipe(own_norms)
    qkv_theirs = to_partner(qkv_mine, "dp", 1)
    first_in = jnp.where(section == 0, ends[0], from_other)
    last_grad = jnp.where(section == 0, from_other, ends[1])
    first_blocks = spread(first_in)
    in_mine = swap_pipe(gate(own_half(in_own), [first_in]))
    down_mine = swap_pipe(gate(own_half(down_own), [out_other]))
    norms = [of_layer(layer, own_norms, other_norms)[:, None] for layer in range(2)]
    qkv_weights = both_layers(flags, qkv_own, qkv_mine, qkv_theirs)
    out_weights = [of_layer(layer, out_own, out_other) for layer in range(2)]
    by_place = jnp.arange(2 * total, dtype=jnp.int32)
    near_rows = jnp.clip(by_place - (total - buckets // 2), 0, buckets - 1)

    def rel_rows(pick):
        one_hot = pick[:, None] == jnp.arange(buckets, dtype=jnp.int32)[None, :]
        return dot(one_hot.astype(BF), rel_table).astype(BF)

    key_first = rel_rows(buckets - 1 - jnp.clip(by_place - (total - buckets // 2), 0, buckets - 1))
    query_first = rel_rows(near_rows)

    saved = []
    rows = first_in
    in_weights = down_weights = None
    for layer in range(2):
        gain_bias = norms[layer]
        attended, parts = attend_forward(
            index,
            bound,
            spread(rows) if layer else first_blocks,
            qkv_weights[layer],
            out_weights[layer],
            table_rows(key_first, qkv_weights[layer]),
        )
        if layer == 0:
            in_theirs = to_partner(gate(in_mine, [parts[0]]), "dp", 1)
        hidden, hidden_low, normed_one, inverse_one = norm_one(
            exchange(parts), rows, gain_bias[0], gain_bias[2]
        )
        if layer == 0:
            down_theirs = to_partner(gate(down_mine, [hidden]), "dp", 1)
            in_weights = both_layers(flags, in_own, in_mine, in_theirs)
            down_weights = both_layers(flags, down_own, down_mine, down_theirs)
        fed, parts = feed_forward(spread(hidden_low), in_weights[layer], down_weights[layer])
        parts = exchange(parts)
        kept = [attended, fed, normed_one, inverse_one]
        if layer == 0:
            rows, normed_two, inverse_two = norm_two(parts, hidden, gain_bias[1], gain_bias[3])
            kept += [normed_two, inverse_two]
        saved.append(kept)
    result, back_two, back_low, sums_two = turn(
        parts, hidden, gain_bias[1], gain_bias[3], last_grad
    )
    other_result = lax.ppermute(result.astype(BF), "pipe", [(0, 1)])

    norm_sums = [[None, None], [None, None]]
    norm_sums[1][1] = sums_two

    def back_feed(layer):
        hidden_whole, active, slope = saved[layer][1]
        (grad_ffn, grad_up), parts = feed_backward(
            spread(back_low), in_weights[layer], down_weights[layer], slope, ()
        )
        return exchange(parts), (hidden_whole, grad_up, active, grad_ffn)

    def back_attention(layer, blocks, after=()):
        rows_whole, qkv, probs, context = saved[layer][0]
        (grad_whole, grad_qkv, grad_table), parts = attend_backward(
            index,
            bound,
            blocks,
            out_weights[layer],
            qkv_weights[layer],
            qkv,
            probs,
            table_rows(query_first, qkv_weights[layer]),
            after,
        )
        factors = (
            rows_whole, grad_qkv, grad_whole, context, rel_table, grad_table, qkv_weights[layer]
        )
        return exchange(parts), factors

    place = lax.axis_index("dp")
    line = Line(jnp.stack([section, ((place == 0) | (place == 3)).astype(jnp.int32)]))
    parts, factors = back_feed(1)
    feed = feed_halves(section_index, *factors)
    in_1 = Sum(*feed[:2])
    normed, inverse = saved[1][2:4]
    back_two, back_low, norm_sums[1][0] = norm_back(
        parts, back_two, normed, inverse, norms[1][0], False, feed
    )
    blocks = spread(back_low)
    done = line.slot(in_1, after=blocks[1:2])
    down_send = gate(feed[3], done)
    down_1 = Sum(feed[2], down_send)
    parts, factors = back_attention(1, blocks, [down_send])
    *held, table_1 = attend_halves(section_index, *factors, ())
    done = line.slot(down_1, after=held)
    attention_1 = Sum(*held, done)
    normed, inverse = saved[0][4:]
    back_two, back_low, norm_sums[0][1] = norm_back(
        parts, back_two, normed, inverse, norms[0][1], True, done
    )
    parts, factors = back_feed(0)
    done = line.slot(attention_1, after=factors[1:2])
    feed = feed_halves(section_index, *factors, done)
    in_0 = Sum(*feed[:2])
    normed, inverse = saved[0][2:4]
    back_two, back_low, norm_sums[0][0] = norm_back(
        parts, back_two, normed, inverse, norms[0][0], False, feed
    )
    blocks = spread(back_low)
    done = line.slot(in_0, after=blocks[1:2])
    down_send = gate(feed[3], done)
    down_0 = Sum(feed[2], down_send)
    parts, factors = back_attention(0, blocks, [down_send])
    done = line.slot(down_0, after=factors[1:2])
    *held, table_0 = attend_halves(section_index, *factors, done)
    attention_0 = Sum(*held)
    grad = back_two
    for part in parts:
        grad = grad + part.astype(F32)
    positions = 2 * lax.axis_size("tensor")
    norm_rows = jnp.concatenate([rows for pair in norm_sums for rows in pair], 0)
    small = jnp.concatenate(
        [
            (table_0 + table_1).reshape(positions, -1, features),
            norm_rows.reshape(positions, -1, features),
            jnp.zeros((positions, 15, features), F32),
        ],
        1,
    )
    small = small.reshape(-1, features)
    small = halved(halved(small, "tensor", 1), "tensor", 2)
    half = small.shape[0] // 2
    small_keep = lax.dynamic_slice_in_dim(small, section * half, half, 0).astype(BF)
    small_send = lax.dynamic_slice_in_dim(small, (1 - section) * half, half, 0).astype(BF)
    attention_0.pairs.append((small_keep, swap_pipe(small_send)))
    done = line.slot(attention_0)
    in_1_other = lax.ppermute(in_1.final, "pipe", [(0, 1)])
    other_grad = lax.ppermute(grad.astype(BF), "pipe", [(1, 0)])
    done, crossed_one = line.slot(None, (down_1, in_0), [in_1_other, other_grad])
    done, crossed_two = line.slot(None, (attention_1, down_0), [crossed_one])
    (into,) = join(section_index, [(in_0.final, crossed_one), (in_1.final, in_1_other)])
    line.slot(None, after=[crossed_two])
    crossed_three = swap_pipe(attention_0.final)
    (downward,) = join(section_index, [(down_0.final, crossed_two), (down_1.final, crossed_one)])
    end_values = jnp.where(
        section == 0,
        jnp.stack([grad, other_grad.astype(F32)]),
        jnp.stack([other_result.astype(F32), result]),
    )
    attention = join(
        section_index,
        [(attention_0.final, crossed_three), (attention_1.final, crossed_two)],
        width,
    )
    small = [attention_0.final[-half:], crossed_three[-half:]]
    small = jnp.where(section == 0, jnp.concatenate(small, 0), jnp.concatenate(small[::-1], 0))
    small = rejoined(rejoined(small, "tensor", 2), "tensor", 1).astype(F32)
    small = small.reshape(positions, half, features)
    of_table = buckets // positions
    table_grad = small[:, :of_table].reshape(buckets, features)
    norm_rows = small[:, of_table : half - 15].reshape(2, 2, 2, features)
    norm_rows = lax.dynamic_index_in_dim(norm_rows, section, 0, keepdims=False)
    return (
        end_values[None, :, None],
        *(grad[None] for grad in attention),
        into[None],
        downward[None],
        norm_rows[:, 0][None],
        norm_rows[:, 1][None],
        table_grad,
    )


def solution(mesh):
    in_specs = (
        P("pipe", None, "dp", "tensor", None),
        P(None, "dp", None),
        P("pipe", None, "tensor"),
        P("pipe", None, "tensor"),
        P("pipe", None, "tensor"),
        P("pipe", "tensor", None),
        P("pipe", None, "tensor"),
        P("pipe", "tensor", None),
        P("pipe", None, None),
        P("pipe", None, None),
        P(),
    )
    out_specs = (
        P("pipe", None, "dp", "tensor", None),
        P("pipe", None, "tensor"),
        P("pipe", None, "tensor"),
        P("pipe", None, "tensor"),
        P("pipe", "tensor", None),
        P("pipe", None, "tensor"),
        P("pipe", "tensor", None),
        P("pipe", None, None),
        P("pipe", None, None),
        P(),
    )
    return jax.shard_map(
        per_device, mesh=mesh, in_specs=in_specs, out_specs=out_specs, check_vma=False
    )
```

```python
import functools
import math

import jax
import jax.numpy as jnp
from jax import lax
from jax.experimental import pallas as pl
from jax.experimental.pallas import tpu as pltpu
from jax.sharding import PartitionSpec as P

HEAD = 64
BLOCK = 128
EPSILON = 1e-05
MASKED = -1e30
BF = jnp.bfloat16
F32 = jnp.float32
SCALE = (3.0 * HEAD) ** (-0.5)


def dot(left, right):
    return lax.dot_general(left, right, (((1,), (0,)), ((), ())), preferred_element_type=F32)


def dot_t(left, right):
    return lax.dot_general(left, right, (((1,), (1,)), ((), ())), preferred_element_type=F32)


def t_dot(left, right):
    return lax.dot_general(left, right, (((0,), (0,)), ((), ())), preferred_element_type=F32)


def low(shape):
    return jax.ShapeDtypeStruct(shape, BF)


def wide(shape):
    return jax.ShapeDtypeStruct(shape, F32)


def run_kernel(body, outs, scalars, arrays, after=(), scratch=(), spare=4, far=0):
    after = tuple(after)
    held = sum(math.prod(one.shape) * one.dtype.itemsize for one in (*outs, *arrays, *scratch))
    vmem = pl.BlockSpec(memory_space=pltpu.VMEM)
    lead = len(scalars) + len(arrays)
    near = len(outs) - far

    def whole_body(*refs):
        results = refs[lead + len(after) : lead + len(after) + len(outs)]
        rest = refs[lead + len(after) + len(outs) :]
        if not far:
            body(*refs[:lead], *results, *rest)
            return
        held_results, semaphores = rest[-1 - far : -1], rest[-1]
        body(*refs[:lead], *results[:near], *held_results, *rest[: -1 - far])
        copies = [
            pltpu.make_async_copy(source, target, semaphores.at[number])
            for number, (source, target) in enumerate(zip(held_results, results[near:]))
        ]
        for copy in copies:
            copy.start()
        for copy in copies:
            copy.wait()

    scratch = list(scratch)
    if far:
        scratch += [pltpu.VMEM(one.shape, one.dtype) for one in outs[near:]]
        scratch.append(pltpu.SemaphoreType.DMA((far,)))
    return pl.pallas_call(
        whole_body,
        out_shape=tuple(
            one if number < near else pltpu.HBM(one.shape, one.dtype)
            for number, one in enumerate(outs)
        ),
        in_specs=[pl.BlockSpec(memory_space=pltpu.SMEM)] * len(scalars)
        + [vmem] * len(arrays)
        + [pl.BlockSpec(memory_space=pl.ANY)] * len(after),
        out_specs=tuple(
            vmem if number < near else pl.BlockSpec(memory_space=pltpu.HBM)
            for number in range(len(outs))
        ),
        scratch_shapes=scratch,
        compiler_params=pltpu.CompilerParams(vmem_limit_bytes=held + spare * 2**20),
    )(*scalars, *arrays, *after)


def gate(array, after):
    def nothing(*refs):
        del refs

    anywhere = pl.BlockSpec(memory_space=pl.ANY)
    return pl.pallas_call(
        nothing,
        out_shape=jax.ShapeDtypeStruct(array.shape, array.dtype),
        in_specs=[anywhere] * (1 + len(after)),
        out_specs=anywhere,
        input_output_aliases={0: 0},
    )(array, *after)


def to_partner(block, axis, distance):
    count = lax.axis_size(axis)
    return lax.ppermute(block, axis, [(i, i ^ distance) for i in range(count)])


def swap_pipe(block):
    return to_partner(block, "pipe", 1)


def spread(block):
    count = lax.axis_size("tensor")
    distances = [2**step for step in range(1, count.bit_length() - 1)]
    blocks = {0: block}
    for distance in distances:
        blocks.update({d + distance: to_partner(blocks[d], "tensor", distance) for d in list(blocks)})
    blocks.update({d + 1: to_partner(blocks[d], "tensor", 1) for d in list(blocks)})
    return [blocks[d] for d in range(count)]


def exchange(parts):
    return [parts[0]] + [to_partner(parts[d], "tensor", d) for d in range(1, len(parts))]


def row_place(index_ref, distance, size):
    return pl.ds(pl.multiple_of((index_ref[0] ^ distance) * size, size), size)


def store_parts(index_ref, whole_ref, part_refs):
    size = part_refs[0].shape[0]
    for distance, part_ref in enumerate(part_refs):
        part_ref[...] = whole_ref[row_place(index_ref, distance, size), :].astype(part_ref.dtype)


def part_shapes(count, size, features):
    return [wide((size, features))] + [low((size, features))] * (count - 1)


def added(refs):
    total = refs[0][...].astype(F32)
    for ref in refs[1:]:
        total = total + ref[...].astype(F32)
    return total


def normalize(summed):
    row_mean = jnp.mean(summed, axis=-1, keepdims=True)
    centred = summed - row_mean
    spread_of = jnp.mean(centred * centred, axis=-1, keepdims=True)
    inverse = lax.rsqrt(spread_of + EPSILON)
    return centred * inverse, inverse


def normalize_back(grad_result, normed, inverse, gain_row):
    sums = jnp.concatenate(
        [
            jnp.sum(grad_result * normed, axis=0, keepdims=True),
            jnp.sum(grad_result, axis=0, keepdims=True),
        ],
        0,
    )
    scaled = grad_result * gain_row
    centre_one = jnp.mean(scaled, axis=-1, keepdims=True)
    centre_two = jnp.mean(scaled * normed, axis=-1, keepdims=True)
    return inverse * (scaled - centre_one - normed * centre_two), sums


def by_segment(rows, split_at):
    first = lax.broadcasted_iota(jnp.int32, rows.shape, 0) < split_at
    zero = jnp.zeros_like(rows)
    return jnp.concatenate([jnp.where(first, rows, zero), jnp.where(first, zero, rows)], axis=1)


def placed_blocks(rows, first_table, second_table, first_columns):
    total = rows.shape[0]
    span = total + BLOCK
    blocks = []
    for start in range(0, total, BLOCK):
        begin = total - BLOCK - start
        part = rows[start : start + BLOCK]
        first = dot_t(part, first_table[begin : begin + span])
        second = dot_t(part, second_table[begin : begin + span])
        first = pltpu.roll(first, total + 1, 1, stride=1, stride_axis=0)[:, :total]
        second = pltpu.roll(second, total + 1, 1, stride=1, stride_axis=0)[:, :total]
        blocks.append(jnp.where(first_columns, first, second))
    return blocks


def attend_kernel(count, index_ref, bound_ref, *refs):
    blocks = refs[:count]
    qkv_weight_ref, out_weight_ref, table_ref = refs[count : count + 3]
    rows_ref, qkv_ref, context_ref, probs_ref = refs[count + 3 : count + 7]
    part_refs = refs[count + 7 : 2 * count + 7]
    held_ref = refs[2 * count + 7]
    size = blocks[0].shape[0]
    for distance, block in enumerate(blocks):
        rows_ref[row_place(index_ref, distance, size), :] = block[...]
    split_at = bound_ref[0]
    total = rows_ref.shape[0]
    width = out_weight_ref.shape[0]
    qkv = dot_t(rows_ref[...], qkv_weight_ref[...]).astype(BF)
    qkv_ref[...] = qkv
    table = table_ref[...]
    table_wide = table.astype(F32)
    later = pltpu.roll(table_wide, 2 * total - split_at, 0).astype(BF)
    earlier = pltpu.roll(table_wide, split_at, 0).astype(BF)
    first_columns = lax.broadcasted_iota(jnp.int32, (BLOCK, total), 1) < split_at
    live = lax.broadcasted_iota(jnp.int32, (total, total), 1) < bound_ref[1]
    contexts = []
    for head in range(width // HEAD):
        at = head * HEAD
        query = qkv[:, at : at + HEAD]
        key = qkv[:, width + at : width + at + HEAD]
        value = qkv[:, 2 * width + at : 2 * width + at + HEAD]

        def tables(offset):
            cut = slice(offset + at, offset + at + HEAD)
            return (
                jnp.concatenate([table[:, cut], later[:, cut]], 1),
                jnp.concatenate([earlier[:, cut], table[:, cut]], 1),
            )

        near = jnp.concatenate(
            placed_blocks(by_segment(query, split_at), *tables(0), first_columns), 0
        )
        far = placed_blocks(by_segment(key, split_at), *tables(width), first_columns)
        far = jnp.concatenate([block.T for block in far], 1)
        scores = jnp.where(live, (dot_t(query, key) + near + far) * SCALE, MASKED)
        raised = jnp.exp(scores - jnp.max(scores, axis=1, keepdims=True))
        probs = raised / jnp.sum(raised, axis=1, keepdims=True)
        probs_ref[head] = probs
        contexts.append(dot(probs.astype(BF), value).astype(BF))
    context = jnp.concatenate(contexts, 1)
    context_ref[...] = context
    held_ref[...] = dot(context, out_weight_ref[...])
    store_parts(index_ref, held_ref, part_refs)


def attend_forward(index, bound, blocks, qkv_weight, out_weight, table):
    count = len(blocks)
    size, features = blocks[0].shape
    total = count * size
    width = out_weight.shape[0]
    outs = run_kernel(
        functools.partial(attend_kernel, count),
        [
            low((total, features)),
            low((total, 3 * width)),
            low((total, width)),
            wide((width // HEAD, total, total)),
        ]
        + part_shapes(count, size, features),
        (index, bound),
        (*blocks, qkv_weight, out_weight, table),
        scratch=[pltpu.VMEM((total, features), F32)],
        spare=16,
    )
    return outs[:4], outs[4:]


def attend_back_kernel(count, index_ref, bound_ref, *refs):
    blocks = refs[:count]
    out_weight_ref, qkv_weight_ref, qkv_ref, probs_ref, table_ref = refs[count : count + 5]
    rows_ref, grad_qkv_ref, grad_table_ref = refs[count + 5 : count + 8]
    part_refs = refs[count + 8 : 2 * count + 8]
    held_ref, sum_ref = refs[2 * count + 8 :]
    size = blocks[0].shape[0]
    for distance, block in enumerate(blocks):
        rows_ref[row_place(index_ref, distance, size), :] = block[...]
    split_at = bound_ref[0]
    total = rows_ref.shape[0]
    width = out_weight_ref.shape[0]
    heads = width // HEAD
    span = total + BLOCK
    grad_context = dot_t(rows_ref[...], out_weight_ref[...]).astype(BF)
    grad_context_t = grad_context.astype(F32).T.astype(BF)
    qkv = qkv_ref[...]
    rows_t = qkv[:, : 2 * width].astype(F32).T.astype(BF)
    table = table_ref[...]
    moved = pltpu.roll(table.astype(F32), split_at, 0).astype(BF)
    row_ids = lax.broadcasted_iota(jnp.int32, (total, total), 0)
    places = jnp.where(row_ids < split_at, row_ids, row_ids - split_at)
    turned = lax.broadcasted_iota(jnp.int32, (total, total), 1) == total - 1 - places
    merge = jnp.where(turned, 1.0, 0.0).astype(BF)
    first_lanes = lax.broadcasted_iota(jnp.int32, (HEAD, total), 1) < split_at
    first_rows = lax.broadcasted_iota(jnp.int32, (total, HEAD), 0) < split_at
    pad = jnp.zeros((BLOCK, BLOCK), F32)
    held_ref[...] = jnp.zeros(held_ref.shape, F32)

    def along_table(merged, offset, head):
        cut = slice(offset + head * HEAD, offset + (head + 1) * HEAD)
        pair = jnp.concatenate([table[:, cut], moved[:, cut]], 1)
        turned_rows = rows_t[cut]
        zero = jnp.zeros_like(turned_rows)
        turned_rows = jnp.concatenate(
            [jnp.where(first_lanes, turned_rows, zero), jnp.where(first_lanes, zero, turned_rows)],
            0,
        )
        parts = []
        slot = offset // HEAD + head
        for start in range(0, total, BLOCK):
            block = jnp.concatenate([merged[start : start + BLOCK], pad], 1)
            block = pltpu.roll(block, 1, 1, stride=1, stride_axis=0).astype(BF)
            parts.append(dot(block, pair[start : start + span]))
            held_ref[slot, :, start : start + span] += dot(
                turned_rows[:, start : start + BLOCK], block
            )
        both = jnp.concatenate(parts, 0)
        return jnp.where(first_rows, both[:, :HEAD], both[:, HEAD:])

    grad_queries = []
    grad_keys = []
    grad_values_t = []
    for head in range(heads):
        at = head * HEAD
        cut = slice(at, at + HEAD)
        query = qkv[:, at : at + HEAD]
        key = qkv[:, width + at : width + at + HEAD]
        value = qkv[:, 2 * width + at : 2 * width + at + HEAD]
        grad_probs = dot_t(grad_context[:, cut], value)
        probs = probs_ref[head]
        centre = jnp.sum(probs * grad_probs, axis=1, keepdims=True)
        score_grad = (probs * (grad_probs - centre) * SCALE).astype(BF)
        score_grad_t = score_grad.astype(F32).T.astype(BF)
        grad_values_t.append(dot(grad_context_t[cut], probs.astype(BF)))
        grad_queries.append(dot(score_grad, key) + along_table(dot(score_grad, merge), 0, head))
        grad_keys.append(
            dot(score_grad_t, query) + along_table(dot(score_grad_t, merge), width, head)
        )
    grad_values = jnp.concatenate(grad_values_t, 0).T
    grad_qkv = jnp.concatenate(grad_queries + grad_keys + [grad_values], 1).astype(BF)
    grad_qkv_ref[...] = grad_qkv
    sum_ref[...] = dot(grad_qkv, qkv_weight_ref[...])
    store_parts(index_ref, sum_ref, part_refs)
    lanes = lax.broadcasted_iota(jnp.int32, (HEAD, span), 1)
    for slot in range(2 * heads):
        first = held_ref[slot, :HEAD]
        second = pltpu.roll(held_ref[slot, HEAD:], 2 * total - split_at, 1)
        both = first + second
        bottom = jnp.sum(both[:, :BLOCK], axis=1, keepdims=True)
        top = jnp.sum(both[:, 2 * total - BLOCK :], axis=1, keepdims=True)
        middle = both[:, BLOCK : 2 * total - BLOCK]
        middle = middle + jnp.where(lanes == 0, bottom, 0.0)
        middle = middle + jnp.where(lanes == span - 1, top, 0.0)
        grad_table_ref[slot * HEAD : (slot + 1) * HEAD] = middle.astype(BF)


def attend_backward(index, bound, blocks, out_weight, qkv_weight, qkv, probs, table, after):
    count = len(blocks)
    size, features = blocks[0].shape
    total = count * size
    width = out_weight.shape[0]
    outs = run_kernel(
        functools.partial(attend_back_kernel, count),
        [low((total, features)), low((total, 3 * width)), low((2 * width, total + BLOCK))]
        + part_shapes(count, size, features),
        (index, bound),
        (*blocks, out_weight, qkv_weight, qkv, probs, table),
        after=after,
        scratch=[
            pltpu.VMEM((2 * width // HEAD, 2 * HEAD, 2 * total), F32),
            pltpu.VMEM((total, features), F32),
        ],
        spare=16,
    )
    return outs[:3], outs[3:]


def feed_kernel(count, *refs):
    blocks = refs[:count]
    in_ref, down_ref = refs[count : count + 2]
    rows_ref, active_ref, slope_ref = refs[count + 2 : count + 5]
    part_refs = refs[count + 5 : 2 * count + 5]
    size = blocks[0].shape[0]
    for distance, block in enumerate(blocks):
        cut = slice(distance * size, (distance + 1) * size)
        rows = block[...]
        rows_ref[cut] = rows
        upward = dot(rows, in_ref[...])
        below = 0.5 * (1.0 + lax.erf(upward * (1.0 / math.sqrt(2.0))))
        density = jnp.exp(-0.5 * upward * upward) * (1.0 / math.sqrt(2.0 * math.pi))
        active = (upward * below).astype(BF)
        active_ref[cut] = active
        slope_ref[cut] = below + upward * density
        part_refs[distance][...] = dot(active, down_ref[...]).astype(part_refs[distance].dtype)


def feed_forward(blocks, in_weight, down_weight):
    count = len(blocks)
    size, features = blocks[0].shape
    units = in_weight.shape[1]
    total = count * size
    outs = run_kernel(
        functools.partial(feed_kernel, count),
        [low((total, features)), low((total, units)), wide((total, units))]
        + part_shapes(count, size, features),
        (),
        (*blocks, in_weight, down_weight),
    )
    return outs[:3], outs[3:]


def feed_back_kernel(count, *refs):
    blocks = refs[:count]
    in_ref, down_ref, slope_ref = refs[count : count + 3]
    rows_ref, grad_up_ref = refs[count + 3 : count + 5]
    part_refs = refs[count + 5 : 2 * count + 5]
    size = blocks[0].shape[0]
    for distance, block in enumerate(blocks):
        cut = slice(distance * size, (distance + 1) * size)
        rows = block[...]
        rows_ref[cut] = rows
        grad_up = (dot_t(rows, down_ref[...]) * slope_ref[cut]).astype(BF)
        grad_up_ref[cut] = grad_up
        part_refs[distance][...] = dot_t(grad_up, in_ref[...]).astype(part_refs[distance].dtype)


def feed_backward(blocks, in_weight, down_weight, slope, after):
    count = len(blocks)
    size, features = blocks[0].shape
    units = in_weight.shape[1]
    total = count * size
    outs = run_kernel(
        functools.partial(feed_back_kernel, count),
        [low((total, features)), low((total, units))] + part_shapes(count, size, features),
        (),
        (*blocks, in_weight, down_weight, slope),
        after=after,
    )
    return outs[:2], outs[2:]


def norm_one_kernel(count, *refs):
    rows_ref, gain_ref, bias_ref, low_ref, normed_ref, inverse_ref = refs[count:]
    normed, inverse = normalize(rows_ref[...].astype(F32) + added(refs[:count]))
    low_ref[...] = (normed * gain_ref[...] + bias_ref[...]).astype(BF)
    normed_ref[...] = normed
    inverse_ref[...] = inverse


def norm_one(parts, rows, gain_row, bias_row, after=()):
    shape = rows.shape
    return run_kernel(
        functools.partial(norm_one_kernel, len(parts)),
        [low(shape), wide(shape), wide((shape[0], 1))],
        (),
        (*parts, rows, gain_row, bias_row),
        after=after,
    )


def norm_two_kernel(count, *refs):
    before_ref, gains_ref, low_ref, normed_ref, inverse_ref = refs[count:]
    hidden = before_ref[...] * gains_ref[0:1] + gains_ref[2:3]
    normed, inverse = normalize(hidden + added(refs[:count]))
    low_ref[...] = (normed * gains_ref[1:2] + gains_ref[3:4]).astype(BF)
    normed_ref[...] = normed
    inverse_ref[...] = inverse


def norm_two(parts, before, gains, after=()):
    shape = before.shape
    return run_kernel(
        functools.partial(norm_two_kernel, len(parts)),
        [low(shape), wide(shape), wide((shape[0], 1))],
        (),
        (*parts, before, gains),
        after=after,
    )


def turn_kernel(count, *refs):
    before_ref, gains_ref, grad_ref, result_ref, back_ref, low_ref, sums_ref = refs[count:]
    hidden = before_ref[...] * gains_ref[0:1] + gains_ref[2:3]
    normed, inverse = normalize(hidden + added(refs[:count]))
    result_ref[...] = normed * gains_ref[1:2] + gains_ref[3:4]
    back, sums_ref[...] = normalize_back(
        grad_ref[...].astype(F32), normed, inverse, gains_ref[1:2]
    )
    back_ref[...] = back
    low_ref[...] = back.astype(BF)


def turn(parts, before, gains, grad):
    shape = before.shape
    return run_kernel(
        functools.partial(turn_kernel, len(parts)),
        [wide(shape), wide(shape), low(shape), wide((2, shape[1]))],
        (),
        (*parts, before, gains, grad),
    )


def norm_back_kernel(count, rounded, *refs):
    add_ref, normed_ref, inverse_ref, gain_ref, back_ref, low_ref, sums_ref = refs[count:]
    grad = add_ref[...] + added(refs[:count])
    if rounded:
        grad = grad.astype(BF).astype(F32)
    back, sums_ref[...] = normalize_back(
        grad, normed_ref[...], inverse_ref[...], gain_ref[...]
    )
    back_ref[...] = back
    low_ref[...] = back.astype(BF)


def norm_back(parts, add, normed, inverse, gain_row, rounded, after):
    shape = add.shape
    return run_kernel(
        functools.partial(norm_back_kernel, len(parts), rounded),
        [wide(shape), low(shape), wide((2, shape[1]))],
        (),
        (*parts, add, normed, inverse, gain_row),
        after=after,
    )


def feed_halves_kernel(section_ref, hidden_ref, grad_up_ref, active_ref, grad_ref, *refs):
    held_ref = refs[-1]
    pairs = ((hidden_ref, grad_up_ref, refs[:2]), (active_ref, grad_ref, refs[2:4]))
    half = held_ref.shape[0] // 2
    for left, right, (keep_ref, send_ref) in pairs:
        held_ref[...] = t_dot(left[...], right[...])
        keep_ref[...] = held_ref[row_place(section_ref, 0, half), :].astype(BF)
        send_ref[...] = held_ref[row_place(section_ref, 1, half), :].astype(BF)


def feed_halves(section, hidden, grad_up, active, grad, after=()):
    features = hidden.shape[1]
    units = active.shape[1]
    return run_kernel(
        feed_halves_kernel,
        [low((features // 2, units))] * 2 + [low((units // 2, features))] * 2,
        (section,),
        (hidden, grad_up, active, grad),
        after=after,
        scratch=[pltpu.VMEM((features, units), F32)],
        spare=8,
    )


def attend_halves_kernel(
    section_ref, rows_ref, grad_qkv_ref, grad_ref, context_ref, rel_ref, grad_table_ref, keep_ref, send_ref, held_ref
):
    width = context_ref.shape[1]
    held_ref[: 3 * width] = t_dot(grad_qkv_ref[...], rows_ref[...])
    held_ref[:width] += dot(grad_table_ref[width:], rel_ref[...])
    held_ref[width : 2 * width] += dot(grad_table_ref[:width], rel_ref[...])
    held_ref[3 * width :] = t_dot(context_ref[...], grad_ref[...])
    half = held_ref.shape[0] // 2
    keep_ref[...] = held_ref[row_place(section_ref, 0, half), :].astype(BF)
    send_ref[...] = held_ref[row_place(section_ref, 1, half), :].astype(BF)


def attend_halves(section, rows, grad_qkv, grad, context, rel_table, grad_table, after=()):
    features = rows.shape[1]
    width = context.shape[1]
    half = low((2 * width, features))
    return run_kernel(
        attend_halves_kernel,
        [half, half],
        (section,),
        (rows, grad_qkv, grad, context, rel_table, grad_table),
        after=after,
        scratch=[pltpu.VMEM((4 * width, features), F32)],
        spare=8,
    )


def table_grad_kernel(grad_table_ref, weight_ref, out_ref):
    width = grad_table_ref.shape[0] // 2
    out_ref[...] = t_dot(grad_table_ref[:width], weight_ref[width : 2 * width]) + t_dot(
        grad_table_ref[width:], weight_ref[:width]
    )


def table_grad(grad_table, qkv_weight, after=()):
    outs = [wide((grad_table.shape[1], qkv_weight.shape[1]))]
    return run_kernel(table_grad_kernel, outs, (), (grad_table, qkv_weight), after=after)[0]


class Sum:
    def __init__(self, keep, send, after=()):
        self.pairs = [(keep, swap_pipe(gate(send, after) if after else send))]
        self.held = self.final = None


def slot_kernel(pairs, first, second, third, crossing, extra, flags_ref, *refs):
    refs = list(refs)

    def take(count):
        taken = refs[:count]
        del refs[:count]
        return taken

    entering = take(2 * pairs)
    in_first, in_second, in_third = take(first), take(second), take(third)
    (by_neighbour,) = take(1) if first or third else (None,)
    (by_middle,) = take(1) if second else (None,)
    across = take(crossing)
    extras = take(2 * extra)
    at_end = flags_ref[1] == 1
    sums = {}

    def give(name, value):
        (ref,) = take(1)
        ref[...] = value
        sums[name] = value

    if pairs:
        (ref,) = take(1)
        start = 0
        for keep, arrived in zip(entering[::2], entering[1::2]):
            rows = keep.shape[0]
            ref[start : start + rows] = (keep[...].astype(F32) + arrived[...].astype(F32)).astype(BF)
            start += rows
        sums["entered"] = ref[...]
    if first:
        held = in_first[0][...]
        arrived = by_neighbour[: held.shape[0]]
        total = (held.astype(F32) + arrived.astype(F32)).astype(BF)
        give("first", jnp.where(at_end, held, total))
    if second:
        held = in_second[0][...].astype(F32)
        give("second", (held + by_middle[: held.shape[0]].astype(F32)).astype(BF))
    if third:
        held = in_third[0][...]
        give("third", jnp.where(at_end, by_neighbour[: held.shape[0]], held))
    if pairs and second:
        (ref,) = take(1)
        small, large = sums["second"].shape[0], sums["entered"].shape[0]
        ref[:small] = jnp.where(at_end, sums["entered"][:small], sums["second"])
        if large > small:
            ref[small:] = sums["entered"][small:]
    if crossing:
        (ref,) = take(1)
        from_zero = across[0][...]
        from_one = across[1][...] if crossing == 2 else sums["third"]
        ref[...] = jnp.where(flags_ref[0] == 0, from_zero, from_one)
    if extra:
        (ref,) = take(1)
        ref[...] = (extras[0][...].astype(F32) + extras[1][...].astype(F32)).astype(BF)


class Line:
    def __init__(self, flags):
        self.flags = flags
        self.direct = lax.axis_size("dp") == 4
        self.first = self.second = self.third = None
        self.by_neighbour = self.by_middle = None

    def slot(self, entering=None, crossing=(), extra=(), after=()):
        first, second, third = self.first, self.second, self.third
        arrays = [array for pair in (entering.pairs if entering else ()) for array in pair]
        outs = []
        if entering:
            rows = sum(keep.shape[0] for keep, moved in entering.pairs)
            outs.append(low((rows, arrays[0].shape[1])))
        for one in (first, second, third):
            if one:
                arrays.append(one.held)
                outs.append(low(one.held.shape))
        if first or third:
            arrays.append(self.by_neighbour)
        if second:
            arrays.append(self.by_middle)
        across = [one.final for one in crossing if one.final is not None]
        arrays += across
        arrays += extra
        if entering and second:
            outs.append(outs[0])
        if crossing:
            outs.append(low(across[0].shape))
        if extra:
            outs.append(low(extra[0].shape))
        body = functools.partial(
            slot_kernel,
            len(entering.pairs) if entering else 0,
            int(first is not None),
            int(second is not None),
            int(third is not None),
            len(across),
            int(len(extra) > 0),
        )
        results = list(run_kernel(body, outs, (self.flags,), arrays, after=after))
        done = list(results)
        payload = None
        if entering:
            payload = entering.held = results.pop(0)
        if first:
            first.held = results.pop(0)
        if second:
            second.held = results.pop(0)
            payload = second.held if payload is None else payload
        if third:
            third.final = results.pop(0)
        if entering and second:
            payload = results.pop(0)
        if not self.direct:
            if entering:
                entering.final = lax.psum(entering.held, "dp")
        else:
            if payload is not None:
                self.by_neighbour = lax.ppermute(
                    payload, "dp", [(0, 1), (1, 0), (2, 3), (3, 2)]
                )
            if first:
                self.by_middle = lax.ppermute(first.held, "dp", [(1, 2), (2, 1)])
            self.first, self.second, self.third = entering, first, second
        return done, swap_pipe(results.pop(0)) if crossing else None


def table_kernel(rel_ref, weight_ref, out_ref):
    width = weight_ref.shape[0] // 3
    out_ref[:, :width] = dot_t(rel_ref[...], weight_ref[width : 2 * width]).astype(BF)
    out_ref[:, width:] = dot_t(rel_ref[...], weight_ref[:width]).astype(BF)


def table_rows(rel_rows, qkv_weight):
    outs = [low((rel_rows.shape[0], 2 * qkv_weight.shape[0] // 3))]
    return run_kernel(table_kernel, outs, (), (rel_rows, qkv_weight))[0]


def halved(part, axis, distance):
    bit = (lax.axis_index(axis) // distance) % 2
    half = part.shape[0] // 2
    keep = lax.dynamic_slice_in_dim(part, bit * half, half, 0)
    send = lax.dynamic_slice_in_dim(part, (1 - bit) * half, half, 0).astype(BF)
    return keep + to_partner(send, axis, distance).astype(F32)


def rejoined(part, axis, distance):
    bit = (lax.axis_index(axis) // distance) % 2
    other = to_partner(part, axis, distance)
    return jnp.where(
        bit == 0, jnp.concatenate([part, other], 0), jnp.concatenate([other, part], 0)
    )


def join_kernel(section_ref, *refs):
    outs = refs[4:]

    def write(halves):
        rows = outs[0].shape[0]
        start = 0
        for out_ref in outs:
            for half_ref in halves:
                begin, size = start, half_ref.shape[0]
                from_row, to_row = max(begin, 0), min(begin + rows, size)
                if from_row < to_row:
                    out_ref[from_row - begin : to_row - begin] = half_ref[from_row:to_row].astype(F32)
                start -= size
            start += rows + sum(half_ref.shape[0] for half_ref in halves)

    @pl.when(section_ref[0] == 0)
    def first_section():
        write((refs[0], refs[1]))

    @pl.when(section_ref[0] == 1)
    def second_section():
        write((refs[3], refs[2]))


def join(section, halves, count=1, after=()):
    arrays = [array for pair in halves for array in pair]
    rows, columns = 2 * arrays[0].shape[0] // count, arrays[0].shape[1]
    return run_kernel(
        join_kernel, [wide((rows, columns))] * count, (section,), arrays, after=after
    )


def ends_kernel(section_ref, grad_ref, other_grad_ref, result_ref, other_result_ref, out_ref):
    @pl.when(section_ref[0] == 0)
    def first_section():
        out_ref[0] = grad_ref[...]
        out_ref[1] = other_grad_ref[...].astype(F32)

    @pl.when(section_ref[0] == 1)
    def second_section():
        out_ref[0] = other_result_ref[...].astype(F32)
        out_ref[1] = result_ref[...]


def choose_kernel(flags_ref, own_ref, mine_ref, theirs_ref, first_ref, second_ref):
    half = mine_ref.shape[0]
    own = row_place(flags_ref.at[pl.ds(1, 1)], 0, half)
    other = row_place(flags_ref.at[pl.ds(1, 1)], 1, half)

    def write(own_out_ref, other_out_ref):
        own_out_ref[...] = own_ref[...]
        other_out_ref[own, :] = mine_ref[...]
        other_out_ref[other, :] = theirs_ref[...]

    @pl.when(flags_ref[0] == 0)
    def first_section():
        write(first_ref, second_ref)

    @pl.when(flags_ref[0] == 1)
    def second_section():
        write(second_ref, first_ref)


def both_layers(flags, own, mine, theirs, after=()):
    shape = low(own.shape)
    return run_kernel(choose_kernel, [shape, shape], (flags,), (own, mine, theirs), after=after)


def per_device(
    pipe_ends,
    bounds,
    query_weight,
    key_weight,
    value_weight,
    attention_out_weight,
    feedforward_in_weight,
    down_weight,
    norm_gain,
    norm_bias,
    rel_table,
):
    section = lax.axis_index("pipe")
    index = lax.axis_index("tensor").reshape(1)
    section_index = section.reshape(1)
    ends = pipe_ends[0, :, 0]
    size = ends.shape[1]
    total = size * lax.axis_size("tensor")
    buckets, features = rel_table.shape
    width = query_weight.shape[2]
    bound = lax.dynamic_index_in_dim(bounds, section, 0, keepdims=False)[0]
    parity = lax.axis_index("dp") % 2
    flags = jnp.stack([section, parity])

    def own_half(weight):
        half = weight.shape[0] // 2
        return lax.dynamic_slice_in_dim(weight, parity * half, half, 0)

    def of_layer(layer, own, other):
        return jnp.where(section == layer, own, other)

    from_other = swap_pipe(lax.dynamic_index_in_dim(ends, 1 - section, 0, keepdims=False))
    qkv_own = jnp.concatenate([query_weight[0].T, key_weight[0].T, value_weight[0].T], 0)
    out_own, in_own, down_own = attention_out_weight[0], feedforward_in_weight[0], down_weight[0]
    qkv_mine = swap_pipe(own_half(qkv_own))
    first_in = jnp.where(section == 0, ends[0], from_other)
    last_grad = jnp.where(section == 0, from_other, ends[1])
    first_blocks = spread(first_in)
    qkv_theirs = to_partner(qkv_mine, "dp", 1)
    out_other = swap_pipe(gate(out_own, [qkv_mine]))
    own_norms = jnp.concatenate([norm_gain[0], norm_bias[0]], 0)
    other_norms = swap_pipe(gate(own_norms, [qkv_mine]))
    in_mine = swap_pipe(gate(own_half(in_own), [out_other]))
    down_mine = swap_pipe(gate(own_half(down_own), [out_other]))
    norms = [of_layer(layer, own_norms, other_norms) for layer in range(2)]
    qkv_weights = both_layers(flags, qkv_own, qkv_mine, qkv_theirs)
    out_weights = [of_layer(layer, out_own, out_other) for layer in range(2)]
    by_place = jnp.arange(2 * total, dtype=jnp.int32)
    near_rows = jnp.clip(by_place - (total - buckets // 2), 0, buckets - 1)

    def rel_rows(pick):
        one_hot = pick[:, None] == jnp.arange(buckets, dtype=jnp.int32)[None, :]
        return dot(one_hot.astype(BF), rel_table).astype(BF)

    key_first = rel_rows(buckets - 1 - jnp.clip(by_place - (total - buckets // 2), 0, buckets - 1))
    query_first = rel_rows(near_rows)

    def row(layer, number):
        return norms[layer][number : number + 1]

    tables = [
        [table_rows(rel, qkv_weights[layer]) for rel in (key_first, query_first)]
        for layer in range(2)
    ]
    saved = []
    rows = first_in
    in_weights = down_weights = None
    for layer in range(2):
        attended, parts = attend_forward(
            index,
            bound,
            spread(rows) if layer else first_blocks,
            qkv_weights[layer],
            out_weights[layer],
            tables[layer][0],
        )
        early = [tables[layer][1]]
        if layer == 0:
            in_theirs = to_partner(in_mine, "dp", 1)
            early.append(in_theirs)
        hidden_low, normed_one, inverse_one = norm_one(
            exchange(parts), rows, row(layer, 0), row(layer, 2), early
        )
        if layer == 0:
            down_mine = gate(down_mine, [parts[0]])
            down_theirs = to_partner(down_mine, "dp", 1)
            in_weights = both_layers(flags, in_own, in_mine, in_theirs)
            down_weights = both_layers(flags, down_own, down_mine, down_theirs)
        fed, parts = feed_forward(spread(hidden_low), in_weights[layer], down_weights[layer])
        parts = exchange(parts)
        kept = [attended, fed, normed_one, inverse_one]
        if layer == 0:
            rows, normed_two, inverse_two = norm_two(
                parts, normed_one, norms[0], [tables[1][0]]
            )
            kept += [normed_two, inverse_two]
        saved.append(kept)
    result, back_two, back_low, sums_two = turn(parts, normed_one, norms[1], last_grad)
    other_result = lax.ppermute(result.astype(BF), "pipe", [(0, 1)])

    norm_sums = [[None, None], [None, None]]
    norm_sums[1][1] = sums_two

    def back_feed(layer):
        hidden_whole, active, slope = saved[layer][1]
        (grad_ffn, grad_up), parts = feed_backward(
            spread(back_low), in_weights[layer], down_weights[layer], slope, ()
        )
        return exchange(parts), (hidden_whole, grad_up, active, grad_ffn)

    def back_attention(layer, blocks, after=()):
        rows_whole, qkv, context, probs = saved[layer][0]
        (grad_whole, grad_qkv, grad_table), parts = attend_backward(
            index,
            bound,
            blocks,
            out_weights[layer],
            qkv_weights[layer],
            qkv,
            probs,
            tables[layer][1],
            after,
        )
        factors = (rows_whole, grad_qkv, grad_whole, context, rel_table, grad_table)
        return exchange(parts), factors

    place = lax.axis_index("dp")
    line = Line(jnp.stack([section, ((place == 0) | (place == 3)).astype(jnp.int32)]))
    parts, factors = back_feed(1)
    feed = feed_halves(section_index, *factors)
    in_1 = Sum(*feed[:2])
    normed, inverse = saved[1][2:4]
    back_two, back_low, norm_sums[1][0] = norm_back(
        parts, back_two, normed, inverse, row(1, 0), False, feed
    )
    blocks = spread(back_low)
    done, _ = line.slot(in_1, after=blocks[1:2])
    down_send = gate(feed[3], done)
    down_1 = Sum(feed[2], down_send)
    parts, factors = back_attention(1, blocks, [down_send])
    held = attend_halves(section_index, *factors)
    done, _ = line.slot(down_1, after=held)
    attention_1 = Sum(*held, done)
    table_1 = table_grad(factors[-1], qkv_weights[1])
    normed, inverse = saved[0][4:]
    back_two, back_low, norm_sums[0][1] = norm_back(
        parts, back_two, normed, inverse, row(0, 1), True, [*done, table_1]
    )
    parts, factors = back_feed(0)
    done, _ = line.slot(attention_1, after=factors[1:2])
    feed = feed_halves(section_index, *factors, done)
    in_0 = Sum(*feed[:2])
    normed, inverse = saved[0][2:4]
    back_two, back_low, norm_sums[0][0] = norm_back(
        parts, back_two, normed, inverse, row(0, 0), False, feed
    )
    blocks = spread(back_low)
    done, _ = line.slot(in_0, after=blocks[1:2])
    down_send = gate(feed[3], done)
    down_0 = Sum(feed[2], down_send)
    parts, factors = back_attention(0, blocks, [down_send])
    held = attend_halves(section_index, *factors)
    attention_0 = Sum(*held)
    done, _ = line.slot(down_0, after=held)
    norm_rows = jnp.concatenate([rows for pair in norm_sums for rows in pair], 0)
    table_0 = table_grad(factors[-1], qkv_weights[0], done)
    positions = lax.axis_size("tensor")
    padding = -(norm_rows.shape[0] // positions) % 16
    small = jnp.concatenate(
        [
            (table_0 + table_1).reshape(positions, -1, features),
            norm_rows.reshape(positions, -1, features),
            jnp.zeros((positions, padding, features), F32),
        ],
        1,
    )
    half = small.shape[1]
    small = small.reshape(-1, features)
    small = halved(halved(small, "tensor", 1), "tensor", 2).astype(BF)
    done, _ = line.slot(attention_0)
    moved = swap_pipe(small)
    in_1_other = lax.ppermute(in_1.final, "pipe", [(0, 1)])
    grad = back_two
    for part in parts:
        grad = grad + part.astype(F32)
    other_grad = lax.ppermute(grad.astype(BF), "pipe", [(1, 0)])
    done, crossed_one = line.slot(None, (down_1, in_0), (small, moved), [in_1_other])
    small = done[-1]
    if line.direct:
        moved = to_partner(small, "dp", 1)
    else:
        moved = jnp.zeros_like(small)
        small = lax.psum(small, "dp")
    (end_values,) = run_kernel(
        ends_kernel,
        [wide((2, size, features))],
        (section_index,),
        (grad, other_grad, result, other_result),
    )
    done, crossed_two = line.slot(
        None, (attention_1, down_0), (small, moved), [crossed_one]
    )
    small = done[-1]
    moved = to_partner(small, "dp", 2) if line.direct else moved
    (into,) = join(section_index, [(in_0.final, crossed_one), (in_1.final, in_1_other)])
    done, _ = line.slot(None, (), (small, moved), [crossed_two, into, end_values])
    small = done[-1]
    crossed_three = swap_pipe(attention_0.final)
    (downward,) = join(section_index, [(down_0.final, crossed_two), (down_1.final, crossed_one)])
    small = rejoined(rejoined(small, "tensor", 2), "tensor", 1).astype(F32)
    small = small.reshape(positions, half, features)
    of_table = buckets // positions
    table_grads = small[:, :of_table].reshape(buckets, features)
    norm_rows = small[:, of_table : half - padding].reshape(2, 2, 2, features)
    norm_rows = lax.dynamic_index_in_dim(norm_rows, section, 0, keepdims=False)
    attention = join(
        section_index,
        [(attention_0.final, crossed_three), (attention_1.final, crossed_two)],
        4,
        [downward],
    )
    return (
        end_values[None, :, None],
        *(grad.T[None] for grad in attention[:3]),
        attention[3][None],
        into[None],
        downward[None],
        norm_rows[:, 0][None],
        norm_rows[:, 1][None],
        table_grads,
    )


def solution(mesh):
    in_specs = (
        P("pipe", None, "dp", "tensor", None),
        P(None, "dp", None),
        P("pipe", None, "tensor"),
        P("pipe", None, "tensor"),
        P("pipe", None, "tensor"),
        P("pipe", "tensor", None),
        P("pipe", None, "tensor"),
        P("pipe", "tensor", None),
        P("pipe", None, None),
        P("pipe", None, None),
        P(),
    )
    out_specs = (
        P("pipe", None, "dp", "tensor", None),
        P("pipe", None, "tensor"),
        P("pipe", None, "tensor"),
        P("pipe", None, "tensor"),
        P("pipe", "tensor", None),
        P("pipe", None, "tensor"),
        P("pipe", "tensor", None),
        P("pipe", None, None),
        P("pipe", None, None),
        P(),
    )
    return jax.shard_map(
        per_device, mesh=mesh, in_specs=in_specs, out_specs=out_specs, check_vma=False
    )
```

```python
import functools
import math

import jax
import jax.numpy as jnp
from jax import lax
from jax.experimental import pallas as pl
from jax.experimental.pallas import tpu as pltpu
from jax.sharding import PartitionSpec as P

HEAD = 64
BLOCK = 128
EPSILON = 1e-05
MASKED = -1e30
BF = jnp.bfloat16
F32 = jnp.float32
SCALE = (3.0 * HEAD) ** (-0.5)


def dot(left, right):
    return lax.dot_general(left, right, (((1,), (0,)), ((), ())), preferred_element_type=F32)


def dot_t(left, right):
    return lax.dot_general(left, right, (((1,), (1,)), ((), ())), preferred_element_type=F32)


def t_dot(left, right):
    return lax.dot_general(left, right, (((0,), (0,)), ((), ())), preferred_element_type=F32)


def low(shape):
    return jax.ShapeDtypeStruct(shape, BF)


def wide(shape):
    return jax.ShapeDtypeStruct(shape, F32)


def run_kernel(body, outs, scalars, arrays, after=(), scratch=(), spare=4, far=0):
    after = tuple(after)
    held = sum(math.prod(one.shape) * one.dtype.itemsize for one in (*outs, *arrays, *scratch))
    vmem = pl.BlockSpec(memory_space=pltpu.VMEM)
    lead = len(scalars) + len(arrays)
    near = len(outs) - far

    def whole_body(*refs):
        results = refs[lead + len(after) : lead + len(after) + len(outs)]
        rest = refs[lead + len(after) + len(outs) :]
        if not far:
            body(*refs[:lead], *results, *rest)
            return
        held_results, semaphores = rest[-1 - far : -1], rest[-1]
        body(*refs[:lead], *results[:near], *held_results, *rest[: -1 - far])
        copies = [
            pltpu.make_async_copy(source, target, semaphores.at[number])
            for number, (source, target) in enumerate(zip(held_results, results[near:]))
        ]
        for copy in copies:
            copy.start()
        for copy in copies:
            copy.wait()

    scratch = list(scratch)
    if far:
        scratch += [pltpu.VMEM(one.shape, one.dtype) for one in outs[near:]]
        scratch.append(pltpu.SemaphoreType.DMA((far,)))
    return pl.pallas_call(
        whole_body,
        out_shape=tuple(
            one if number < near else pltpu.HBM(one.shape, one.dtype)
            for number, one in enumerate(outs)
        ),
        in_specs=[pl.BlockSpec(memory_space=pltpu.SMEM)] * len(scalars)
        + [vmem] * len(arrays)
        + [pl.BlockSpec(memory_space=pl.ANY)] * len(after),
        out_specs=tuple(
            vmem if number < near else pl.BlockSpec(memory_space=pltpu.HBM)
            for number in range(len(outs))
        ),
        scratch_shapes=scratch,
        compiler_params=pltpu.CompilerParams(vmem_limit_bytes=held + spare * 2**20),
    )(*scalars, *arrays, *after)


def in_hbm(array):
    return pltpu.with_memory_space_constraint(array, pltpu.HBM)


def gate(array, after):
    def nothing(*refs):
        del refs

    anywhere = pl.BlockSpec(memory_space=pl.ANY)
    return pl.pallas_call(
        nothing,
        out_shape=jax.ShapeDtypeStruct(array.shape, array.dtype),
        in_specs=[anywhere] * (1 + len(after)),
        out_specs=anywhere,
        input_output_aliases={0: 0},
    )(array, *after)


def to_partner(block, axis, distance):
    count = lax.axis_size(axis)
    return lax.ppermute(block, axis, [(i, i ^ distance) for i in range(count)])


def swap_pipe(block):
    return to_partner(block, "pipe", 1)


def spread(block):
    count = lax.axis_size("tensor")
    distances = [2**step for step in range(1, count.bit_length() - 1)]
    blocks = {0: block}
    for distance in distances:
        blocks.update({d + distance: to_partner(blocks[d], "tensor", distance) for d in list(blocks)})
    blocks.update({d + 1: to_partner(blocks[d], "tensor", 1) for d in list(blocks)})
    return [blocks[d] for d in range(count)]


def exchange(parts):
    return [parts[0]] + [to_partner(parts[d], "tensor", d) for d in range(1, len(parts))]


def row_place(index_ref, distance, size):
    return pl.ds(pl.multiple_of((index_ref[0] ^ distance) * size, size), size)


def store_parts(index_ref, whole_ref, part_refs):
    size = part_refs[0].shape[0]
    for distance, part_ref in enumerate(part_refs):
        part_ref[...] = whole_ref[row_place(index_ref, distance, size), :].astype(part_ref.dtype)


def part_shapes(count, size, features):
    return [wide((size, features))] + [low((size, features))] * (count - 1)


def added(refs):
    total = refs[0][...].astype(F32)
    for ref in refs[1:]:
        total = total + ref[...].astype(F32)
    return total


def normalize(summed):
    row_mean = jnp.mean(summed, axis=-1, keepdims=True)
    centred = summed - row_mean
    spread_of = jnp.mean(centred * centred, axis=-1, keepdims=True)
    inverse = lax.rsqrt(spread_of + EPSILON)
    return centred * inverse, inverse


def normalize_back(grad_result, normed, inverse, gain_row):
    sums = jnp.concatenate(
        [
            jnp.sum(grad_result * normed, axis=0, keepdims=True),
            jnp.sum(grad_result, axis=0, keepdims=True),
        ],
        0,
    )
    scaled = grad_result * gain_row
    centre_one = jnp.mean(scaled, axis=-1, keepdims=True)
    centre_two = jnp.mean(scaled * normed, axis=-1, keepdims=True)
    return inverse * (scaled - centre_one - normed * centre_two), sums


def by_segment(rows, split_at):
    first = lax.broadcasted_iota(jnp.int32, rows.shape, 0) < split_at
    zero = jnp.zeros_like(rows)
    return jnp.concatenate([jnp.where(first, rows, zero), jnp.where(first, zero, rows)], axis=1)


def placed_blocks(rows, first_table, second_table, first_lanes):
    total = rows.shape[0]
    span = total + BLOCK
    blocks = []
    for start in range(0, total, BLOCK):
        begin = total - BLOCK - start
        part = rows[start : start + BLOCK]
        first = dot_t(part, first_table[begin : begin + span])
        second = dot_t(part, second_table[begin : begin + span])
        both = jnp.where(first_lanes, first, second)
        blocks.append(pltpu.roll(both, total + 1, 1, stride=1, stride_axis=0)[:, :total])
    return blocks


def attend_kernel(count, index_ref, bound_ref, *refs):
    blocks = refs[:count]
    qkv_weight_ref, out_weight_ref, table_ref = refs[count : count + 3]
    rows_ref, qkv_ref, context_ref, probs_ref = refs[count + 3 : count + 7]
    part_refs = refs[count + 7 : 2 * count + 7]
    held_ref = refs[2 * count + 7]
    size = blocks[0].shape[0]
    for distance, block in enumerate(blocks):
        rows_ref[row_place(index_ref, distance, size), :] = block[...]
    split_at = bound_ref[0]
    total = rows_ref.shape[0]
    width = out_weight_ref.shape[0]
    qkv = dot_t(rows_ref[...], qkv_weight_ref[...]).astype(BF)
    qkv_ref[...] = qkv
    table = table_ref[...]
    table_wide = table.astype(F32)
    later = pltpu.roll(table_wide, 2 * total - split_at, 0).astype(BF)
    earlier = pltpu.roll(table_wide, split_at, 0).astype(BF)
    skewed = lax.broadcasted_iota(jnp.int32, (BLOCK, total + BLOCK), 0)
    skewed = skewed + lax.broadcasted_iota(jnp.int32, (BLOCK, total + BLOCK), 1)
    first_columns = skewed < split_at + BLOCK - 1
    live = lax.broadcasted_iota(jnp.int32, (total, total), 1) < bound_ref[1]
    contexts = []
    for head in range(width // HEAD):
        at = head * HEAD
        query = qkv[:, at : at + HEAD]
        key = qkv[:, width + at : width + at + HEAD]
        value = qkv[:, 2 * width + at : 2 * width + at + HEAD]

        def tables(offset):
            cut = slice(offset + at, offset + at + HEAD)
            return (
                jnp.concatenate([table[:, cut], later[:, cut]], 1),
                jnp.concatenate([earlier[:, cut], table[:, cut]], 1),
            )

        near = jnp.concatenate(
            placed_blocks(by_segment(query, split_at), *tables(0), first_columns), 0
        )
        far = placed_blocks(by_segment(key, split_at), *tables(width), first_columns)
        far = jnp.concatenate([block.T for block in far], 1)
        scores = jnp.where(live, (dot_t(query, key) + near + far) * SCALE, MASKED)
        raised = jnp.exp(scores - jnp.max(scores, axis=1, keepdims=True))
        probs = raised / jnp.sum(raised, axis=1, keepdims=True)
        probs_ref[head] = probs
        contexts.append(dot(probs.astype(BF), value).astype(BF))
    context = jnp.concatenate(contexts, 1)
    context_ref[...] = context
    held_ref[...] = dot(context, out_weight_ref[...])
    store_parts(index_ref, held_ref, part_refs)


def attend_forward(index, bound, blocks, qkv_weight, out_weight, table):
    count = len(blocks)
    size, features = blocks[0].shape
    total = count * size
    width = out_weight.shape[0]
    outs = run_kernel(
        functools.partial(attend_kernel, count),
        [
            low((total, features)),
            low((total, 3 * width)),
            low((total, width)),
            wide((width // HEAD, total, total)),
        ]
        + part_shapes(count, size, features),
        (index, bound),
        (*blocks, qkv_weight, out_weight, table),
        scratch=[pltpu.VMEM((total, features), F32)],
        spare=16,
    )
    return outs[:4], outs[4:]


def attend_back_kernel(count, index_ref, bound_ref, *refs):
    blocks = refs[:count]
    out_weight_ref, qkv_weight_ref, qkv_ref, probs_ref, table_ref = refs[count : count + 5]
    rows_ref, grad_qkv_ref, grad_table_ref = refs[count + 5 : count + 8]
    part_refs = refs[count + 8 : 2 * count + 8]
    held_ref, sum_ref = refs[2 * count + 8 :]
    size = blocks[0].shape[0]
    for distance, block in enumerate(blocks):
        rows_ref[row_place(index_ref, distance, size), :] = block[...]
    split_at = bound_ref[0]
    total = rows_ref.shape[0]
    width = out_weight_ref.shape[0]
    heads = width // HEAD
    span = total + BLOCK
    grad_context = dot_t(rows_ref[...], out_weight_ref[...]).astype(BF)
    grad_context_t = grad_context.astype(F32).T.astype(BF)
    qkv = qkv_ref[...]
    rows_t = qkv[:, : 2 * width].astype(F32).T.astype(BF)
    table = table_ref[...]
    moved = pltpu.roll(table.astype(F32), split_at, 0).astype(BF)
    row_ids = lax.broadcasted_iota(jnp.int32, (total, total), 0)
    places = jnp.where(row_ids < split_at, row_ids, row_ids - split_at)
    turned = lax.broadcasted_iota(jnp.int32, (total, total), 1) == total - 1 - places
    merge = jnp.where(turned, 1.0, 0.0).astype(BF)
    first_lanes = lax.broadcasted_iota(jnp.int32, (HEAD, total), 1) < split_at
    first_rows = lax.broadcasted_iota(jnp.int32, (total, HEAD), 0) < split_at
    pad = jnp.zeros((BLOCK, BLOCK), F32)
    held_ref[...] = jnp.zeros(held_ref.shape, F32)

    def along_table(merged, offset, head):
        cut = slice(offset + head * HEAD, offset + (head + 1) * HEAD)
        pair = jnp.concatenate([table[:, cut], moved[:, cut]], 1)
        turned_rows = rows_t[cut]
        zero = jnp.zeros_like(turned_rows)
        turned_rows = jnp.concatenate(
            [jnp.where(first_lanes, turned_rows, zero), jnp.where(first_lanes, zero, turned_rows)],
            0,
        )
        parts = []
        slot = offset // HEAD + head
        for start in range(0, total, BLOCK):
            block = jnp.concatenate([merged[start : start + BLOCK], pad], 1)
            block = pltpu.roll(block, 1, 1, stride=1, stride_axis=0).astype(BF)
            parts.append(dot(block, pair[start : start + span]))
            held_ref[slot, :, start : start + span] += dot(
                turned_rows[:, start : start + BLOCK], block
            )
        both = jnp.concatenate(parts, 0)
        return jnp.where(first_rows, both[:, :HEAD], both[:, HEAD:])

    grad_queries = []
    grad_keys = []
    grad_values_t = []
    for head in range(heads):
        at = head * HEAD
        cut = slice(at, at + HEAD)
        query = qkv[:, at : at + HEAD]
        key = qkv[:, width + at : width + at + HEAD]
        value = qkv[:, 2 * width + at : 2 * width + at + HEAD]
        grad_probs = dot_t(grad_context[:, cut], value)
        probs = probs_ref[head]
        centre = jnp.sum(probs * grad_probs, axis=1, keepdims=True)
        score_grad = (probs * (grad_probs - centre) * SCALE).astype(BF)
        score_grad_t = score_grad.astype(F32).T.astype(BF)
        grad_values_t.append(dot(grad_context_t[cut], probs.astype(BF)))
        grad_queries.append(dot(score_grad, key) + along_table(dot(score_grad, merge), 0, head))
        grad_keys.append(
            dot(score_grad_t, query) + along_table(dot(score_grad_t, merge), width, head)
        )
    grad_values = jnp.concatenate(grad_values_t, 0).T
    grad_qkv = jnp.concatenate(grad_queries + grad_keys + [grad_values], 1).astype(BF)
    grad_qkv_ref[...] = grad_qkv
    sum_ref[...] = dot(grad_qkv, qkv_weight_ref[...])
    store_parts(index_ref, sum_ref, part_refs)
    lanes = lax.broadcasted_iota(jnp.int32, (HEAD, span), 1)
    for slot in range(2 * heads):
        first = held_ref[slot, :HEAD]
        second = pltpu.roll(held_ref[slot, HEAD:], 2 * total - split_at, 1)
        both = first + second
        bottom = jnp.sum(both[:, :BLOCK], axis=1, keepdims=True)
        top = jnp.sum(both[:, 2 * total - BLOCK :], axis=1, keepdims=True)
        middle = both[:, BLOCK : 2 * total - BLOCK]
        middle = middle + jnp.where(lanes == 0, bottom, 0.0)
        middle = middle + jnp.where(lanes == span - 1, top, 0.0)
        grad_table_ref[slot * HEAD : (slot + 1) * HEAD] = middle.astype(BF)


def attend_backward(index, bound, blocks, out_weight, qkv_weight, qkv, probs, table, after):
    count = len(blocks)
    size, features = blocks[0].shape
    total = count * size
    width = out_weight.shape[0]
    outs = run_kernel(
        functools.partial(attend_back_kernel, count),
        [low((total, features)), low((total, 3 * width)), low((2 * width, total + BLOCK))]
        + part_shapes(count, size, features),
        (index, bound),
        (*blocks, out_weight, qkv_weight, *map(in_hbm, (qkv, probs, table))),
        after=after,
        scratch=[
            pltpu.VMEM((2 * width // HEAD, 2 * HEAD, 2 * total), F32),
            pltpu.VMEM((total, features), F32),
        ],
        spare=16,
    )
    return outs[:3], outs[3:]


def feed_kernel(count, *refs):
    blocks = refs[:count]
    in_ref, down_ref = refs[count : count + 2]
    rows_ref, active_ref, slope_ref = refs[count + 2 : count + 5]
    part_refs = refs[count + 5 : 2 * count + 5]
    size = blocks[0].shape[0]
    for distance, block in enumerate(blocks):
        cut = slice(distance * size, (distance + 1) * size)
        rows = block[...]
        rows_ref[cut] = rows
        upward = dot(rows, in_ref[...])
        below = 0.5 * (1.0 + lax.erf(upward * (1.0 / math.sqrt(2.0))))
        density = jnp.exp(-0.5 * upward * upward) * (1.0 / math.sqrt(2.0 * math.pi))
        active = (upward * below).astype(BF)
        active_ref[cut] = active
        slope_ref[cut] = below + upward * density
        part_refs[distance][...] = dot(active, down_ref[...]).astype(part_refs[distance].dtype)


def feed_forward(blocks, in_weight, down_weight):
    count = len(blocks)
    size, features = blocks[0].shape
    units = in_weight.shape[1]
    total = count * size
    outs = run_kernel(
        functools.partial(feed_kernel, count),
        [low((total, features)), low((total, units)), wide((total, units))]
        + part_shapes(count, size, features),
        (),
        (*blocks, in_weight, down_weight),
    )
    return outs[:3], outs[3:]


def feed_back_kernel(count, *refs):
    blocks = refs[:count]
    in_ref, down_ref, slope_ref = refs[count : count + 3]
    rows_ref, grad_up_ref = refs[count + 3 : count + 5]
    part_refs = refs[count + 5 : 2 * count + 5]
    size = blocks[0].shape[0]
    for distance, block in enumerate(blocks):
        cut = slice(distance * size, (distance + 1) * size)
        rows = block[...]
        rows_ref[cut] = rows
        grad_up = (dot_t(rows, down_ref[...]) * slope_ref[cut]).astype(BF)
        grad_up_ref[cut] = grad_up
        part_refs[distance][...] = dot_t(grad_up, in_ref[...]).astype(part_refs[distance].dtype)


def feed_backward(blocks, in_weight, down_weight, slope, after):
    count = len(blocks)
    size, features = blocks[0].shape
    units = in_weight.shape[1]
    total = count * size
    outs = run_kernel(
        functools.partial(feed_back_kernel, count),
        [low((total, features)), low((total, units))] + part_shapes(count, size, features),
        (),
        (*blocks, in_weight, down_weight, slope),
        after=after,
    )
    return outs[:2], outs[2:]


def norm_one_kernel(count, *refs):
    rows_ref, gain_ref, bias_ref, low_ref, normed_ref, inverse_ref = refs[count:]
    normed, inverse = normalize(rows_ref[...].astype(F32) + added(refs[:count]))
    low_ref[...] = (normed * gain_ref[...] + bias_ref[...]).astype(BF)
    normed_ref[...] = normed
    inverse_ref[...] = inverse


def norm_one(parts, rows, gain_row, bias_row, after=()):
    shape = rows.shape
    return run_kernel(
        functools.partial(norm_one_kernel, len(parts)),
        [low(shape), wide(shape), wide((shape[0], 1))],
        (),
        (*parts, rows, gain_row, bias_row),
        after=after,
    )


def norm_two_kernel(count, *refs):
    before_ref, gains_ref, low_ref, normed_ref, inverse_ref = refs[count:]
    hidden = before_ref[...] * gains_ref[0:1] + gains_ref[2:3]
    normed, inverse = normalize(hidden + added(refs[:count]))
    low_ref[...] = (normed * gains_ref[1:2] + gains_ref[3:4]).astype(BF)
    normed_ref[...] = normed
    inverse_ref[...] = inverse


def norm_two(parts, before, gains, after=()):
    shape = before.shape
    return run_kernel(
        functools.partial(norm_two_kernel, len(parts)),
        [low(shape), wide(shape), wide((shape[0], 1))],
        (),
        (*parts, before, gains),
        after=after,
    )


def turn_kernel(count, *refs):
    before_ref, gains_ref, grad_ref, result_ref, back_ref, low_ref, sums_ref = refs[count:]
    hidden = before_ref[...] * gains_ref[0:1] + gains_ref[2:3]
    normed, inverse = normalize(hidden + added(refs[:count]))
    result_ref[...] = normed * gains_ref[1:2] + gains_ref[3:4]
    back, sums_ref[...] = normalize_back(
        grad_ref[...].astype(F32), normed, inverse, gains_ref[1:2]
    )
    back_ref[...] = back
    low_ref[...] = back.astype(BF)


def turn(parts, before, gains, grad):
    shape = before.shape
    return run_kernel(
        functools.partial(turn_kernel, len(parts)),
        [wide(shape), wide(shape), low(shape), wide((2, shape[1]))],
        (),
        (*parts, before, gains, grad),
    )


def norm_back_kernel(count, rounded, *refs):
    add_ref, normed_ref, inverse_ref, gain_ref, back_ref, low_ref, sums_ref = refs[count:]
    grad = add_ref[...] + added(refs[:count])
    if rounded:
        grad = grad.astype(BF).astype(F32)
    back, sums_ref[...] = normalize_back(
        grad, normed_ref[...], inverse_ref[...], gain_ref[...]
    )
    back_ref[...] = back
    low_ref[...] = back.astype(BF)


def norm_back(parts, add, normed, inverse, gain_row, rounded, after):
    shape = add.shape
    return run_kernel(
        functools.partial(norm_back_kernel, len(parts), rounded),
        [wide(shape), low(shape), wide((2, shape[1]))],
        (),
        (*parts, add, normed, inverse, gain_row),
        after=after,
    )


def feed_halves_kernel(section_ref, hidden_ref, grad_up_ref, active_ref, grad_ref, *refs):
    held_ref = refs[-1]
    pairs = ((hidden_ref, grad_up_ref, refs[:2]), (active_ref, grad_ref, refs[2:4]))
    half = held_ref.shape[0] // 2
    for left, right, (keep_ref, send_ref) in pairs:
        held_ref[...] = t_dot(left[...], right[...])
        keep_ref[...] = held_ref[row_place(section_ref, 0, half), :].astype(BF)
        send_ref[...] = held_ref[row_place(section_ref, 1, half), :].astype(BF)


def feed_halves(section, hidden, grad_up, active, grad, after=()):
    features = hidden.shape[1]
    units = active.shape[1]
    return run_kernel(
        feed_halves_kernel,
        [low((features // 2, units))] * 2 + [low((units // 2, features))] * 2,
        (section,),
        (hidden, grad_up, active, grad),
        after=after,
        scratch=[pltpu.VMEM((features, units), F32)],
        spare=8,
    )


def attend_halves_kernel(
    section_ref, rows_ref, grad_qkv_ref, grad_ref, context_ref, rel_ref, grad_table_ref, keep_ref, send_ref, held_ref
):
    width = context_ref.shape[1]
    held_ref[: 3 * width] = t_dot(grad_qkv_ref[...], rows_ref[...])
    held_ref[:width] += dot(grad_table_ref[width:], rel_ref[...])
    held_ref[width : 2 * width] += dot(grad_table_ref[:width], rel_ref[...])
    held_ref[3 * width :] = t_dot(context_ref[...], grad_ref[...])
    half = held_ref.shape[0] // 2
    keep_ref[...] = held_ref[row_place(section_ref, 0, half), :].astype(BF)
    send_ref[...] = held_ref[row_place(section_ref, 1, half), :].astype(BF)


def attend_halves(section, rows, grad_qkv, grad, context, rel_table, grad_table, after=()):
    features = rows.shape[1]
    width = context.shape[1]
    half = low((2 * width, features))
    return run_kernel(
        attend_halves_kernel,
        [half, half],
        (section,),
        (rows, grad_qkv, grad, context, rel_table, grad_table),
        after=after,
        scratch=[pltpu.VMEM((4 * width, features), F32)],
        spare=8,
    )


def table_grad_kernel(grad_table_ref, weight_ref, out_ref):
    width = grad_table_ref.shape[0] // 2
    out_ref[...] = t_dot(grad_table_ref[:width], weight_ref[width : 2 * width]) + t_dot(
        grad_table_ref[width:], weight_ref[:width]
    )


def table_grad(grad_table, qkv_weight, after=()):
    outs = [wide((grad_table.shape[1], qkv_weight.shape[1]))]
    return run_kernel(table_grad_kernel, outs, (), (grad_table, qkv_weight), after=after)[0]


class Sum:
    def __init__(self, keep, send, after=()):
        self.pairs = [(keep, swap_pipe(gate(send, after) if after else send))]
        self.held = self.final = None


def slot_kernel(pairs, first, second, third, crossing, extra, flags_ref, *refs):
    refs = list(refs)

    def take(count):
        taken = refs[:count]
        del refs[:count]
        return taken

    entering = take(2 * pairs)
    in_first, in_second, in_third = take(first), take(second), take(third)
    (by_neighbour,) = take(1) if first or third else (None,)
    (by_middle,) = take(1) if second else (None,)
    across = take(crossing)
    extras = take(2 * extra)
    at_end = flags_ref[1] == 1
    sums = {}

    def give(name, value):
        (ref,) = take(1)
        ref[...] = value
        sums[name] = value

    if pairs:
        (ref,) = take(1)
        start = 0
        for keep, arrived in zip(entering[::2], entering[1::2]):
            rows = keep.shape[0]
            ref[start : start + rows] = (keep[...].astype(F32) + arrived[...].astype(F32)).astype(BF)
            start += rows
        sums["entered"] = ref[...]
    if first:
        held = in_first[0][...]
        total = (held.astype(F32) + by_neighbour[...].astype(F32)).astype(BF)
        give("first", jnp.where(at_end, held, total))
    if second:
        held = in_second[0][...].astype(F32)
        sums["second"] = (held + by_middle[...].astype(F32)).astype(BF)
        if not pairs:
            give("second", sums["second"])
    if third:
        held = in_third[0][...]
        give("third", jnp.where(at_end, by_neighbour[...], held))
    if pairs and second:
        (ref,) = take(1)
        ref[...] = jnp.where(at_end, sums["entered"], sums["second"])
    if crossing:
        (ref,) = take(1)
        from_zero = across[0][...]
        from_one = across[1][...] if crossing == 2 else sums["third"]
        ref[...] = jnp.where(flags_ref[0] == 0, from_zero, from_one)
    if extra:
        (ref,) = take(1)
        ref[...] = (extras[0][...].astype(F32) + extras[1][...].astype(F32)).astype(BF)


class Line:
    def __init__(self, flags):
        self.flags = flags
        self.direct = lax.axis_size("dp") == 4
        self.first = self.second = self.third = None
        self.by_neighbour = self.by_middle = None

    def slot(self, entering=None, crossing=(), extra=(), after=()):
        first, second, third = self.first, self.second, self.third
        arrays = [array for pair in (entering.pairs if entering else ()) for array in pair]
        outs = []
        if entering:
            rows = sum(keep.shape[0] for keep, moved in entering.pairs)
            outs.append(low((rows, arrays[0].shape[1])))
        for one in (first, second, third):
            if one:
                arrays.append(one.held)
                if one is not second or not entering:
                    outs.append(low(one.held.shape))
        if first or third:
            arrays.append(self.by_neighbour)
        if second:
            arrays.append(self.by_middle)
        across = [one.final for one in crossing if one.final is not None]
        arrays += across
        arrays += extra
        if entering and second:
            outs.append(outs[0])
        if crossing:
            outs.append(low(across[0].shape))
        if extra:
            outs.append(low(extra[0].shape))
        body = functools.partial(
            slot_kernel,
            len(entering.pairs) if entering else 0,
            int(first is not None),
            int(second is not None),
            int(third is not None),
            len(across),
            int(len(extra) > 0),
        )
        results = list(run_kernel(body, outs, (self.flags,), arrays, after=after))
        done = list(results)
        payload = None
        if entering:
            payload = entering.held = results.pop(0)
        if first:
            first.held = results.pop(0)
        if second and not entering:
            payload = second.held = results.pop(0)
        if third:
            third.final = results.pop(0)
        if entering and second:
            payload = second.held = results.pop(0)
        if not self.direct:
            if entering:
                entering.final = lax.psum(entering.held, "dp")
        else:
            if payload is not None:
                self.by_neighbour = lax.ppermute(
                    payload, "dp", [(0, 1), (1, 0), (2, 3), (3, 2)]
                )
            if first:
                self.by_middle = lax.ppermute(first.held, "dp", [(1, 2), (2, 1)])
            self.first, self.second, self.third = entering, first, second
        return done, swap_pipe(results.pop(0)) if crossing else None


def table_kernel(rel_ref, weight_ref, out_ref):
    width = weight_ref.shape[0] // 3
    out_ref[:, :width] = dot_t(rel_ref[...], weight_ref[width : 2 * width]).astype(BF)
    out_ref[:, width:] = dot_t(rel_ref[...], weight_ref[:width]).astype(BF)


def table_rows(rel_rows, qkv_weight):
    outs = [low((rel_rows.shape[0], 2 * qkv_weight.shape[0] // 3))]
    return run_kernel(table_kernel, outs, (), (rel_rows, qkv_weight))[0]


def halved(part, axis, distance):
    bit = (lax.axis_index(axis) // distance) % 2
    half = part.shape[0] // 2
    keep = lax.dynamic_slice_in_dim(part, bit * half, half, 0)
    send = lax.dynamic_slice_in_dim(part, (1 - bit) * half, half, 0).astype(BF)
    return keep + to_partner(send, axis, distance).astype(F32)


def rejoined(part, axis, distance):
    bit = (lax.axis_index(axis) // distance) % 2
    other = to_partner(part, axis, distance)
    return jnp.where(
        bit == 0, jnp.concatenate([part, other], 0), jnp.concatenate([other, part], 0)
    )


def join_kernel(section_ref, *refs):
    outs = refs[4:]

    def write(halves):
        rows = outs[0].shape[0]
        start = 0
        for out_ref in outs:
            for half_ref in halves:
                begin, size = start, half_ref.shape[0]
                from_row, to_row = max(begin, 0), min(begin + rows, size)
                if from_row < to_row:
                    out_ref[from_row - begin : to_row - begin] = half_ref[from_row:to_row].astype(F32)
                start -= size
            start += rows + sum(half_ref.shape[0] for half_ref in halves)

    @pl.when(section_ref[0] == 0)
    def first_section():
        write((refs[0], refs[1]))

    @pl.when(section_ref[0] == 1)
    def second_section():
        write((refs[3], refs[2]))


def join(section, halves, count=1, after=()):
    arrays = [array for pair in halves for array in pair]
    rows, columns = 2 * arrays[0].shape[0] // count, arrays[0].shape[1]
    return run_kernel(
        join_kernel, [wide((rows, columns))] * count, (section,), arrays, after=after
    )


def ends_kernel(section_ref, grad_ref, other_grad_ref, result_ref, other_result_ref, out_ref):
    @pl.when(section_ref[0] == 0)
    def first_section():
        out_ref[0] = grad_ref[...]
        out_ref[1] = other_grad_ref[...].astype(F32)

    @pl.when(section_ref[0] == 1)
    def second_section():
        out_ref[0] = other_result_ref[...].astype(F32)
        out_ref[1] = result_ref[...]


def choose_kernel(flags_ref, own_ref, mine_ref, theirs_ref, first_ref, second_ref):
    half = mine_ref.shape[0]
    own = row_place(flags_ref.at[pl.ds(1, 1)], 0, half)
    other = row_place(flags_ref.at[pl.ds(1, 1)], 1, half)

    def write(own_out_ref, other_out_ref):
        own_out_ref[...] = own_ref[...]
        other_out_ref[own, :] = mine_ref[...]
        other_out_ref[other, :] = theirs_ref[...]

    @pl.when(flags_ref[0] == 0)
    def first_section():
        write(first_ref, second_ref)

    @pl.when(flags_ref[0] == 1)
    def second_section():
        write(second_ref, first_ref)


def both_layers(flags, own, mine, theirs, after=()):
    shape = low(own.shape)
    return run_kernel(choose_kernel, [shape, shape], (flags,), (own, mine, theirs), after=after)


def per_device(
    pipe_ends,
    bounds,
    query_weight,
    key_weight,
    value_weight,
    attention_out_weight,
    feedforward_in_weight,
    down_weight,
    norm_gain,
    norm_bias,
    rel_table,
):
    section = lax.axis_index("pipe")
    index = lax.axis_index("tensor").reshape(1)
    section_index = section.reshape(1)
    ends = pipe_ends[0, :, 0]
    size = ends.shape[1]
    total = size * lax.axis_size("tensor")
    buckets, features = rel_table.shape
    width = query_weight.shape[2]
    bound = lax.dynamic_index_in_dim(bounds, section, 0, keepdims=False)[0]
    parity = lax.axis_index("dp") % 2
    flags = jnp.stack([section, parity])

    def own_half(weight):
        half = weight.shape[0] // 2
        return lax.dynamic_slice_in_dim(weight, parity * half, half, 0)

    def of_layer(layer, own, other):
        return jnp.where(section == layer, own, other)

    from_other = swap_pipe(lax.dynamic_index_in_dim(ends, 1 - section, 0, keepdims=False))
    qkv_own = jnp.concatenate([query_weight[0].T, key_weight[0].T, value_weight[0].T], 0)
    out_own, in_own, down_own = attention_out_weight[0], feedforward_in_weight[0], down_weight[0]
    qkv_mine = swap_pipe(own_half(qkv_own))
    first_in = jnp.where(section == 0, ends[0], from_other)
    last_grad = jnp.where(section == 0, from_other, ends[1])
    first_blocks = spread(first_in)
    qkv_theirs = to_partner(qkv_mine, "dp", 1)
    out_other = swap_pipe(gate(out_own, [qkv_mine]))
    own_norms = jnp.concatenate([norm_gain[0], norm_bias[0]], 0)
    other_norms = swap_pipe(gate(own_norms, [qkv_mine]))
    in_mine = swap_pipe(gate(own_half(in_own), [out_other]))
    down_mine = swap_pipe(gate(own_half(down_own), [out_other]))
    norms = [of_layer(layer, own_norms, other_norms) for layer in range(2)]
    qkv_weights = both_layers(flags, qkv_own, qkv_mine, qkv_theirs)
    out_weights = [of_layer(layer, out_own, out_other) for layer in range(2)]
    by_place = jnp.arange(2 * total, dtype=jnp.int32)
    near_rows = jnp.clip(by_place - (total - buckets // 2), 0, buckets - 1)

    def rel_rows(pick):
        one_hot = pick[:, None] == jnp.arange(buckets, dtype=jnp.int32)[None, :]
        return dot(one_hot.astype(BF), rel_table).astype(BF)

    key_first = rel_rows(buckets - 1 - jnp.clip(by_place - (total - buckets // 2), 0, buckets - 1))
    query_first = rel_rows(near_rows)

    def row(layer, number):
        return norms[layer][number : number + 1]

    tables = [
        [table_rows(rel, qkv_weights[layer]) for rel in (key_first, query_first)]
        for layer in range(2)
    ]
    saved = []
    rows = first_in
    in_weights = down_weights = None
    for layer in range(2):
        attended, parts = attend_forward(
            index,
            bound,
            spread(rows) if layer else first_blocks,
            qkv_weights[layer],
            out_weights[layer],
            tables[layer][0],
        )
        early = [tables[layer][1]]
        if layer == 0:
            in_mine = gate(in_mine, [parts[0]])
            in_theirs = to_partner(in_mine, "dp", 1)
        hidden_low, normed_one, inverse_one = norm_one(
            exchange(parts), rows, row(layer, 0), row(layer, 2), early
        )
        if layer == 0:
            down_mine = gate(down_mine, [parts[0]])
            down_theirs = to_partner(down_mine, "dp", 1)
            in_weights = both_layers(flags, in_own, in_mine, in_theirs)
            down_weights = both_layers(flags, down_own, down_mine, down_theirs)
        fed, parts = feed_forward(spread(hidden_low), in_weights[layer], down_weights[layer])
        parts = exchange(parts)
        kept = [attended, fed, normed_one, inverse_one]
        if layer == 0:
            rows, normed_two, inverse_two = norm_two(
                parts, normed_one, norms[0], [tables[1][0]]
            )
            kept += [normed_two, inverse_two]
        saved.append(kept)
    result, back_two, back_low, sums_two = turn(parts, normed_one, norms[1], last_grad)
    other_result = lax.ppermute(result.astype(BF), "pipe", [(0, 1)])

    norm_sums = [[None, None], [None, None]]
    norm_sums[1][1] = sums_two

    def back_feed(layer):
        hidden_whole, active, slope = saved[layer][1]
        (grad_ffn, grad_up), parts = feed_backward(
            spread(back_low), in_weights[layer], down_weights[layer], slope, ()
        )
        return exchange(parts), (hidden_whole, grad_up, active, grad_ffn)

    def back_attention(layer, blocks, after=()):
        rows_whole, qkv, context, probs = saved[layer][0]
        (grad_whole, grad_qkv, grad_table), parts = attend_backward(
            index,
            bound,
            blocks,
            out_weights[layer],
            qkv_weights[layer],
            qkv,
            probs,
            tables[layer][1],
            after,
        )
        factors = (rows_whole, grad_qkv, grad_whole, context, rel_table, grad_table)
        return exchange(parts), factors

    place = lax.axis_index("dp")
    line = Line(jnp.stack([section, ((place == 0) | (place == 3)).astype(jnp.int32)]))
    parts, factors = back_feed(1)
    feed = feed_halves(section_index, *factors)
    in_1 = Sum(*feed[:2])
    normed, inverse = saved[1][2:4]
    back_two, back_low, norm_sums[1][0] = norm_back(
        parts, back_two, normed, inverse, row(1, 0), False, feed
    )
    blocks = spread(back_low)
    done, _ = line.slot(in_1, after=blocks[1:2])
    down_send = gate(feed[3], done)
    down_1 = Sum(feed[2], down_send)
    parts, factors = back_attention(1, blocks, [down_send])
    held = attend_halves(section_index, *factors)
    done, _ = line.slot(down_1, after=held)
    attention_1 = Sum(*held, done)
    table_1 = table_grad(factors[-1], qkv_weights[1])
    normed, inverse = saved[0][4:]
    back_two, back_low, norm_sums[0][1] = norm_back(
        parts, back_two, normed, inverse, row(0, 1), True, [*done, table_1]
    )
    parts, factors = back_feed(0)
    done, _ = line.slot(attention_1, after=factors[1:2])
    feed = feed_halves(section_index, *factors, done)
    in_0 = Sum(*feed[:2])
    normed, inverse = saved[0][2:4]
    back_two, back_low, norm_sums[0][0] = norm_back(
        parts, back_two, normed, inverse, row(0, 0), False, feed
    )
    blocks = spread(back_low)
    done, _ = line.slot(in_0, after=blocks[1:2])
    down_send = gate(feed[3], done)
    down_0 = Sum(feed[2], down_send)
    parts, factors = back_attention(0, blocks, [down_send])
    held = attend_halves(section_index, *factors)
    attention_0 = Sum(*held)
    done, _ = line.slot(down_0, after=held)
    norm_rows = jnp.concatenate([rows for pair in norm_sums for rows in pair], 0)
    table_0 = table_grad(factors[-1], qkv_weights[0], done)
    positions = lax.axis_size("tensor")
    padding = -(norm_rows.shape[0] // positions) % 16
    small = jnp.concatenate(
        [
            (table_0 + table_1).reshape(positions, -1, features),
            norm_rows.reshape(positions, -1, features),
            jnp.zeros((positions, padding, features), F32),
        ],
        1,
    )
    half = small.shape[1]
    small = small.reshape(-1, features)
    small = halved(halved(small, "tensor", 1), "tensor", 2).astype(BF)
    done, _ = line.slot(attention_0)
    moved = swap_pipe(small)
    in_1_other = lax.ppermute(in_1.final, "pipe", [(0, 1)])
    grad = back_two
    for part in parts:
        grad = grad + part.astype(F32)
    other_grad = lax.ppermute(grad.astype(BF), "pipe", [(1, 0)])
    done, crossed_one = line.slot(None, (down_1, in_0), (small, moved), [in_1_other])
    small = done[-1]
    if line.direct:
        moved = to_partner(small, "dp", 1)
    else:
        moved = jnp.zeros_like(small)
        small = lax.psum(small, "dp")
    (end_values,) = run_kernel(
        ends_kernel,
        [wide((2, size, features))],
        (section_index,),
        (grad, other_grad, result, other_result),
    )
    done, crossed_two = line.slot(
        None, (attention_1, down_0), (small, moved), [crossed_one]
    )
    small = done[-1]
    moved = to_partner(small, "dp", 2) if line.direct else moved
    (into,) = join(section_index, [(in_0.final, crossed_one), (in_1.final, in_1_other)])
    done, _ = line.slot(None, (), (small, moved), [crossed_two, into, end_values])
    small = done[-1]
    crossed_three = swap_pipe(attention_0.final)
    (downward,) = join(section_index, [(down_0.final, crossed_two), (down_1.final, crossed_one)])
    small = rejoined(rejoined(small, "tensor", 2), "tensor", 1).astype(F32)
    small = small.reshape(positions, half, features)
    of_table = buckets // positions
    table_grads = small[:, :of_table].reshape(buckets, features)
    norm_rows = small[:, of_table : half - padding].reshape(2, 2, 2, features)
    norm_rows = lax.dynamic_index_in_dim(norm_rows, section, 0, keepdims=False)
    attention = join(
        section_index,
        [(attention_0.final, crossed_three), (attention_1.final, crossed_two)],
        4,
        [downward],
    )
    return (
        end_values[None, :, None],
        *(grad.T[None] for grad in attention[:3]),
        attention[3][None],
        into[None],
        downward[None],
        norm_rows[:, 0][None],
        norm_rows[:, 1][None],
        table_grads,
    )


def solution(mesh):
    in_specs = (
        P("pipe", None, "dp", "tensor", None),
        P(None, "dp", None),
        P("pipe", None, "tensor"),
        P("pipe", None, "tensor"),
        P("pipe", None, "tensor"),
        P("pipe", "tensor", None),
        P("pipe", None, "tensor"),
        P("pipe", "tensor", None),
        P("pipe", None, None),
        P("pipe", None, None),
        P(),
    )
    out_specs = (
        P("pipe", None, "dp", "tensor", None),
        P("pipe", None, "tensor"),
        P("pipe", None, "tensor"),
        P("pipe", None, "tensor"),
        P("pipe", "tensor", None),
        P("pipe", None, "tensor"),
        P("pipe", "tensor", None),
        P("pipe", None, None),
        P("pipe", None, None),
        P(),
    )
    return jax.shard_map(
        per_device, mesh=mesh, in_specs=in_specs, out_specs=out_specs, check_vma=False
    )
```

```python
import functools
import math

import jax
import jax.numpy as jnp
from jax import lax
from jax.experimental import pallas as pl
from jax.experimental.pallas import tpu as pltpu
from jax.sharding import PartitionSpec as P

HEAD = 64
BLOCK = 128
EPSILON = 1e-05
MASKED = -1e30
BF = jnp.bfloat16
F32 = jnp.float32
SCALE = (3.0 * HEAD) ** (-0.5)


def dot(left, right):
    return lax.dot_general(left, right, (((1,), (0,)), ((), ())), preferred_element_type=F32)


def dot_t(left, right):
    return lax.dot_general(left, right, (((1,), (1,)), ((), ())), preferred_element_type=F32)


def t_dot(left, right):
    return lax.dot_general(left, right, (((0,), (0,)), ((), ())), preferred_element_type=F32)


def low(shape):
    return jax.ShapeDtypeStruct(shape, BF)


def wide(shape):
    return jax.ShapeDtypeStruct(shape, F32)


def run_kernel(body, outs, scalars, arrays, after=(), scratch=(), spare=4, far=0):
    after = tuple(after)
    held = sum(math.prod(one.shape) * one.dtype.itemsize for one in (*outs, *arrays, *scratch))
    vmem = pl.BlockSpec(memory_space=pltpu.VMEM)
    lead = len(scalars) + len(arrays)
    near = len(outs) - far

    def whole_body(*refs):
        results = refs[lead + len(after) : lead + len(after) + len(outs)]
        rest = refs[lead + len(after) + len(outs) :]
        if not far:
            body(*refs[:lead], *results, *rest)
            return
        held_results, semaphores = rest[-1 - far : -1], rest[-1]
        body(*refs[:lead], *results[:near], *held_results, *rest[: -1 - far])
        copies = [
            pltpu.make_async_copy(source, target, semaphores.at[number])
            for number, (source, target) in enumerate(zip(held_results, results[near:]))
        ]
        for copy in copies:
            copy.start()
        for copy in copies:
            copy.wait()

    scratch = list(scratch)
    if far:
        scratch += [pltpu.VMEM(one.shape, one.dtype) for one in outs[near:]]
        scratch.append(pltpu.SemaphoreType.DMA((far,)))
    return pl.pallas_call(
        whole_body,
        out_shape=tuple(
            one if number < near else pltpu.HBM(one.shape, one.dtype)
            for number, one in enumerate(outs)
        ),
        in_specs=[pl.BlockSpec(memory_space=pltpu.SMEM)] * len(scalars)
        + [vmem] * len(arrays)
        + [pl.BlockSpec(memory_space=pl.ANY)] * len(after),
        out_specs=tuple(
            vmem if number < near else pl.BlockSpec(memory_space=pltpu.HBM)
            for number in range(len(outs))
        ),
        scratch_shapes=scratch,
        compiler_params=pltpu.CompilerParams(vmem_limit_bytes=held + spare * 2**20),
    )(*scalars, *arrays, *after)


def in_hbm(array):
    return pltpu.with_memory_space_constraint(array, pltpu.HBM)


def gate(array, after):
    def nothing(*refs):
        del refs

    anywhere = pl.BlockSpec(memory_space=pl.ANY)
    return pl.pallas_call(
        nothing,
        out_shape=jax.ShapeDtypeStruct(array.shape, array.dtype),
        in_specs=[anywhere] * (1 + len(after)),
        out_specs=anywhere,
        input_output_aliases={0: 0},
    )(array, *after)


def to_partner(block, axis, distance):
    count = lax.axis_size(axis)
    return lax.ppermute(block, axis, [(i, i ^ distance) for i in range(count)])


def swap_pipe(block):
    return to_partner(block, "pipe", 1)


def spread(block):
    count = lax.axis_size("tensor")
    distances = [2**step for step in range(1, count.bit_length() - 1)]
    blocks = {0: block}
    for distance in distances:
        blocks.update({d + distance: to_partner(blocks[d], "tensor", distance) for d in list(blocks)})
    blocks.update({d + 1: to_partner(blocks[d], "tensor", 1) for d in list(blocks)})
    return [blocks[d] for d in range(count)]


def exchange(parts):
    return [parts[0]] + [to_partner(parts[d], "tensor", d) for d in range(1, len(parts))]


def row_place(index_ref, distance, size):
    return pl.ds(pl.multiple_of((index_ref[0] ^ distance) * size, size), size)


def store_parts(index_ref, whole_ref, part_refs):
    size = part_refs[0].shape[0]
    for distance, part_ref in enumerate(part_refs):
        part_ref[...] = whole_ref[row_place(index_ref, distance, size), :].astype(part_ref.dtype)


def part_shapes(count, size, features):
    return [wide((size, features))] + [low((size, features))] * (count - 1)


def added(refs):
    total = refs[0][...].astype(F32)
    for ref in refs[1:]:
        total = total + ref[...].astype(F32)
    return total


def normalize(summed):
    row_mean = jnp.mean(summed, axis=-1, keepdims=True)
    centred = summed - row_mean
    spread_of = jnp.mean(centred * centred, axis=-1, keepdims=True)
    inverse = lax.rsqrt(spread_of + EPSILON)
    return centred * inverse, inverse


def normalize_back(grad_result, normed, inverse, gain_row):
    sums = jnp.concatenate(
        [
            jnp.sum(grad_result * normed, axis=0, keepdims=True),
            jnp.sum(grad_result, axis=0, keepdims=True),
        ],
        0,
    )
    scaled = grad_result * gain_row
    centre_one = jnp.mean(scaled, axis=-1, keepdims=True)
    centre_two = jnp.mean(scaled * normed, axis=-1, keepdims=True)
    return inverse * (scaled - centre_one - normed * centre_two), sums


def by_segment(rows, split_at):
    first = lax.broadcasted_iota(jnp.int32, rows.shape, 0) < split_at
    zero = jnp.zeros_like(rows)
    return jnp.concatenate([jnp.where(first, rows, zero), jnp.where(first, zero, rows)], axis=1)


def placed_blocks(rows, first_table, second_table, first_lanes):
    total = rows.shape[0]
    span = total + BLOCK
    blocks = []
    for start in range(0, total, BLOCK):
        begin = total - BLOCK - start
        part = rows[start : start + BLOCK]
        first = dot_t(part, first_table[begin : begin + span])
        second = dot_t(part, second_table[begin : begin + span])
        both = jnp.where(first_lanes, first, second)
        blocks.append(pltpu.roll(both, total + 1, 1, stride=1, stride_axis=0)[:, :total])
    return blocks


def attend_kernel(count, index_ref, bound_ref, *refs):
    blocks = refs[:count]
    qkv_weight_ref, out_weight_ref, table_ref = refs[count : count + 3]
    rows_ref, qkv_ref, context_ref, probs_ref = refs[count + 3 : count + 7]
    part_refs = refs[count + 7 : 2 * count + 7]
    held_ref = refs[2 * count + 7]
    size = blocks[0].shape[0]
    for distance, block in enumerate(blocks):
        rows_ref[row_place(index_ref, distance, size), :] = block[...]
    split_at = bound_ref[0]
    total = rows_ref.shape[0]
    width = out_weight_ref.shape[0]
    qkv = dot_t(rows_ref[...], qkv_weight_ref[...]).astype(BF)
    qkv_ref[...] = qkv
    table = table_ref[...]
    table_wide = table.astype(F32)
    later = pltpu.roll(table_wide, 2 * total - split_at, 0).astype(BF)
    earlier = pltpu.roll(table_wide, split_at, 0).astype(BF)
    skewed = lax.broadcasted_iota(jnp.int32, (BLOCK, total + BLOCK), 0)
    skewed = skewed + lax.broadcasted_iota(jnp.int32, (BLOCK, total + BLOCK), 1)
    first_columns = skewed < split_at + BLOCK - 1
    live = lax.broadcasted_iota(jnp.int32, (total, total), 1) < bound_ref[1]
    contexts = []
    for head in range(width // HEAD):
        at = head * HEAD
        query = qkv[:, at : at + HEAD]
        key = qkv[:, width + at : width + at + HEAD]
        value = qkv[:, 2 * width + at : 2 * width + at + HEAD]

        def tables(offset):
            cut = slice(offset + at, offset + at + HEAD)
            return (
                jnp.concatenate([table[:, cut], later[:, cut]], 1),
                jnp.concatenate([earlier[:, cut], table[:, cut]], 1),
            )

        near = jnp.concatenate(
            placed_blocks(by_segment(query, split_at), *tables(0), first_columns), 0
        )
        far = placed_blocks(by_segment(key, split_at), *tables(width), first_columns)
        far = jnp.concatenate([block.T for block in far], 1)
        scores = jnp.where(live, (dot_t(query, key) + near + far) * SCALE, MASKED)
        raised = jnp.exp(scores - jnp.max(scores, axis=1, keepdims=True))
        probs = raised / jnp.sum(raised, axis=1, keepdims=True)
        probs_ref[head] = probs
        contexts.append(dot(probs.astype(BF), value).astype(BF))
    context = jnp.concatenate(contexts, 1)
    context_ref[...] = context
    held_ref[...] = dot(context, out_weight_ref[...])
    store_parts(index_ref, held_ref, part_refs)


def attend_forward(index, bound, blocks, qkv_weight, out_weight, table):
    count = len(blocks)
    size, features = blocks[0].shape
    total = count * size
    width = out_weight.shape[0]
    outs = run_kernel(
        functools.partial(attend_kernel, count),
        [
            low((total, features)),
            low((total, 3 * width)),
            low((total, width)),
            wide((width // HEAD, total, total)),
        ]
        + part_shapes(count, size, features),
        (index, bound),
        (*blocks, qkv_weight, out_weight, table),
        scratch=[pltpu.VMEM((total, features), F32)],
        spare=16,
    )
    return outs[:4], outs[4:]


def attend_back_kernel(count, index_ref, bound_ref, *refs):
    blocks = refs[:count]
    out_weight_ref, qkv_weight_ref, qkv_ref, probs_ref, table_ref = refs[count : count + 5]
    rows_ref, grad_qkv_ref, grad_table_ref = refs[count + 5 : count + 8]
    part_refs = refs[count + 8 : 2 * count + 8]
    held_ref, sum_ref = refs[2 * count + 8 :]
    size = blocks[0].shape[0]
    for distance, block in enumerate(blocks):
        rows_ref[row_place(index_ref, distance, size), :] = block[...]
    split_at = bound_ref[0]
    total = rows_ref.shape[0]
    width = out_weight_ref.shape[0]
    heads = width // HEAD
    span = total + BLOCK
    grad_context = dot_t(rows_ref[...], out_weight_ref[...]).astype(BF)
    grad_context_t = grad_context.astype(F32).T.astype(BF)
    qkv = qkv_ref[...]
    rows_t = qkv[:, : 2 * width].astype(F32).T.astype(BF)
    table = table_ref[...]
    moved = pltpu.roll(table.astype(F32), split_at, 0).astype(BF)
    row_ids = lax.broadcasted_iota(jnp.int32, (total, total), 0)
    places = jnp.where(row_ids < split_at, row_ids, row_ids - split_at)
    turned = lax.broadcasted_iota(jnp.int32, (total, total), 1) == total - 1 - places
    merge = jnp.where(turned, 1.0, 0.0).astype(BF)
    first_lanes = lax.broadcasted_iota(jnp.int32, (HEAD, total), 1) < split_at
    first_rows = lax.broadcasted_iota(jnp.int32, (total, HEAD), 0) < split_at
    pad = jnp.zeros((BLOCK, BLOCK), F32)
    held_ref[...] = jnp.zeros(held_ref.shape, F32)

    def along_table(merged, offset, head):
        cut = slice(offset + head * HEAD, offset + (head + 1) * HEAD)
        pair = jnp.concatenate([table[:, cut], moved[:, cut]], 1)
        turned_rows = rows_t[cut]
        zero = jnp.zeros_like(turned_rows)
        turned_rows = jnp.concatenate(
            [jnp.where(first_lanes, turned_rows, zero), jnp.where(first_lanes, zero, turned_rows)],
            0,
        )
        parts = []
        slot = offset // HEAD + head
        for start in range(0, total, BLOCK):
            block = jnp.concatenate([merged[start : start + BLOCK], pad], 1)
            block = pltpu.roll(block, 1, 1, stride=1, stride_axis=0).astype(BF)
            parts.append(dot(block, pair[start : start + span]))
            held_ref[slot, :, start : start + span] += dot(
                turned_rows[:, start : start + BLOCK], block
            )
        both = jnp.concatenate(parts, 0)
        return jnp.where(first_rows, both[:, :HEAD], both[:, HEAD:])

    grad_queries = []
    grad_keys = []
    grad_values_t = []
    for head in range(heads):
        at = head * HEAD
        cut = slice(at, at + HEAD)
        query = qkv[:, at : at + HEAD]
        key = qkv[:, width + at : width + at + HEAD]
        value = qkv[:, 2 * width + at : 2 * width + at + HEAD]
        grad_probs = dot_t(grad_context[:, cut], value)
        probs = probs_ref[head]
        centre = jnp.sum(probs * grad_probs, axis=1, keepdims=True)
        score_grad = (probs * (grad_probs - centre) * SCALE).astype(BF)
        score_grad_t = score_grad.astype(F32).T.astype(BF)
        grad_values_t.append(dot(grad_context_t[cut], probs.astype(BF)))
        grad_queries.append(dot(score_grad, key) + along_table(dot(score_grad, merge), 0, head))
        grad_keys.append(
            dot(score_grad_t, query) + along_table(dot(score_grad_t, merge), width, head)
        )
    grad_values = jnp.concatenate(grad_values_t, 0).T
    grad_qkv = jnp.concatenate(grad_queries + grad_keys + [grad_values], 1).astype(BF)
    grad_qkv_ref[...] = grad_qkv
    sum_ref[...] = dot(grad_qkv, qkv_weight_ref[...])
    store_parts(index_ref, sum_ref, part_refs)
    lanes = lax.broadcasted_iota(jnp.int32, (HEAD, span), 1)
    for slot in range(2 * heads):
        first = held_ref[slot, :HEAD]
        second = pltpu.roll(held_ref[slot, HEAD:], 2 * total - split_at, 1)
        both = first + second
        bottom = jnp.sum(both[:, :BLOCK], axis=1, keepdims=True)
        top = jnp.sum(both[:, 2 * total - BLOCK :], axis=1, keepdims=True)
        middle = both[:, BLOCK : 2 * total - BLOCK]
        middle = middle + jnp.where(lanes == 0, bottom, 0.0)
        middle = middle + jnp.where(lanes == span - 1, top, 0.0)
        grad_table_ref[slot * HEAD : (slot + 1) * HEAD] = middle.astype(BF)


def attend_backward(index, bound, blocks, out_weight, qkv_weight, qkv, probs, table, after):
    count = len(blocks)
    size, features = blocks[0].shape
    total = count * size
    width = out_weight.shape[0]
    outs = run_kernel(
        functools.partial(attend_back_kernel, count),
        [low((total, features)), low((total, 3 * width)), low((2 * width, total + BLOCK))]
        + part_shapes(count, size, features),
        (index, bound),
        (*blocks, out_weight, qkv_weight, *map(in_hbm, (qkv, probs, table))),
        after=after,
        scratch=[
            pltpu.VMEM((2 * width // HEAD, 2 * HEAD, 2 * total), F32),
            pltpu.VMEM((total, features), F32),
        ],
        spare=16,
    )
    return outs[:3], outs[3:]


def feed_kernel(count, *refs):
    blocks = refs[:count]
    in_ref, down_ref = refs[count : count + 2]
    rows_ref, active_ref, slope_ref = refs[count + 2 : count + 5]
    part_refs = refs[count + 5 : 2 * count + 5]
    size = blocks[0].shape[0]
    for distance, block in enumerate(blocks):
        cut = slice(distance * size, (distance + 1) * size)
        rows = block[...]
        rows_ref[cut] = rows
        upward = dot(rows, in_ref[...])
        below = 0.5 * (1.0 + lax.erf(upward * (1.0 / math.sqrt(2.0))))
        density = jnp.exp(-0.5 * upward * upward) * (1.0 / math.sqrt(2.0 * math.pi))
        active = (upward * below).astype(BF)
        active_ref[cut] = active
        slope_ref[cut] = below + upward * density
        part_refs[distance][...] = dot(active, down_ref[...]).astype(part_refs[distance].dtype)


def feed_forward(blocks, in_weight, down_weight):
    count = len(blocks)
    size, features = blocks[0].shape
    units = in_weight.shape[1]
    total = count * size
    outs = run_kernel(
        functools.partial(feed_kernel, count),
        [low((total, features)), low((total, units)), wide((total, units))]
        + part_shapes(count, size, features),
        (),
        (*blocks, in_weight, down_weight),
    )
    return outs[:3], outs[3:]


def feed_back_kernel(count, *refs):
    blocks = refs[:count]
    in_ref, down_ref, slope_ref = refs[count : count + 3]
    rows_ref, grad_up_ref = refs[count + 3 : count + 5]
    part_refs = refs[count + 5 : 2 * count + 5]
    size = blocks[0].shape[0]
    for distance, block in enumerate(blocks):
        cut = slice(distance * size, (distance + 1) * size)
        rows = block[...]
        rows_ref[cut] = rows
        grad_up = (dot_t(rows, down_ref[...]) * slope_ref[cut]).astype(BF)
        grad_up_ref[cut] = grad_up
        part_refs[distance][...] = dot_t(grad_up, in_ref[...]).astype(part_refs[distance].dtype)


def feed_backward(blocks, in_weight, down_weight, slope, after):
    count = len(blocks)
    size, features = blocks[0].shape
    units = in_weight.shape[1]
    total = count * size
    outs = run_kernel(
        functools.partial(feed_back_kernel, count),
        [low((total, features)), low((total, units))] + part_shapes(count, size, features),
        (),
        (*blocks, in_weight, down_weight, slope),
        after=after,
    )
    return outs[:2], outs[2:]


def norm_one_kernel(count, *refs):
    rows_ref, gain_ref, bias_ref, low_ref, normed_ref, inverse_ref = refs[count:]
    normed, inverse = normalize(rows_ref[...].astype(F32) + added(refs[:count]))
    low_ref[...] = (normed * gain_ref[...] + bias_ref[...]).astype(BF)
    normed_ref[...] = normed
    inverse_ref[...] = inverse


def norm_one(parts, rows, gain_row, bias_row, after=()):
    shape = rows.shape
    return run_kernel(
        functools.partial(norm_one_kernel, len(parts)),
        [low(shape), wide(shape), wide((shape[0], 1))],
        (),
        (*parts, rows, gain_row, bias_row),
        after=after,
    )


def norm_two_kernel(count, *refs):
    before_ref, gains_ref, low_ref, normed_ref, inverse_ref = refs[count:]
    hidden = before_ref[...] * gains_ref[0:1] + gains_ref[2:3]
    normed, inverse = normalize(hidden + added(refs[:count]))
    low_ref[...] = (normed * gains_ref[1:2] + gains_ref[3:4]).astype(BF)
    normed_ref[...] = normed
    inverse_ref[...] = inverse


def norm_two(parts, before, gains, after=()):
    shape = before.shape
    return run_kernel(
        functools.partial(norm_two_kernel, len(parts)),
        [low(shape), wide(shape), wide((shape[0], 1))],
        (),
        (*parts, before, gains),
        after=after,
    )


def turn_kernel(count, *refs):
    before_ref, gains_ref, grad_ref, result_ref, back_ref, low_ref, sums_ref = refs[count:]
    hidden = before_ref[...] * gains_ref[0:1] + gains_ref[2:3]
    normed, inverse = normalize(hidden + added(refs[:count]))
    result_ref[...] = normed * gains_ref[1:2] + gains_ref[3:4]
    back, sums_ref[...] = normalize_back(
        grad_ref[...].astype(F32), normed, inverse, gains_ref[1:2]
    )
    back_ref[...] = back
    low_ref[...] = back.astype(BF)


def turn(parts, before, gains, grad):
    shape = before.shape
    return run_kernel(
        functools.partial(turn_kernel, len(parts)),
        [wide(shape), wide(shape), low(shape), wide((2, shape[1]))],
        (),
        (*parts, before, gains, grad),
    )


def norm_back_kernel(count, rounded, *refs):
    add_ref, normed_ref, inverse_ref, gain_ref, back_ref, low_ref, sums_ref = refs[count:]
    grad = add_ref[...] + added(refs[:count])
    if rounded:
        grad = grad.astype(BF).astype(F32)
    back, sums_ref[...] = normalize_back(
        grad, normed_ref[...], inverse_ref[...], gain_ref[...]
    )
    back_ref[...] = back
    low_ref[...] = back.astype(BF)


def norm_back(parts, add, normed, inverse, gain_row, rounded, after):
    shape = add.shape
    return run_kernel(
        functools.partial(norm_back_kernel, len(parts), rounded),
        [wide(shape), low(shape), wide((2, shape[1]))],
        (),
        (*parts, *map(in_hbm, (add, normed, inverse)), gain_row),
        after=after,
    )


def feed_halves_kernel(section_ref, hidden_ref, grad_up_ref, active_ref, grad_ref, *refs):
    pairs = ((hidden_ref, grad_up_ref, refs[:2]), (active_ref, grad_ref, refs[2:]))
    for left_ref, right_ref, halves in pairs:
        for distance, half_ref in enumerate(halves):
            columns = row_place(section_ref, distance, half_ref.shape[0])
            half_ref[...] = t_dot(left_ref[:, columns], right_ref[...]).astype(BF)


def feed_halves(section, hidden, grad_up, active, grad, after=()):
    features = hidden.shape[1]
    units = active.shape[1]
    return run_kernel(
        feed_halves_kernel,
        [low((features // 2, units))] * 2 + [low((units // 2, features))] * 2,
        (section,),
        (hidden, grad_up, active, grad),
        after=after,
        spare=8,
    )


def attend_halves_kernel(
    section_ref, rows_ref, grad_qkv_ref, grad_ref, context_ref, rel_ref, grad_table_ref, keep_ref, send_ref
):
    width = context_ref.shape[1]
    from_rows = t_dot(grad_qkv_ref[...], rows_ref[...])
    queries = from_rows[:width] + dot(grad_table_ref[width:], rel_ref[...])
    keys = from_rows[width : 2 * width] + dot(grad_table_ref[:width], rel_ref[...])
    first = jnp.concatenate([queries, keys], 0).astype(BF)
    outward = t_dot(context_ref[...], grad_ref[...])
    second = jnp.concatenate([from_rows[2 * width :], outward], 0).astype(BF)
    keep_ref[...] = jnp.where(section_ref[0] == 0, first, second)
    send_ref[...] = jnp.where(section_ref[0] == 0, second, first)


def attend_halves(section, rows, grad_qkv, grad, context, rel_table, grad_table, after=()):
    features = rows.shape[1]
    width = context.shape[1]
    half = low((2 * width, features))
    return run_kernel(
        attend_halves_kernel,
        [half, half],
        (section,),
        (rows, grad_qkv, grad, context, rel_table, grad_table),
        after=after,
        spare=8,
    )


def table_grad_kernel(grad_table_ref, weight_ref, out_ref):
    width = grad_table_ref.shape[0] // 2
    out_ref[...] = t_dot(grad_table_ref[:width], weight_ref[width : 2 * width]) + t_dot(
        grad_table_ref[width:], weight_ref[:width]
    )


def table_grad(grad_table, qkv_weight, after=()):
    outs = [wide((grad_table.shape[1], qkv_weight.shape[1]))]
    return run_kernel(table_grad_kernel, outs, (), (grad_table, qkv_weight), after=after)[0]


class Sum:
    def __init__(self, keep, send, after=()):
        self.pairs = [(keep, swap_pipe(gate(send, after) if after else send))]
        self.held = self.final = None


def slot_kernel(pairs, first, second, third, crossing, extra, flags_ref, *refs):
    refs = list(refs)

    def take(count):
        taken = refs[:count]
        del refs[:count]
        return taken

    entering = take(2 * pairs)
    in_first, in_second, in_third = take(first), take(second), take(third)
    (by_neighbour,) = take(1) if first or third else (None,)
    (by_middle,) = take(1) if second else (None,)
    across = take(crossing)
    extras = take(2 * extra)
    at_end = flags_ref[1] == 1
    sums = {}

    def give(name, value):
        (ref,) = take(1)
        ref[...] = value
        sums[name] = value

    if pairs:
        (ref,) = take(1)
        start = 0
        for keep, arrived in zip(entering[::2], entering[1::2]):
            rows = keep.shape[0]
            ref[start : start + rows] = (keep[...].astype(F32) + arrived[...].astype(F32)).astype(BF)
            start += rows
        sums["entered"] = ref[...]
    if first:
        held = in_first[0][...]
        total = (held.astype(F32) + by_neighbour[...].astype(F32)).astype(BF)
        give("first", jnp.where(at_end, held, total))
    if second:
        held = in_second[0][...].astype(F32)
        sums["second"] = (held + by_middle[...].astype(F32)).astype(BF)
        if not pairs:
            give("second", sums["second"])
    if third:
        held = in_third[0][...]
        give("third", jnp.where(at_end, by_neighbour[...], held))
    if pairs and second:
        (ref,) = take(1)
        ref[...] = jnp.where(at_end, sums["entered"], sums["second"])
    if crossing:
        (ref,) = take(1)
        from_zero = across[0][...]
        from_one = across[1][...] if crossing == 2 else sums["third"]
        ref[...] = jnp.where(flags_ref[0] == 0, from_zero, from_one)
    if extra:
        (ref,) = take(1)
        ref[...] = (extras[0][...].astype(F32) + extras[1][...].astype(F32)).astype(BF)


class Line:
    def __init__(self, flags):
        self.flags = flags
        self.direct = lax.axis_size("dp") == 4
        self.first = self.second = self.third = None
        self.by_neighbour = self.by_middle = None

    def slot(self, entering=None, crossing=(), extra=(), after=()):
        first, second, third = self.first, self.second, self.third
        arrays = [array for pair in (entering.pairs if entering else ()) for array in pair]
        outs = []
        if entering:
            rows = sum(keep.shape[0] for keep, moved in entering.pairs)
            outs.append(low((rows, arrays[0].shape[1])))
        for one in (first, second, third):
            if one:
                arrays.append(one.held)
                if one is not second or not entering:
                    outs.append(low(one.held.shape))
        if first or third:
            arrays.append(self.by_neighbour)
        if second:
            arrays.append(self.by_middle)
        across = [one.final for one in crossing if one.final is not None]
        arrays += across
        arrays += extra
        if entering and second:
            outs.append(outs[0])
        if crossing:
            outs.append(low(across[0].shape))
        if extra:
            outs.append(low(extra[0].shape))
        body = functools.partial(
            slot_kernel,
            len(entering.pairs) if entering else 0,
            int(first is not None),
            int(second is not None),
            int(third is not None),
            len(across),
            int(len(extra) > 0),
        )
        results = list(run_kernel(body, outs, (self.flags,), arrays, after=after))
        done = list(results)
        payload = None
        if entering:
            payload = entering.held = results.pop(0)
        if first:
            first.held = results.pop(0)
        if second and not entering:
            payload = second.held = results.pop(0)
        if third:
            third.final = results.pop(0)
        if entering and second:
            payload = second.held = results.pop(0)
        if not self.direct:
            if entering:
                entering.final = lax.psum(entering.held, "dp")
        else:
            if payload is not None:
                self.by_neighbour = lax.ppermute(
                    payload, "dp", [(0, 1), (1, 0), (2, 3), (3, 2)]
                )
            if first:
                self.by_middle = lax.ppermute(first.held, "dp", [(1, 2), (2, 1)])
            self.first, self.second, self.third = entering, first, second
        return done, swap_pipe(results.pop(0)) if crossing else None


def table_kernel(rel_ref, weight_ref, out_ref):
    width = weight_ref.shape[0] // 3
    out_ref[:, :width] = dot_t(rel_ref[...], weight_ref[width : 2 * width]).astype(BF)
    out_ref[:, width:] = dot_t(rel_ref[...], weight_ref[:width]).astype(BF)


def table_rows(rel_rows, qkv_weight):
    outs = [low((rel_rows.shape[0], 2 * qkv_weight.shape[0] // 3))]
    return run_kernel(table_kernel, outs, (), (in_hbm(rel_rows), qkv_weight))[0]


def halved(part, axis, distance):
    bit = (lax.axis_index(axis) // distance) % 2
    half = part.shape[0] // 2
    keep = lax.dynamic_slice_in_dim(part, bit * half, half, 0)
    send = lax.dynamic_slice_in_dim(part, (1 - bit) * half, half, 0).astype(BF)
    return keep + to_partner(send, axis, distance).astype(F32)


def rejoined(part, axis, distance):
    bit = (lax.axis_index(axis) // distance) % 2
    other = to_partner(part, axis, distance)
    return jnp.where(
        bit == 0, jnp.concatenate([part, other], 0), jnp.concatenate([other, part], 0)
    )


def join_kernel(section_ref, *refs):
    outs = refs[4:]

    def write(halves):
        rows = outs[0].shape[0]
        start = 0
        for out_ref in outs:
            for half_ref in halves:
                begin, size = start, half_ref.shape[0]
                from_row, to_row = max(begin, 0), min(begin + rows, size)
                if from_row < to_row:
                    out_ref[from_row - begin : to_row - begin] = half_ref[from_row:to_row].astype(F32)
                start -= size
            start += rows + sum(half_ref.shape[0] for half_ref in halves)

    @pl.when(section_ref[0] == 0)
    def first_section():
        write((refs[0], refs[1]))

    @pl.when(section_ref[0] == 1)
    def second_section():
        write((refs[3], refs[2]))


def join(section, halves, count=1, after=()):
    arrays = [array for pair in halves for array in pair]
    rows, columns = 2 * arrays[0].shape[0] // count, arrays[0].shape[1]
    return run_kernel(
        join_kernel, [wide((rows, columns))] * count, (section,), arrays, after=after
    )


def finish_kernel(size, of_table, flags_ref, own_ref, other_ref, table_ref, norms_ref):
    first = jnp.where(flags_ref[0] == 0, own_ref[...], other_ref[...]).astype(F32)
    second = jnp.where(flags_ref[0] == 0, other_ref[...], own_ref[...]).astype(F32)
    positions = 2 * own_ref.shape[0] // size
    share = 8 // positions
    norms = []
    for position in range(positions):
        part = first if position < positions // 2 else second
        start = position % (positions // 2) * size
        table_ref[position * of_table : (position + 1) * of_table] = part[start : start + of_table]
        norms.append(part[start + of_table : start + of_table + share])
    norms = jnp.concatenate(norms, 0)
    norms_ref[...] = jnp.where(flags_ref[1] == 0, norms[:4], norms[4:])


def ends_kernel(section_ref, grad_ref, other_grad_ref, result_ref, other_result_ref, out_ref):
    @pl.when(section_ref[0] == 0)
    def first_section():
        out_ref[0] = grad_ref[...]
        out_ref[1] = other_grad_ref[...].astype(F32)

    @pl.when(section_ref[0] == 1)
    def second_section():
        out_ref[0] = other_result_ref[...].astype(F32)
        out_ref[1] = result_ref[...]


def choose_kernel(flags_ref, own_ref, mine_ref, theirs_ref, first_ref, second_ref):
    half = mine_ref.shape[0]
    own = row_place(flags_ref.at[pl.ds(1, 1)], 0, half)
    other = row_place(flags_ref.at[pl.ds(1, 1)], 1, half)

    def write(own_out_ref, other_out_ref):
        own_out_ref[...] = own_ref[...]
        other_out_ref[own, :] = mine_ref[...]
        other_out_ref[other, :] = theirs_ref[...]

    @pl.when(flags_ref[0] == 0)
    def first_section():
        write(first_ref, second_ref)

    @pl.when(flags_ref[0] == 1)
    def second_section():
        write(second_ref, first_ref)


def both_layers(flags, own, mine, theirs, after=()):
    shape = low(own.shape)
    arrays = (own, *map(in_hbm, (mine, theirs)))
    return run_kernel(choose_kernel, [shape, shape], (flags,), arrays, after=after)


def per_device(
    pipe_ends,
    bounds,
    query_weight,
    key_weight,
    value_weight,
    attention_out_weight,
    feedforward_in_weight,
    down_weight,
    norm_gain,
    norm_bias,
    rel_table,
):
    section = lax.axis_index("pipe")
    index = lax.axis_index("tensor").reshape(1)
    section_index = section.reshape(1)
    ends = pipe_ends[0, :, 0]
    size = ends.shape[1]
    total = size * lax.axis_size("tensor")
    buckets, features = rel_table.shape
    width = query_weight.shape[2]
    bound = lax.dynamic_index_in_dim(bounds, section, 0, keepdims=False)[0]
    parity = lax.axis_index("dp") % 2
    flags = jnp.stack([section, parity])

    def own_half(weight):
        half = weight.shape[0] // 2
        return lax.dynamic_slice_in_dim(weight, parity * half, half, 0)

    def of_layer(layer, own, other):
        return jnp.where(section == layer, own, other)

    from_other = swap_pipe(lax.dynamic_index_in_dim(ends, 1 - section, 0, keepdims=False))
    qkv_own = jnp.concatenate([query_weight[0].T, key_weight[0].T, value_weight[0].T], 0)
    out_own, in_own, down_own = attention_out_weight[0], feedforward_in_weight[0], down_weight[0]
    qkv_mine = swap_pipe(own_half(qkv_own))
    first_in = jnp.where(section == 0, ends[0], from_other)
    last_grad = jnp.where(section == 0, from_other, ends[1])
    first_blocks = spread(first_in)
    qkv_theirs = to_partner(qkv_mine, "dp", 1)
    out_other = swap_pipe(gate(out_own, [qkv_mine]))
    own_norms = jnp.concatenate([norm_gain[0], norm_bias[0]], 0)
    other_norms = swap_pipe(gate(own_norms, [qkv_mine]))
    in_mine = swap_pipe(gate(own_half(in_own), [out_other]))
    down_mine = swap_pipe(gate(own_half(down_own), [out_other]))
    norms = [of_layer(layer, own_norms, other_norms) for layer in range(2)]
    qkv_weights = both_layers(flags, qkv_own, qkv_mine, qkv_theirs)
    out_weights = [of_layer(layer, out_own, out_other) for layer in range(2)]
    by_place = jnp.arange(2 * total, dtype=jnp.int32)
    near_rows = jnp.clip(by_place - (total - buckets // 2), 0, buckets - 1)

    def rel_rows(pick):
        one_hot = pick[:, None] == jnp.arange(buckets, dtype=jnp.int32)[None, :]
        return dot(one_hot.astype(BF), rel_table).astype(BF)

    key_first = rel_rows(buckets - 1 - jnp.clip(by_place - (total - buckets // 2), 0, buckets - 1))
    query_first = rel_rows(near_rows)

    def row(layer, number):
        return norms[layer][number : number + 1]

    tables = [
        [table_rows(rel, qkv_weights[layer]) for rel in (key_first, query_first)]
        for layer in range(2)
    ]
    saved = []
    rows = first_in
    in_weights = down_weights = None
    for layer in range(2):
        attended, parts = attend_forward(
            index,
            bound,
            spread(rows) if layer else first_blocks,
            qkv_weights[layer],
            out_weights[layer],
            tables[layer][0],
        )
        early = [tables[layer][1]]
        if layer == 0:
            in_mine = gate(in_mine, [parts[0]])
            in_theirs = to_partner(in_mine, "dp", 1)
        hidden_low, normed_one, inverse_one = norm_one(
            exchange(parts), rows, row(layer, 0), row(layer, 2), early
        )
        if layer == 0:
            down_mine = gate(down_mine, [parts[0]])
            down_theirs = to_partner(down_mine, "dp", 1)
            in_weights = both_layers(flags, in_own, in_mine, in_theirs)
            down_weights = both_layers(flags, down_own, down_mine, down_theirs)
        fed, parts = feed_forward(spread(hidden_low), in_weights[layer], down_weights[layer])
        parts = exchange(parts)
        kept = [attended, fed, normed_one, inverse_one]
        if layer == 0:
            rows, normed_two, inverse_two = norm_two(
                parts, normed_one, norms[0], [tables[1][0]]
            )
            kept += [normed_two, inverse_two]
        saved.append(kept)
    result, back_two, back_low, sums_two = turn(parts, normed_one, norms[1], last_grad)
    other_result = lax.ppermute(result.astype(BF), "pipe", [(0, 1)])

    norm_sums = [[None, None], [None, None]]
    norm_sums[1][1] = sums_two

    def back_feed(layer):
        hidden_whole, active, slope = saved[layer][1]
        (grad_ffn, grad_up), parts = feed_backward(
            spread(back_low), in_weights[layer], down_weights[layer], slope, ()
        )
        return exchange(parts), (hidden_whole, grad_up, active, grad_ffn)

    def back_attention(layer, blocks, after=()):
        rows_whole, qkv, context, probs = saved[layer][0]
        (grad_whole, grad_qkv, grad_table), parts = attend_backward(
            index,
            bound,
            blocks,
            out_weights[layer],
            qkv_weights[layer],
            qkv,
            probs,
            tables[layer][1],
            after,
        )
        factors = (rows_whole, grad_qkv, grad_whole, context, rel_table, grad_table)
        return exchange(parts), factors

    place = lax.axis_index("dp")
    line = Line(jnp.stack([section, ((place == 0) | (place == 3)).astype(jnp.int32)]))
    parts, factors = back_feed(1)
    feed = feed_halves(section_index, *factors)
    in_1 = Sum(*feed[:2])
    normed, inverse = saved[1][2:4]
    back_two, back_low, norm_sums[1][0] = norm_back(
        parts, back_two, normed, inverse, row(1, 0), False, feed
    )
    blocks = spread(back_low)
    done, _ = line.slot(in_1, after=blocks[1:2])
    down_send = gate(feed[3], done)
    down_1 = Sum(feed[2], down_send)
    parts, factors = back_attention(1, blocks, [in_hbm(down_send)])
    done, _ = line.slot(down_1, after=factors[1:2])
    held = attend_halves(section_index, *factors, after=done)
    attention_1 = Sum(*held)
    table_1 = table_grad(factors[-1], qkv_weights[1])
    normed, inverse = saved[0][4:]
    back_two, back_low, norm_sums[0][1] = norm_back(
        parts, back_two, normed, inverse, row(0, 1), True, [*done, table_1]
    )
    parts, factors = back_feed(0)
    done, _ = line.slot(attention_1, after=factors[1:2])
    feed = feed_halves(section_index, *factors, done)
    in_0 = Sum(*feed[:2])
    normed, inverse = saved[0][2:4]
    back_two, back_low, norm_sums[0][0] = norm_back(
        parts, back_two, normed, inverse, row(0, 0), False, feed
    )
    blocks = spread(back_low)
    done, _ = line.slot(in_0, after=blocks[1:2])
    down_send = gate(feed[3], done)
    down_0 = Sum(feed[2], down_send)
    parts, factors = back_attention(0, blocks, [in_hbm(down_send)])
    done, _ = line.slot(down_0, after=factors[1:2])
    held = attend_halves(section_index, *factors, after=done)
    attention_0 = Sum(*held)
    norm_rows = jnp.concatenate([rows for pair in norm_sums for rows in pair], 0)
    table_0 = table_grad(factors[-1], qkv_weights[0], done)
    positions = lax.axis_size("tensor")
    padding = -(norm_rows.shape[0] // positions) % 16
    small = jnp.concatenate(
        [
            (table_0 + table_1).reshape(positions, -1, features),
            norm_rows.reshape(positions, -1, features),
            jnp.zeros((positions, padding, features), F32),
        ],
        1,
    )
    half = small.shape[1]
    small = small.reshape(-1, features)
    small = halved(halved(small, "tensor", 1), "tensor", 2).astype(BF)
    done, _ = line.slot(attention_0)
    moved = swap_pipe(small)
    in_1_other = lax.ppermute(in_1.final, "pipe", [(0, 1)])
    grad = back_two
    for part in parts:
        grad = grad + part.astype(F32)
    other_grad = lax.ppermute(grad.astype(BF), "pipe", [(1, 0)])
    done, crossed_one = line.slot(None, (down_1, in_0), (small, moved), [in_1_other])
    small = done[-1]
    if line.direct:
        moved = to_partner(small, "dp", 1)
    else:
        moved = jnp.zeros_like(small)
        small = lax.psum(small, "dp")
    (end_values,) = run_kernel(
        ends_kernel,
        [wide((2, size, features))],
        (section_index,),
        (grad, other_grad, result, other_result),
    )
    done, crossed_two = line.slot(
        None, (attention_1, down_0), (small, moved), [crossed_one]
    )
    small = done[-1]
    moved = to_partner(small, "dp", 2) if line.direct else moved
    (into,) = join(section_index, [(in_0.final, crossed_one), (in_1.final, in_1_other)])
    done, _ = line.slot(None, (), (small, moved), [crossed_two, in_hbm(into), in_hbm(end_values)])
    small = done[-1]
    crossed_three = swap_pipe(attention_0.final)
    (downward,) = join(section_index, [(down_0.final, crossed_two), (down_1.final, crossed_one)])
    small = rejoined(small, "tensor", 2)
    table_grads, norm_rows = run_kernel(
        functools.partial(finish_kernel, half, buckets // positions),
        [wide((buckets, features)), wide((4, features))],
        (jnp.stack([index[0] % 2, section]),),
        (small, to_partner(small, "tensor", 1)),
    )
    norm_rows = norm_rows.reshape(2, 2, features)
    attention = join(
        section_index,
        [(attention_0.final, crossed_three), (attention_1.final, crossed_two)],
        4,
        [in_hbm(downward)],
    )
    return (
        end_values[None, :, None],
        *(grad.T[None] for grad in attention[:3]),
        attention[3][None],
        into[None],
        downward[None],
        norm_rows[:, 0][None],
        norm_rows[:, 1][None],
        table_grads,
    )


def solution(mesh):
    in_specs = (
        P("pipe", None, "dp", "tensor", None),
        P(None, "dp", None),
        P("pipe", None, "tensor"),
        P("pipe", None, "tensor"),
        P("pipe", None, "tensor"),
        P("pipe", "tensor", None),
        P("pipe", None, "tensor"),
        P("pipe", "tensor", None),
        P("pipe", None, None),
        P("pipe", None, None),
        P(),
    )
    out_specs = (
        P("pipe", None, "dp", "tensor", None),
        P("pipe", None, "tensor"),
        P("pipe", None, "tensor"),
        P("pipe", None, "tensor"),
        P("pipe", "tensor", None),
        P("pipe", None, "tensor"),
        P("pipe", "tensor", None),
        P("pipe", None, None),
        P("pipe", None, None),
        P(),
    )
    return jax.shard_map(
        per_device, mesh=mesh, in_specs=in_specs, out_specs=out_specs, check_vma=False
    )
```

```python
import functools
import math

import jax
import jax.numpy as jnp
from jax import lax
from jax.experimental import pallas as pl
from jax.experimental.pallas import tpu as pltpu
from jax.sharding import PartitionSpec as P

HEAD = 64
BLOCK = 128
EPSILON = 1e-05
MASKED = -1e30
BF = jnp.bfloat16
F32 = jnp.float32
SCALE = (3.0 * HEAD) ** (-0.5)


def dot(left, right):
    return lax.dot_general(left, right, (((1,), (0,)), ((), ())), preferred_element_type=F32)


def dot_t(left, right):
    return lax.dot_general(left, right, (((1,), (1,)), ((), ())), preferred_element_type=F32)


def t_dot(left, right):
    return lax.dot_general(left, right, (((0,), (0,)), ((), ())), preferred_element_type=F32)


def low(shape):
    return jax.ShapeDtypeStruct(shape, BF)


def wide(shape):
    return jax.ShapeDtypeStruct(shape, F32)


def run_kernel(body, outs, scalars, arrays, after=(), scratch=(), spare=4, far=0):
    after = tuple(after)
    held = sum(math.prod(one.shape) * one.dtype.itemsize for one in (*outs, *arrays, *scratch))
    vmem = pl.BlockSpec(memory_space=pltpu.VMEM)
    lead = len(scalars) + len(arrays)
    near = len(outs) - far

    def whole_body(*refs):
        results = refs[lead + len(after) : lead + len(after) + len(outs)]
        rest = refs[lead + len(after) + len(outs) :]
        if not far:
            body(*refs[:lead], *results, *rest)
            return
        held_results, semaphores = rest[-1 - far : -1], rest[-1]
        body(*refs[:lead], *results[:near], *held_results, *rest[: -1 - far])
        copies = [
            pltpu.make_async_copy(source, target, semaphores.at[number])
            for number, (source, target) in enumerate(zip(held_results, results[near:]))
        ]
        for copy in copies:
            copy.start()
        for copy in copies:
            copy.wait()

    scratch = list(scratch)
    if far:
        scratch += [pltpu.VMEM(one.shape, one.dtype) for one in outs[near:]]
        scratch.append(pltpu.SemaphoreType.DMA((far,)))
    return pl.pallas_call(
        whole_body,
        out_shape=tuple(
            one if number < near else pltpu.HBM(one.shape, one.dtype)
            for number, one in enumerate(outs)
        ),
        in_specs=[pl.BlockSpec(memory_space=pltpu.SMEM)] * len(scalars)
        + [vmem] * len(arrays)
        + [pl.BlockSpec(memory_space=pl.ANY)] * len(after),
        out_specs=tuple(
            vmem if number < near else pl.BlockSpec(memory_space=pltpu.HBM)
            for number in range(len(outs))
        ),
        scratch_shapes=scratch,
        compiler_params=pltpu.CompilerParams(vmem_limit_bytes=held + spare * 2**20),
    )(*scalars, *arrays, *after)


def in_hbm(array):
    return pltpu.with_memory_space_constraint(array, pltpu.HBM)


def gate(array, after):
    def nothing(*refs):
        del refs

    anywhere = pl.BlockSpec(memory_space=pl.ANY)
    return pl.pallas_call(
        nothing,
        out_shape=jax.ShapeDtypeStruct(array.shape, array.dtype),
        in_specs=[anywhere] * (1 + len(after)),
        out_specs=anywhere,
        input_output_aliases={0: 0},
    )(array, *after)


def to_partner(block, axis, distance):
    count = lax.axis_size(axis)
    return lax.ppermute(block, axis, [(i, i ^ distance) for i in range(count)])


def swap_pipe(block):
    return to_partner(block, "pipe", 1)


def spread(block):
    count = lax.axis_size("tensor")
    distances = [2**step for step in range(1, count.bit_length() - 1)]
    blocks = {0: block}
    for distance in distances:
        blocks.update({d + distance: to_partner(blocks[d], "tensor", distance) for d in list(blocks)})
    blocks.update({d + 1: to_partner(blocks[d], "tensor", 1) for d in list(blocks)})
    return [blocks[d] for d in range(count)]


def exchange(parts):
    return [parts[0]] + [to_partner(parts[d], "tensor", d) for d in range(1, len(parts))]


def row_place(index_ref, distance, size):
    return pl.ds(pl.multiple_of((index_ref[0] ^ distance) * size, size), size)


def store_parts(index_ref, whole_ref, part_refs):
    size = part_refs[0].shape[0]
    for distance, part_ref in enumerate(part_refs):
        part_ref[...] = whole_ref[row_place(index_ref, distance, size), :].astype(part_ref.dtype)


def part_shapes(count, size, features):
    return [wide((size, features))] + [low((size, features))] * (count - 1)


def added(refs):
    total = refs[0][...].astype(F32)
    for ref in refs[1:]:
        total = total + ref[...].astype(F32)
    return total


def normalize(summed):
    row_mean = jnp.mean(summed, axis=-1, keepdims=True)
    centred = summed - row_mean
    spread_of = jnp.mean(centred * centred, axis=-1, keepdims=True)
    inverse = lax.rsqrt(spread_of + EPSILON)
    return centred * inverse, inverse


def normalize_back(grad_result, normed, inverse, gain_row):
    sums = jnp.concatenate(
        [
            jnp.sum(grad_result * normed, axis=0, keepdims=True),
            jnp.sum(grad_result, axis=0, keepdims=True),
        ],
        0,
    )
    scaled = grad_result * gain_row
    centre_one = jnp.mean(scaled, axis=-1, keepdims=True)
    centre_two = jnp.mean(scaled * normed, axis=-1, keepdims=True)
    return inverse * (scaled - centre_one - normed * centre_two), sums


def by_segment(rows, split_at):
    first = lax.broadcasted_iota(jnp.int32, rows.shape, 0) < split_at
    zero = jnp.zeros_like(rows)
    return jnp.concatenate([jnp.where(first, rows, zero), jnp.where(first, zero, rows)], axis=1)


def placed_blocks(rows, first_table, second_table, first_lanes):
    total = rows.shape[0]
    span = total + BLOCK
    blocks = []
    for start in range(0, total, BLOCK):
        begin = total - BLOCK - start
        part = rows[start : start + BLOCK]
        first = dot_t(part, first_table[begin : begin + span])
        second = dot_t(part, second_table[begin : begin + span])
        both = jnp.where(first_lanes, first, second)
        blocks.append(pltpu.roll(both, total + 1, 1, stride=1, stride_axis=0)[:, :total])
    return blocks


def attend_kernel(count, index_ref, bound_ref, *refs):
    blocks = refs[:count]
    qkv_weight_ref, out_weight_ref, table_ref = refs[count : count + 3]
    rows_ref, qkv_ref, context_ref, probs_ref = refs[count + 3 : count + 7]
    part_refs = refs[count + 7 : 2 * count + 7]
    held_ref = refs[2 * count + 7]
    size = blocks[0].shape[0]
    for distance, block in enumerate(blocks):
        rows_ref[row_place(index_ref, distance, size), :] = block[...]
    split_at = bound_ref[0]
    total = rows_ref.shape[0]
    width = out_weight_ref.shape[0]
    qkv = dot_t(rows_ref[...], qkv_weight_ref[...]).astype(BF)
    qkv_ref[...] = qkv
    table = table_ref[...]
    table_wide = table.astype(F32)
    later = pltpu.roll(table_wide, 2 * total - split_at, 0).astype(BF)
    earlier = pltpu.roll(table_wide, split_at, 0).astype(BF)
    skewed = lax.broadcasted_iota(jnp.int32, (BLOCK, total + BLOCK), 0)
    skewed = skewed + lax.broadcasted_iota(jnp.int32, (BLOCK, total + BLOCK), 1)
    first_columns = skewed < split_at + BLOCK - 1
    live = lax.broadcasted_iota(jnp.int32, (total, total), 1) < bound_ref[1]
    contexts = []
    for head in range(width // HEAD):
        at = head * HEAD
        query = qkv[:, at : at + HEAD]
        key = qkv[:, width + at : width + at + HEAD]
        value = qkv[:, 2 * width + at : 2 * width + at + HEAD]

        def tables(offset):
            cut = slice(offset + at, offset + at + HEAD)
            return (
                jnp.concatenate([table[:, cut], later[:, cut]], 1),
                jnp.concatenate([earlier[:, cut], table[:, cut]], 1),
            )

        near = jnp.concatenate(
            placed_blocks(by_segment(query, split_at), *tables(0), first_columns), 0
        )
        far = placed_blocks(by_segment(key, split_at), *tables(width), first_columns)
        far = jnp.concatenate([block.T for block in far], 1)
        scores = jnp.where(live, (dot_t(query, key) + near + far) * SCALE, MASKED)
        raised = jnp.exp(scores - jnp.max(scores, axis=1, keepdims=True))
        probs = raised / jnp.sum(raised, axis=1, keepdims=True)
        probs_ref[head] = probs
        contexts.append(dot(probs.astype(BF), value).astype(BF))
    context = jnp.concatenate(contexts, 1)
    context_ref[...] = context
    held_ref[...] = dot(context, out_weight_ref[...])
    store_parts(index_ref, held_ref, part_refs)


def attend_forward(index, bound, blocks, qkv_weight, out_weight, table, after):
    count = len(blocks)
    size, features = blocks[0].shape
    total = count * size
    width = out_weight.shape[0]
    outs = run_kernel(
        functools.partial(attend_kernel, count),
        [
            low((total, features)),
            low((total, 3 * width)),
            low((total, width)),
            wide((width // HEAD, total, total)),
        ]
        + part_shapes(count, size, features),
        (index, bound),
        (*blocks, qkv_weight, out_weight, table),
        after=after,
        scratch=[pltpu.VMEM((total, features), F32)],
        spare=16,
    )
    return outs[:4], outs[4:]


def attend_back_kernel(count, index_ref, bound_ref, *refs):
    blocks = refs[:count]
    out_weight_ref, qkv_weight_ref, qkv_ref, probs_ref, table_ref = refs[count : count + 5]
    rows_ref, grad_qkv_ref, grad_table_ref = refs[count + 5 : count + 8]
    part_refs = refs[count + 8 : 2 * count + 8]
    held_ref, sum_ref = refs[2 * count + 8 :]
    size = blocks[0].shape[0]
    for distance, block in enumerate(blocks):
        rows_ref[row_place(index_ref, distance, size), :] = block[...]
    split_at = bound_ref[0]
    total = rows_ref.shape[0]
    width = out_weight_ref.shape[0]
    heads = width // HEAD
    span = total + BLOCK
    grad_context = dot_t(rows_ref[...], out_weight_ref[...]).astype(BF)
    grad_context_t = grad_context.astype(F32).T.astype(BF)
    qkv = qkv_ref[...]
    rows_t = qkv[:, : 2 * width].astype(F32).T.astype(BF)
    table = table_ref[...]
    moved = pltpu.roll(table.astype(F32), split_at, 0).astype(BF)
    row_ids = lax.broadcasted_iota(jnp.int32, (total, total), 0)
    places = jnp.where(row_ids < split_at, row_ids, row_ids - split_at)
    turned = lax.broadcasted_iota(jnp.int32, (total, total), 1) == total - 1 - places
    merge = jnp.where(turned, 1.0, 0.0).astype(BF)
    first_lanes = lax.broadcasted_iota(jnp.int32, (HEAD, total), 1) < split_at
    first_rows = lax.broadcasted_iota(jnp.int32, (total, HEAD), 0) < split_at
    pad = jnp.zeros((BLOCK, BLOCK), F32)
    held_ref[...] = jnp.zeros(held_ref.shape, F32)

    def along_table(merged, offset, head):
        cut = slice(offset + head * HEAD, offset + (head + 1) * HEAD)
        pair = jnp.concatenate([table[:, cut], moved[:, cut]], 1)
        turned_rows = rows_t[cut]
        zero = jnp.zeros_like(turned_rows)
        turned_rows = jnp.concatenate(
            [jnp.where(first_lanes, turned_rows, zero), jnp.where(first_lanes, zero, turned_rows)],
            0,
        )
        parts = []
        slot = offset // HEAD + head
        for start in range(0, total, BLOCK):
            block = jnp.concatenate([merged[start : start + BLOCK], pad], 1)
            block = pltpu.roll(block, 1, 1, stride=1, stride_axis=0).astype(BF)
            parts.append(dot(block, pair[start : start + span]))
            held_ref[slot, :, start : start + span] += dot(
                turned_rows[:, start : start + BLOCK], block
            )
        both = jnp.concatenate(parts, 0)
        return jnp.where(first_rows, both[:, :HEAD], both[:, HEAD:])

    grad_queries = []
    grad_keys = []
    grad_values_t = []
    for head in range(heads):
        at = head * HEAD
        cut = slice(at, at + HEAD)
        query = qkv[:, at : at + HEAD]
        key = qkv[:, width + at : width + at + HEAD]
        value = qkv[:, 2 * width + at : 2 * width + at + HEAD]
        grad_probs = dot_t(grad_context[:, cut], value)
        probs = probs_ref[head]
        centre = jnp.sum(probs * grad_probs, axis=1, keepdims=True)
        score_grad = (probs * (grad_probs - centre) * SCALE).astype(BF)
        score_grad_t = score_grad.astype(F32).T.astype(BF)
        grad_values_t.append(dot(grad_context_t[cut], probs.astype(BF)))
        grad_queries.append(dot(score_grad, key) + along_table(dot(score_grad, merge), 0, head))
        grad_keys.append(
            dot(score_grad_t, query) + along_table(dot(score_grad_t, merge), width, head)
        )
    grad_values = jnp.concatenate(grad_values_t, 0).T
    grad_qkv = jnp.concatenate(grad_queries + grad_keys + [grad_values], 1).astype(BF)
    grad_qkv_ref[...] = grad_qkv
    sum_ref[...] = dot(grad_qkv, qkv_weight_ref[...])
    store_parts(index_ref, sum_ref, part_refs)
    lanes = lax.broadcasted_iota(jnp.int32, (HEAD, span), 1)
    for slot in range(2 * heads):
        first = held_ref[slot, :HEAD]
        second = pltpu.roll(held_ref[slot, HEAD:], 2 * total - split_at, 1)
        both = first + second
        bottom = jnp.sum(both[:, :BLOCK], axis=1, keepdims=True)
        top = jnp.sum(both[:, 2 * total - BLOCK :], axis=1, keepdims=True)
        middle = both[:, BLOCK : 2 * total - BLOCK]
        middle = middle + jnp.where(lanes == 0, bottom, 0.0)
        middle = middle + jnp.where(lanes == span - 1, top, 0.0)
        grad_table_ref[slot * HEAD : (slot + 1) * HEAD] = middle.astype(BF)


def attend_backward(index, bound, blocks, out_weight, qkv_weight, qkv, probs, table, after):
    count = len(blocks)
    size, features = blocks[0].shape
    total = count * size
    width = out_weight.shape[0]
    outs = run_kernel(
        functools.partial(attend_back_kernel, count),
        [low((total, features)), low((total, 3 * width)), low((2 * width, total + BLOCK))]
        + part_shapes(count, size, features),
        (index, bound),
        (*blocks, out_weight, qkv_weight, *map(in_hbm, (qkv, probs, table))),
        after=after,
        scratch=[
            pltpu.VMEM((2 * width // HEAD, 2 * HEAD, 2 * total), F32),
            pltpu.VMEM((total, features), F32),
        ],
        spare=16,
    )
    return outs[:3], outs[3:]


def feed_kernel(count, *refs):
    blocks = refs[:count]
    in_ref, down_ref = refs[count : count + 2]
    rows_ref, active_ref, slope_ref = refs[count + 2 : count + 5]
    part_refs = refs[count + 5 : 2 * count + 5]
    size = blocks[0].shape[0]
    for distance, block in enumerate(blocks):
        cut = slice(distance * size, (distance + 1) * size)
        rows = block[...]
        rows_ref[cut] = rows
        upward = dot(rows, in_ref[...])
        below = 0.5 * (1.0 + lax.erf(upward * (1.0 / math.sqrt(2.0))))
        density = jnp.exp(-0.5 * upward * upward) * (1.0 / math.sqrt(2.0 * math.pi))
        active = (upward * below).astype(BF)
        active_ref[cut] = active
        slope_ref[cut] = below + upward * density
        part_refs[distance][...] = dot(active, down_ref[...]).astype(part_refs[distance].dtype)


def feed_forward(blocks, in_weight, down_weight):
    count = len(blocks)
    size, features = blocks[0].shape
    units = in_weight.shape[1]
    total = count * size
    outs = run_kernel(
        functools.partial(feed_kernel, count),
        [low((total, features)), low((total, units)), wide((total, units))]
        + part_shapes(count, size, features),
        (),
        (*blocks, in_weight, down_weight),
    )
    return outs[:3], outs[3:]


def feed_back_kernel(count, *refs):
    blocks = refs[:count]
    in_ref, down_ref, slope_ref = refs[count : count + 3]
    rows_ref, grad_up_ref = refs[count + 3 : count + 5]
    part_refs = refs[count + 5 : 2 * count + 5]
    size = blocks[0].shape[0]
    for distance, block in enumerate(blocks):
        cut = slice(distance * size, (distance + 1) * size)
        rows = block[...]
        rows_ref[cut] = rows
        grad_up = (dot_t(rows, down_ref[...]) * slope_ref[cut]).astype(BF)
        grad_up_ref[cut] = grad_up
        part_refs[distance][...] = dot_t(grad_up, in_ref[...]).astype(part_refs[distance].dtype)


def feed_backward(blocks, in_weight, down_weight, slope, after):
    count = len(blocks)
    size, features = blocks[0].shape
    units = in_weight.shape[1]
    total = count * size
    outs = run_kernel(
        functools.partial(feed_back_kernel, count),
        [low((total, features)), low((total, units))] + part_shapes(count, size, features),
        (),
        (*blocks, in_weight, down_weight, slope),
        after=after,
    )
    return outs[:2], outs[2:]


def norm_one_kernel(count, *refs):
    rows_ref, gain_ref, bias_ref, low_ref, normed_ref, inverse_ref = refs[count:]
    normed, inverse = normalize(rows_ref[...].astype(F32) + added(refs[:count]))
    low_ref[...] = (normed * gain_ref[...] + bias_ref[...]).astype(BF)
    normed_ref[...] = normed
    inverse_ref[...] = inverse


def norm_one(parts, rows, gain_row, bias_row, after=()):
    shape = rows.shape
    return run_kernel(
        functools.partial(norm_one_kernel, len(parts)),
        [low(shape), wide(shape), wide((shape[0], 1))],
        (),
        (*parts, rows, gain_row, bias_row),
        after=after,
    )


def norm_two_kernel(count, *refs):
    before_ref, gains_ref, low_ref, normed_ref, inverse_ref = refs[count:]
    hidden = before_ref[...] * gains_ref[0:1] + gains_ref[2:3]
    normed, inverse = normalize(hidden + added(refs[:count]))
    low_ref[...] = (normed * gains_ref[1:2] + gains_ref[3:4]).astype(BF)
    normed_ref[...] = normed
    inverse_ref[...] = inverse


def norm_two(parts, before, gains, after=()):
    shape = before.shape
    return run_kernel(
        functools.partial(norm_two_kernel, len(parts)),
        [low(shape), wide(shape), wide((shape[0], 1))],
        (),
        (*parts, before, gains),
        after=after,
    )


def turn_kernel(count, *refs):
    before_ref, gains_ref, grad_ref, result_ref, back_ref, low_ref, sums_ref = refs[count:]
    hidden = before_ref[...] * gains_ref[0:1] + gains_ref[2:3]
    normed, inverse = normalize(hidden + added(refs[:count]))
    result_ref[...] = normed * gains_ref[1:2] + gains_ref[3:4]
    back, sums_ref[...] = normalize_back(
        grad_ref[...].astype(F32), normed, inverse, gains_ref[1:2]
    )
    back_ref[...] = back
    low_ref[...] = back.astype(BF)


def turn(parts, before, gains, grad):
    shape = before.shape
    return run_kernel(
        functools.partial(turn_kernel, len(parts)),
        [wide(shape), wide(shape), low(shape), wide((2, shape[1]))],
        (),
        (*parts, before, gains, grad),
    )


def norm_back_kernel(count, rounded, *refs):
    add_ref, normed_ref, inverse_ref, gain_ref, back_ref, low_ref, sums_ref = refs[count:]
    grad = add_ref[...] + added(refs[:count])
    if rounded:
        grad = grad.astype(BF).astype(F32)
    back, sums_ref[...] = normalize_back(
        grad, normed_ref[...], inverse_ref[...], gain_ref[...]
    )
    back_ref[...] = back
    low_ref[...] = back.astype(BF)


def norm_back(parts, add, normed, inverse, gain_row, rounded, after):
    shape = add.shape
    return run_kernel(
        functools.partial(norm_back_kernel, len(parts), rounded),
        [wide(shape), low(shape), wide((2, shape[1]))],
        (),
        (*parts, *map(in_hbm, (add, normed, inverse)), gain_row),
        after=after,
    )


def feed_halves_kernel(section_ref, hidden_ref, grad_up_ref, active_ref, grad_ref, *refs):
    pairs = ((hidden_ref, grad_up_ref, refs[:2]), (active_ref, grad_ref, refs[2:]))
    for left_ref, right_ref, halves in pairs:
        for distance, half_ref in enumerate(halves):
            columns = row_place(section_ref, distance, half_ref.shape[0])
            half_ref[...] = t_dot(left_ref[:, columns], right_ref[...]).astype(BF)


def feed_halves(section, hidden, grad_up, active, grad, after=()):
    features = hidden.shape[1]
    units = active.shape[1]
    return run_kernel(
        feed_halves_kernel,
        [low((features // 2, units))] * 2 + [low((units // 2, features))] * 2,
        (section,),
        (hidden, grad_up, active, grad),
        after=after,
        spare=8,
    )


def attend_halves_kernel(
    section_ref, rows_ref, grad_qkv_ref, grad_ref, context_ref, rel_ref, grad_table_ref, keep_ref, send_ref
):
    width = context_ref.shape[1]
    from_rows = t_dot(grad_qkv_ref[...], rows_ref[...])
    queries = from_rows[:width] + dot(grad_table_ref[width:], rel_ref[...])
    keys = from_rows[width : 2 * width] + dot(grad_table_ref[:width], rel_ref[...])
    first = jnp.concatenate([queries, keys], 0).astype(BF)
    outward = t_dot(context_ref[...], grad_ref[...])
    second = jnp.concatenate([from_rows[2 * width :], outward], 0).astype(BF)
    keep_ref[...] = jnp.where(section_ref[0] == 0, first, second)
    send_ref[...] = jnp.where(section_ref[0] == 0, second, first)


def attend_halves(section, rows, grad_qkv, grad, context, rel_table, grad_table, after=()):
    features = rows.shape[1]
    width = context.shape[1]
    half = low((2 * width, features))
    return run_kernel(
        attend_halves_kernel,
        [half, half],
        (section,),
        (rows, grad_qkv, grad, context, rel_table, grad_table),
        after=after,
        spare=8,
    )


def table_grad_kernel(grad_table_ref, weight_ref, out_ref):
    width = grad_table_ref.shape[0] // 2
    out_ref[...] = t_dot(grad_table_ref[:width], weight_ref[width : 2 * width]) + t_dot(
        grad_table_ref[width:], weight_ref[:width]
    )


def table_grad(grad_table, qkv_weight, after=()):
    outs = [wide((grad_table.shape[1], qkv_weight.shape[1]))]
    return run_kernel(table_grad_kernel, outs, (), (grad_table, qkv_weight), after=after)[0]


class Sum:
    def __init__(self, keep, send, after=()):
        self.pairs = [(keep, swap_pipe(gate(send, after) if after else send))]
        self.held = self.final = None


def slot_kernel(pairs, first, second, third, crossing, extra, flags_ref, *refs):
    refs = list(refs)

    def take(count):
        taken = refs[:count]
        del refs[:count]
        return taken

    entering = take(2 * pairs)
    in_first, in_second, in_third = take(first), take(second), take(third)
    (by_neighbour,) = take(1) if first or third else (None,)
    (by_middle,) = take(1) if second else (None,)
    across = take(crossing)
    extras = take(2 * extra)
    at_end = flags_ref[1] == 1
    sums = {}

    def give(name, value):
        (ref,) = take(1)
        ref[...] = value
        sums[name] = value

    if pairs:
        (ref,) = take(1)
        start = 0
        for keep, arrived in zip(entering[::2], entering[1::2]):
            rows = keep.shape[0]
            ref[start : start + rows] = (keep[...].astype(F32) + arrived[...].astype(F32)).astype(BF)
            start += rows
        sums["entered"] = ref[...]
    if first:
        held = in_first[0][...]
        total = (held.astype(F32) + by_neighbour[...].astype(F32)).astype(BF)
        give("first", jnp.where(at_end, held, total))
    if second:
        held = in_second[0][...].astype(F32)
        sums["second"] = (held + by_middle[...].astype(F32)).astype(BF)
        if not pairs:
            give("second", sums["second"])
    if third:
        held = in_third[0][...]
        give("third", jnp.where(at_end, by_neighbour[...], held))
    if pairs and second:
        (ref,) = take(1)
        ref[...] = jnp.where(at_end, sums["entered"], sums["second"])
    if crossing:
        (ref,) = take(1)
        from_zero = across[0][...]
        from_one = across[1][...] if crossing == 2 else sums["third"]
        ref[...] = jnp.where(flags_ref[0] == 0, from_zero, from_one)
    if extra:
        (ref,) = take(1)
        ref[...] = (extras[0][...].astype(F32) + extras[1][...].astype(F32)).astype(BF)


class Line:
    def __init__(self, flags):
        self.flags = flags
        self.direct = lax.axis_size("dp") == 4
        self.first = self.second = self.third = None
        self.by_neighbour = self.by_middle = None

    def slot(self, entering=None, crossing=(), extra=(), after=()):
        first, second, third = self.first, self.second, self.third
        arrays = [array for pair in (entering.pairs if entering else ()) for array in pair]
        outs = []
        if entering:
            rows = sum(keep.shape[0] for keep, moved in entering.pairs)
            outs.append(low((rows, arrays[0].shape[1])))
        for one in (first, second, third):
            if one:
                arrays.append(one.held)
                if one is not second or not entering:
                    outs.append(low(one.held.shape))
        if first or third:
            arrays.append(self.by_neighbour)
        if second:
            arrays.append(self.by_middle)
        across = [one.final for one in crossing if one.final is not None]
        arrays += across
        arrays += extra
        if entering and second:
            outs.append(outs[0])
        if crossing:
            outs.append(low(across[0].shape))
        if extra:
            outs.append(low(extra[0].shape))
        body = functools.partial(
            slot_kernel,
            len(entering.pairs) if entering else 0,
            int(first is not None),
            int(second is not None),
            int(third is not None),
            len(across),
            int(len(extra) > 0),
        )
        results = list(run_kernel(body, outs, (self.flags,), arrays, after=after))
        done = list(results)
        payload = None
        if entering:
            payload = entering.held = results.pop(0)
        if first:
            first.held = results.pop(0)
        if second and not entering:
            payload = second.held = results.pop(0)
        if third:
            third.final = results.pop(0)
        if entering and second:
            payload = second.held = results.pop(0)
        if not self.direct:
            if entering:
                entering.final = lax.psum(entering.held, "dp")
        else:
            if payload is not None:
                self.by_neighbour = lax.ppermute(
                    payload, "dp", [(0, 1), (1, 0), (2, 3), (3, 2)]
                )
            if first:
                self.by_middle = lax.ppermute(first.held, "dp", [(1, 2), (2, 1)])
            self.first, self.second, self.third = entering, first, second
        return done, swap_pipe(results.pop(0)) if crossing else None


def table_kernel(rel_ref, weight_ref, out_ref):
    width = weight_ref.shape[0] // 3
    out_ref[:, :width] = dot_t(rel_ref[...], weight_ref[width : 2 * width]).astype(BF)
    out_ref[:, width:] = dot_t(rel_ref[...], weight_ref[:width]).astype(BF)


def table_rows(rel_rows, qkv_weight):
    outs = [low((rel_rows.shape[0], 2 * qkv_weight.shape[0] // 3))]
    return run_kernel(table_kernel, outs, (), (in_hbm(rel_rows), qkv_weight))[0]


def halved(part, axis, distance):
    bit = (lax.axis_index(axis) // distance) % 2
    half = part.shape[0] // 2
    keep = lax.dynamic_slice_in_dim(part, bit * half, half, 0)
    send = lax.dynamic_slice_in_dim(part, (1 - bit) * half, half, 0).astype(BF)
    return keep + to_partner(send, axis, distance).astype(F32)


def rejoined(part, axis, distance):
    bit = (lax.axis_index(axis) // distance) % 2
    other = to_partner(part, axis, distance)
    return jnp.where(
        bit == 0, jnp.concatenate([part, other], 0), jnp.concatenate([other, part], 0)
    )


def join_kernel(section_ref, *refs):
    outs = refs[4:]

    def write(halves):
        rows = outs[0].shape[0]
        start = 0
        for out_ref in outs:
            for half_ref in halves:
                begin, size = start, half_ref.shape[0]
                from_row, to_row = max(begin, 0), min(begin + rows, size)
                if from_row < to_row:
                    out_ref[from_row - begin : to_row - begin] = half_ref[from_row:to_row].astype(F32)
                start -= size
            start += rows + sum(half_ref.shape[0] for half_ref in halves)

    @pl.when(section_ref[0] == 0)
    def first_section():
        write((refs[0], refs[1]))

    @pl.when(section_ref[0] == 1)
    def second_section():
        write((refs[3], refs[2]))


def join(section, halves, count=1, after=()):
    arrays = [array for pair in halves for array in pair]
    rows, columns = 2 * arrays[0].shape[0] // count, arrays[0].shape[1]
    return run_kernel(
        join_kernel, [wide((rows, columns))] * count, (section,), arrays, after=after
    )


def finish_kernel(size, of_table, flags_ref, own_ref, other_ref, table_ref, norms_ref):
    first = jnp.where(flags_ref[0] == 0, own_ref[...], other_ref[...]).astype(F32)
    second = jnp.where(flags_ref[0] == 0, other_ref[...], own_ref[...]).astype(F32)
    positions = 2 * own_ref.shape[0] // size
    share = 8 // positions
    norms = []
    for position in range(positions):
        part = first if position < positions // 2 else second
        start = position % (positions // 2) * size
        table_ref[position * of_table : (position + 1) * of_table] = part[start : start + of_table]
        norms.append(part[start + of_table : start + of_table + share])
    norms = jnp.concatenate(norms, 0)
    norms_ref[...] = jnp.where(flags_ref[1] == 0, norms[:4], norms[4:])


def ends_kernel(section_ref, grad_ref, other_grad_ref, result_ref, other_result_ref, out_ref):
    @pl.when(section_ref[0] == 0)
    def first_section():
        out_ref[0] = grad_ref[...]
        out_ref[1] = other_grad_ref[...].astype(F32)

    @pl.when(section_ref[0] == 1)
    def second_section():
        out_ref[0] = other_result_ref[...].astype(F32)
        out_ref[1] = result_ref[...]


def choose_kernel(flags_ref, own_ref, mine_ref, theirs_ref, first_ref, second_ref):
    half = mine_ref.shape[0]
    own = row_place(flags_ref.at[pl.ds(1, 1)], 0, half)
    other = row_place(flags_ref.at[pl.ds(1, 1)], 1, half)

    def write(own_out_ref, other_out_ref):
        own_out_ref[...] = own_ref[...]
        other_out_ref[own, :] = mine_ref[...]
        other_out_ref[other, :] = theirs_ref[...]

    @pl.when(flags_ref[0] == 0)
    def first_section():
        write(first_ref, second_ref)

    @pl.when(flags_ref[0] == 1)
    def second_section():
        write(second_ref, first_ref)


def both_layers(flags, own, mine, theirs, after=()):
    shape = low(own.shape)
    arrays = (own, *map(in_hbm, (mine, theirs)))
    return run_kernel(choose_kernel, [shape, shape], (flags,), arrays, after=after)


def per_device(
    pipe_ends,
    bounds,
    query_weight,
    key_weight,
    value_weight,
    attention_out_weight,
    feedforward_in_weight,
    down_weight,
    norm_gain,
    norm_bias,
    rel_table,
):
    section = lax.axis_index("pipe")
    index = lax.axis_index("tensor").reshape(1)
    section_index = section.reshape(1)
    ends = pipe_ends[0, :, 0]
    size = ends.shape[1]
    total = size * lax.axis_size("tensor")
    buckets, features = rel_table.shape
    width = query_weight.shape[2]
    bound = lax.dynamic_index_in_dim(bounds, section, 0, keepdims=False)[0]
    parity = lax.axis_index("dp") % 2
    flags = jnp.stack([section, parity])

    def own_half(weight):
        half = weight.shape[0] // 2
        return lax.dynamic_slice_in_dim(weight, parity * half, half, 0)

    def of_layer(layer, own, other):
        return jnp.where(section == layer, own, other)

    from_other = swap_pipe(lax.dynamic_index_in_dim(ends, 1 - section, 0, keepdims=False))
    qkv_own = jnp.concatenate([query_weight[0].T, key_weight[0].T, value_weight[0].T], 0)
    out_own, in_own, down_own = attention_out_weight[0], feedforward_in_weight[0], down_weight[0]
    qkv_mine = swap_pipe(own_half(qkv_own))
    first_in = jnp.where(section == 0, ends[0], from_other)
    last_grad = jnp.where(section == 0, from_other, ends[1])
    first_blocks = spread(first_in)
    qkv_theirs = to_partner(qkv_mine, "dp", 1)
    out_other = swap_pipe(gate(out_own, [qkv_mine]))
    own_norms = jnp.concatenate([norm_gain[0], norm_bias[0]], 0)
    other_norms = swap_pipe(gate(own_norms, [qkv_mine]))
    in_mine = swap_pipe(gate(own_half(in_own), [out_other]))
    down_mine = swap_pipe(gate(own_half(down_own), [out_other]))
    norms = [of_layer(layer, own_norms, other_norms) for layer in range(2)]
    qkv_weights = both_layers(flags, qkv_own, qkv_mine, qkv_theirs)
    out_weights = [of_layer(layer, out_own, out_other) for layer in range(2)]
    by_place = jnp.arange(2 * total, dtype=jnp.int32)
    near_rows = jnp.clip(by_place - (total - buckets // 2), 0, buckets - 1)

    def rel_rows(pick):
        one_hot = pick[:, None] == jnp.arange(buckets, dtype=jnp.int32)[None, :]
        return dot(one_hot.astype(BF), rel_table).astype(BF)

    key_first = rel_rows(buckets - 1 - jnp.clip(by_place - (total - buckets // 2), 0, buckets - 1))
    query_first = rel_rows(near_rows)

    def row(layer, number):
        return norms[layer][number : number + 1]

    tables = [
        [table_rows(rel, qkv_weights[layer]) for rel in (key_first, query_first)]
        for layer in range(2)
    ]
    in_mine = gate(in_mine, [qkv_theirs])
    saved = []
    rows = first_in
    in_weights = down_weights = None
    for layer in range(2):
        attended, parts = attend_forward(
            index,
            bound,
            spread(rows) if layer else first_blocks,
            qkv_weights[layer],
            out_weights[layer],
            tables[layer][0],
            [] if layer else [in_hbm(in_mine)],
        )
        early = [tables[layer][1]]
        if layer == 0:
            in_theirs = to_partner(in_mine, "dp", 1)
        hidden_low, normed_one, inverse_one = norm_one(
            exchange(parts), rows, row(layer, 0), row(layer, 2), early
        )
        if layer == 0:
            down_mine = gate(down_mine, [parts[0]])
            down_theirs = to_partner(down_mine, "dp", 1)
            in_weights = both_layers(flags, in_own, in_mine, in_theirs)
            down_weights = both_layers(flags, down_own, down_mine, down_theirs)
        fed, parts = feed_forward(spread(hidden_low), in_weights[layer], down_weights[layer])
        parts = exchange(parts)
        kept = [attended, fed, normed_one, inverse_one]
        if layer == 0:
            rows, normed_two, inverse_two = norm_two(
                parts, normed_one, norms[0], [tables[1][0]]
            )
            kept += [normed_two, inverse_two]
        saved.append(kept)
    result, back_two, back_low, sums_two = turn(parts, normed_one, norms[1], last_grad)
    other_result = lax.ppermute(result.astype(BF), "pipe", [(0, 1)])

    norm_sums = [[None, None], [None, None]]
    norm_sums[1][1] = sums_two

    def back_feed(layer):
        hidden_whole, active, slope = saved[layer][1]
        (grad_ffn, grad_up), parts = feed_backward(
            spread(back_low), in_weights[layer], down_weights[layer], slope, ()
        )
        return exchange(parts), (hidden_whole, grad_up, active, grad_ffn)

    def back_attention(layer, blocks, after=()):
        rows_whole, qkv, context, probs = saved[layer][0]
        (grad_whole, grad_qkv, grad_table), parts = attend_backward(
            index,
            bound,
            blocks,
            out_weights[layer],
            qkv_weights[layer],
            qkv,
            probs,
            tables[layer][1],
            after,
        )
        factors = (rows_whole, grad_qkv, grad_whole, context, rel_table, grad_table)
        return exchange(parts), factors

    place = lax.axis_index("dp")
    line = Line(jnp.stack([section, ((place == 0) | (place == 3)).astype(jnp.int32)]))
    parts, factors = back_feed(1)
    feed = feed_halves(section_index, *factors)
    in_1 = Sum(*feed[:2])
    normed, inverse = saved[1][2:4]
    back_two, back_low, norm_sums[1][0] = norm_back(
        parts, back_two, normed, inverse, row(1, 0), False, feed
    )
    blocks = spread(back_low)
    done, _ = line.slot(in_1, after=blocks[1:2])
    down_send = gate(feed[3], done)
    down_1 = Sum(feed[2], down_send)
    parts, factors = back_attention(1, blocks, [in_hbm(down_send)])
    done, _ = line.slot(down_1, after=factors[1:2])
    held = attend_halves(section_index, *factors, after=done)
    attention_1 = Sum(*held)
    table_1 = table_grad(factors[-1], qkv_weights[1])
    normed, inverse = saved[0][4:]
    back_two, back_low, norm_sums[0][1] = norm_back(
        parts, back_two, normed, inverse, row(0, 1), True, [*done, table_1]
    )
    parts, factors = back_feed(0)
    done, _ = line.slot(attention_1, after=factors[1:2])
    feed = feed_halves(section_index, *factors, done)
    in_0 = Sum(*feed[:2])
    normed, inverse = saved[0][2:4]
    back_two, back_low, norm_sums[0][0] = norm_back(
        parts, back_two, normed, inverse, row(0, 0), False, feed
    )
    blocks = spread(back_low)
    done, _ = line.slot(in_0, after=blocks[1:2])
    down_send = gate(feed[3], done)
    down_0 = Sum(feed[2], down_send)
    parts, factors = back_attention(0, blocks, [in_hbm(down_send)])
    done, _ = line.slot(down_0, after=factors[1:2])
    held = attend_halves(section_index, *factors, after=done)
    attention_0 = Sum(*held)
    norm_rows = jnp.concatenate([rows for pair in norm_sums for rows in pair], 0)
    table_0 = table_grad(factors[-1], qkv_weights[0], done)
    positions = lax.axis_size("tensor")
    padding = -(norm_rows.shape[0] // positions) % 16
    small = jnp.concatenate(
        [
            (table_0 + table_1).reshape(positions, -1, features),
            norm_rows.reshape(positions, -1, features),
            jnp.zeros((positions, padding, features), F32),
        ],
        1,
    )
    half = small.shape[1]
    small = small.reshape(-1, features)
    small = halved(halved(small, "tensor", 1), "tensor", 2).astype(BF)
    done, _ = line.slot(attention_0)
    moved = swap_pipe(small)
    in_1_other = lax.ppermute(in_1.final, "pipe", [(0, 1)])
    grad = back_two
    for part in parts:
        grad = grad + part.astype(F32)
    other_grad = lax.ppermute(grad.astype(BF), "pipe", [(1, 0)])
    done, crossed_one = line.slot(None, (down_1, in_0), (small, moved), [in_1_other])
    small = done[-1]
    if line.direct:
        moved = to_partner(small, "dp", 1)
    else:
        moved = jnp.zeros_like(small)
        small = lax.psum(small, "dp")
    (end_values,) = run_kernel(
        ends_kernel,
        [wide((2, size, features))],
        (section_index,),
        (grad, other_grad, result, other_result),
    )
    done, crossed_two = line.slot(
        None, (attention_1, down_0), (small, moved), [crossed_one]
    )
    small = done[-1]
    moved = to_partner(small, "dp", 2) if line.direct else moved
    (into,) = join(section_index, [(in_0.final, crossed_one), (in_1.final, in_1_other)])
    done, _ = line.slot(None, (), (small, moved), [crossed_two, in_hbm(into), in_hbm(end_values)])
    small = done[-1]
    crossed_three = swap_pipe(attention_0.final)
    (downward,) = join(section_index, [(down_0.final, crossed_two), (down_1.final, crossed_one)])
    small = rejoined(small, "tensor", 2)
    table_grads, norm_rows = run_kernel(
        functools.partial(finish_kernel, half, buckets // positions),
        [wide((buckets, features)), wide((4, features))],
        (jnp.stack([index[0] % 2, section]),),
        (small, to_partner(small, "tensor", 1)),
    )
    norm_rows = norm_rows.reshape(2, 2, features)
    attention = join(
        section_index,
        [(attention_0.final, crossed_three), (attention_1.final, crossed_two)],
        4,
        [in_hbm(downward)],
    )
    return (
        end_values[None, :, None],
        *(grad.T[None] for grad in attention[:3]),
        attention[3][None],
        into[None],
        downward[None],
        norm_rows[:, 0][None],
        norm_rows[:, 1][None],
        table_grads,
    )


def solution(mesh):
    in_specs = (
        P("pipe", None, "dp", "tensor", None),
        P(None, "dp", None),
        P("pipe", None, "tensor"),
        P("pipe", None, "tensor"),
        P("pipe", None, "tensor"),
        P("pipe", "tensor", None),
        P("pipe", None, "tensor"),
        P("pipe", "tensor", None),
        P("pipe", None, None),
        P("pipe", None, None),
        P(),
    )
    out_specs = (
        P("pipe", None, "dp", "tensor", None),
        P("pipe", None, "tensor"),
        P("pipe", None, "tensor"),
        P("pipe", None, "tensor"),
        P("pipe", "tensor", None),
        P("pipe", None, "tensor"),
        P("pipe", "tensor", None),
        P("pipe", None, None),
        P("pipe", None, None),
        P(),
    )
    return jax.shard_map(
        per_device, mesh=mesh, in_specs=in_specs, out_specs=out_specs, check_vma=False
    )
```
